512 devices in a mesh: kpool: 8 (over x, core), fft: 64 (over z, y).
Axes of the slice: x: 4, y: 4, z: 16, core: 2. Of those that a mesh axis runs over, the one named last changes fastest.
Arguments:
- orbitals: float32 [8, 8, 4, 16384], P('kpool', None, None, 'fft'), may hold values from -6 to 6
- response: float32 [8, 8, 4, 16384], P('kpool', None, None, 'fft'), may hold values from -6 to 6
- residual: float32 [8, 8, 4, 16384], P('kpool', None, None, 'fft'), may hold values from -9 to 9
- old_direction: float32 [8, 8, 4, 16384], P('kpool', None, None, 'fft'), may hold values from -6 to 6
- old_norm: float32 [8, 8], P('kpool'), may hold values from 9830.4 to 7208960
- band_energy: float32 [8, 8], P('kpool'), may hold values from -1 to 0.4
- kinetic: float32 [8, 16384], P('kpool', 'fft'), may hold values from 0.5 to 20
- form_factor: float32 [8, 2, 16, 16384], P('kpool', None, None, 'fft'), may hold values from -0.046875 to 0.046875
- sphere_index: int32 [8, 16384], P('kpool', 'fft'), may hold values from 0 to 262143, as said below
- atom_positions: float32 [3, 64], replicated, may hold values from 0 to 1
- proj_atom: int32 [1024], replicated, may hold values from 0 to 63
- coupling: float32 [2, 32, 32], replicated, may hold values from -0.03 to 3
- potential: float32 [4, 64, 4096], P(None, 'fft'), may hold values from -0.3 to 2
Outputs:
- response_next: float32 [8, 8, 4, 16384], P('kpool', None, None, 'fft')
- residual_next: float32 [8, 8, 4, 16384], P('kpool', None, None, 'fft')
- direction: float32 [8, 8, 4, 16384], P('kpool', None, None, 'fft')
- induced_density: float32 [4, 64, 4096], P(None, 'fft')
The draws below stay inside these ranges and needn't reach their ends.
Inputs may be any that keep to these rules, and one draw needn't show every extreme that they name: `sphere_index`: within one point the entries are distinct. Entry j = b * 32 + t (t < 32) has gz = (t - 16) mod 64, and the 32 entries of one b share one column (gx, gy), so the plane waves of every device are whole columns. The columns of one point are the 512 columns nearest the anchor in signed frequencies f(gx)^2 + f(gy)^2, ties broken at random, in a random order.
All inputs are finite; a program needn't handle non-finite values.
Results may differ from the reference program's by a relative error of at most 0.0003.
Values sent between devices are 32-bit elements; how exact they have to be, the bound alone decides.
No kernel may reach another device: no remote copies, remote signals or barrier semaphores. Data moves between devices by JAX's collectives and lax.ppermute only.
A program may use at most 64 MiB of HBM per device.

```python
import math
import jax
import jax.numpy as jnp
from jax import lax

NG = 64
NB = 8
NK = 8
STICK_LEN = 32
NPW = 16384
NATOM = 64
PA = 16
NPROJ = 1024


def band_scales(key):
    return jnp.exp(jax.random.uniform(jax.random.fold_in(key, 5), (NK, NB), jnp.float32, math.log(0.3), math.log(3.0)))


def draw_residual(key, part):
    scales = band_scales(key)
    key = jax.random.fold_in(key, 15)
    first = jax.random.fold_in(key, 0)
    ramp = jnp.exp(math.log(3.0) * jnp.arange(NPW, dtype=jnp.float32) / max(NPW - 1, 1))
    noise = jax.random.uniform(first, (NK, NB, 4, NPW), jnp.float32, -1.0, 1.0)
    return noise * ramp[None, None, None, :] * scales[:, :, None, None]


def draw_old_norm(key, part):
    scales = band_scales(key)
    key = jax.random.fold_in(key, 16)
    factor = jnp.exp(jax.random.uniform(key, (NK, NB), jnp.float32, math.log(1.5), math.log(10.0)))
    return scales * scales * (4.85 * NPW) * factor


def draw_sphere_index(key, part):
    key = jax.random.fold_in(key, 11)
    columns = NPW // STICK_LEN
    cells = jnp.arange(NG * NG, dtype=jnp.int32)
    half = NG // 2
    col_x = cells // NG
    col_y = cells % NG
    signed_x = jnp.where(col_x < half, col_x, col_x - NG)
    signed_y = jnp.where(col_y < half, col_y, col_y - NG)
    radius = signed_x * signed_x + signed_y * signed_y
    depth = (jnp.arange(STICK_LEN, dtype=jnp.int32) - STICK_LEN // 2) % NG
    keys = jax.random.split(key, NK)

    def one_point(point_key):
        first, second = jax.random.split(point_key)
        tiebreak = jax.random.permutation(first, NG * NG).astype(jnp.int32)
        score = radius * (NG * NG) + tiebreak
        chosen = jnp.argsort(score, stable=True)[:columns].astype(jnp.int32)
        shuffled = jnp.take(chosen, jax.random.permutation(second, columns).astype(jnp.int32))
        return (shuffled[:, None] * NG + depth[None, :]).reshape(NPW).astype(jnp.int32)
    return jax.vmap(one_point)(keys)


def draw_coupling(key, part):
    key = jax.random.fold_in(key, 13)
    first, second = jax.random.split(key)
    width = 2 * PA
    offdiag = jax.random.uniform(first, (2, width, width), jnp.float32, -0.03, 0.03)
    diagonal = jax.random.uniform(second, (width,), jnp.float32, 1.5, 3.0)
    steps = jnp.arange(width, dtype=jnp.int32)
    unit = (steps[:, None] == steps[None, :]).astype(jnp.float32)
    real_part = offdiag[0] * (1.0 - unit) + unit * diagonal[None, :]
    imag_part = offdiag[1] * (1.0 - unit)
    return jnp.stack([real_part, imag_part])


def draw_potential(key, part):
    key = jax.random.fold_in(key, 14)
    first, second = jax.random.split(key)
    shape = (NG, NG * NG)
    base = jax.random.uniform(first, shape, jnp.float32, 1.0, 2.0)
    field = jax.random.uniform(second, (3,) + shape, jnp.float32, -0.3, 0.3)
    return jnp.concatenate([base[None], field], axis=0)


def place_ends(entries, key, least, high):
    longest = entries.shape.index(max(entries.shape))
    spots = []
    for shift in (0, 1):
        where = [jax.random.randint(jax.random.fold_in(key, axis), (), 0, length) for axis, length in enumerate(entries.shape)]
        where[longest] = (where[longest] + shift) % entries.shape[longest]
        spots.append(tuple(where))
    return entries.at[spots[0]].set(least).at[spots[1]].set(high)


def shard_levels(key, dims, cuts, least, largest):
    loudness, own = 1.0, jax.random.fold_in(key, 6)
    for dim, parts in cuts:
        draws = jnp.exp(jax.random.uniform(jax.random.fold_in(own, dim), (parts,), jnp.float32, least / len(cuts), largest / len(cuts)))
        loudness = loudness * jnp.repeat(draws, dims[dim] // parts).reshape([-1 if axis == dim else 1 for axis in range(len(dims))])
    return loudness


def scatter_about(stream_key, shape, scale, limit, cuts=(), held_as=jnp.bfloat16):
    array = scale * jax.random.normal(stream_key, shape, jnp.float32)
    if cuts:
        array = array * shard_levels(stream_key, shape, cuts, -0.22, 0.18)
    return jnp.clip(array, -limit, limit).astype(held_as)


def setup_inputs(seed: int = 0) -> dict:
    splits = jax.random.split(jax.random.key(seed), 14)
    return {
        "orbitals": scatter_about(splits[0], (NK, NB, 4, NPW), 1.0, 6.0, ((0, 8), (3, 64)), jnp.float32),
        "response": scatter_about(splits[1], (NK, NB, 4, NPW), 1.0, 6.0, ((0, 8), (3, 64)), jnp.float32),
        "residual": draw_residual(jax.random.fold_in(splits[13], 71), 0),
        "old_direction": scatter_about(splits[3], (NK, NB, 4, NPW), 1.0, 6.0, ((0, 8), (3, 64)), jnp.float32),
        "old_norm": draw_old_norm(jax.random.fold_in(splits[13], 71), 0),
        "band_energy": jnp.clip(-1.0 + 1.4 * jax.random.uniform(splits[5], (NK, NB), jnp.float32) ** shard_levels(splits[5], (NK, NB), ((0, 8),), -0.2, 0.2), -1.0, 0.4),
        "kinetic": jnp.clip(jnp.exp(math.log(20.0) - 3.6888795 * jax.random.uniform(splits[6], (NK, NPW), jnp.float32) ** shard_levels(splits[6], (NK, NPW), ((0, 8), (1, 64)), -0.2, 0.2)), 0.5, 20.0),
        "form_factor": scatter_about(splits[7], (NK, 2, PA, NPW), NPW ** -0.5, 0.046875, ((0, 8), (3, 64)), jnp.float32),
        "sphere_index": draw_sphere_index(jax.random.fold_in(splits[13], 71), 0),
        "atom_positions": jnp.clip(jax.random.uniform(splits[9], (3, NATOM), jnp.float32, 0.0, 1.0), 0.0, 1.0),
        "proj_atom": place_ends(jax.random.randint(splits[10], (NPROJ,), 0, NATOM), jax.random.fold_in(splits[10], 1), 0, NATOM - 1).astype(jnp.int32),
        "coupling": draw_coupling(jax.random.fold_in(splits[13], 71), 0),
        "potential": draw_potential(jax.random.fold_in(splits[13], 71), 0),
    }


TWO_PI = 2.0 * math.pi
SMALL_TERM = 1e-6
HIGHEST = lax.Precision.HIGHEST


def contract(form_text, *operands):
    return jnp.einsum(form_text, *operands, precision=HIGHEST)


def frequencies(index, length):
    def signed(values):
        return jnp.where(values < length // 2, values, values - length).astype(jnp.float32)
    return signed(index // (length * length)), signed((index // length) % length), signed(index % length)


def projector_tables(form_factor, sphere_index, atom_positions, proj_atom, length):
    freq_x, freq_y, freq_z = frequencies(sphere_index, length)
    theta = TWO_PI * (atom_positions[0][:, None] * freq_x[None, :] + atom_positions[1][:, None] * freq_y[None, :] + atom_positions[2][:, None] * freq_z[None, :])
    cosine = jnp.cos(theta)
    sine = jnp.sin(theta)
    channels = form_factor.shape[1]
    slots = proj_atom.reshape(channels, -1)
    cos_rows = jnp.take(cosine, slots, axis=0)
    sin_rows = jnp.take(sine, slots, axis=0)
    real_part = form_factor[0][:, None, :]
    imag_part = form_factor[1][:, None, :]
    return real_part * cos_rows + imag_part * sin_rows, imag_part * cos_rows - real_part * sin_rows


def project(values, tab_real, tab_imag):
    val_real = values[:, 0::2]
    val_imag = values[:, 1::2]
    amp_real = contract('ckg,nsg->sckn', tab_real, val_real) + contract('ckg,nsg->sckn', tab_imag, val_imag)
    amp_imag = contract('ckg,nsg->sckn', tab_real, val_imag) - contract('ckg,nsg->sckn', tab_imag, val_real)
    return amp_real, amp_imag


def combine(amp_real, amp_imag, proj_atom, coupling):
    channels = amp_real.shape[1]
    atoms = amp_real.shape[2]
    slots = proj_atom.reshape(channels, atoms)
    onehot = (slots[:, None, :] == jnp.arange(atoms, dtype=jnp.int32)[None, :, None]).astype(amp_real.dtype)
    by_real = contract('cak,sckn->scan', onehot, amp_real)
    by_imag = contract('cak,sckn->scan', onehot, amp_imag)
    herm_real = (0.5 * (coupling[0] + coupling[0].T)).reshape(2, channels, 2, channels)
    herm_imag = (0.5 * (coupling[1] - coupling[1].T)).reshape(2, channels, 2, channels)
    out_real = contract('scte,tean->scan', herm_real, by_real) - contract('scte,tean->scan', herm_imag, by_imag)
    out_imag = contract('scte,tean->scan', herm_real, by_imag) + contract('scte,tean->scan', herm_imag, by_real)
    return contract('cak,scan->sckn', onehot, out_real), contract('cak,scan->sckn', onehot, out_imag)


def expand(q_real, q_imag, tab_real, tab_imag):
    new_real = contract('ckg,sckn->nsg', tab_real, q_real) - contract('ckg,sckn->nsg', tab_imag, q_imag)
    new_imag = contract('ckg,sckn->nsg', tab_real, q_imag) + contract('ckg,sckn->nsg', tab_imag, q_real)
    bands, points = new_real.shape[0], new_real.shape[2]
    return jnp.stack([new_real, new_imag], axis=2).reshape(bands, 4, points)


def apply_potential(values, potential):
    up_re, up_im, down_re, down_im = values[:, 0], values[:, 1], values[:, 2], values[:, 3]
    scalar, field_x, field_y, field_z = potential[0], potential[1], potential[2], potential[3]
    upper = scalar + field_z
    lower = scalar - field_z
    new_up_re = upper * up_re + field_x * down_re + field_y * down_im
    new_up_im = upper * up_im + field_x * down_im - field_y * down_re
    new_down_re = field_x * up_re - field_y * up_im + lower * down_re
    new_down_im = field_x * up_im + field_y * up_re + lower * down_im
    return jnp.stack([new_up_re, new_up_im, new_down_re, new_down_im], axis=1)


def density_terms(orbital, changed):
    up_re, up_im, down_re, down_im = orbital[:, 0], orbital[:, 1], orbital[:, 2], orbital[:, 3]
    ch_up_re, ch_up_im, ch_down_re, ch_down_im = changed[:, 0], changed[:, 1], changed[:, 2], changed[:, 3]
    same_up = up_re * ch_up_re + up_im * ch_up_im
    same_down = down_re * ch_down_re + down_im * ch_down_im
    charge = 2.0 * (same_up + same_down)
    spin_x = 2.0 * (up_re * ch_down_re + up_im * ch_down_im + down_re * ch_up_re + down_im * ch_up_im)
    spin_y = 2.0 * ((up_re * ch_down_im - up_im * ch_down_re) - (down_re * ch_up_im - down_im * ch_up_re))
    spin_z = 2.0 * (same_up - same_down)
    return jnp.stack([jnp.sum(charge, axis=0), jnp.sum(spin_x, axis=0), jnp.sum(spin_y, axis=0), jnp.sum(spin_z, axis=0)])


def to_real(coefficients, sphere_index):
    complex_values = lax.complex(coefficients[0::2], coefficients[1::2])
    box = jnp.zeros((2, NG * NG * NG), complex_values.dtype).at[:, sphere_index].set(complex_values)
    grid_values = jnp.fft.ifftn(box.reshape(2, NG, NG, NG), axes=(1, 2, 3)) * (NG * NG * NG)
    grid_values = jnp.transpose(grid_values, (0, 3, 1, 2)).reshape(2, NG, NG * NG)
    return jnp.stack([grid_values.real, grid_values.imag], axis=1).reshape(4, NG, NG * NG)


def to_recip(values, sphere_index):
    complex_values = lax.complex(values[0::2], values[1::2]).reshape(2, NG, NG, NG)
    complex_values = jnp.transpose(complex_values, (0, 2, 3, 1))
    spectrum = jnp.fft.fftn(complex_values, axes=(1, 2, 3)).reshape(2, NG * NG * NG) / (NG * NG * NG)
    picked = jnp.take(spectrum, sphere_index, axis=1)
    return jnp.stack([picked.real, picked.imag], axis=1).reshape(4, -1)


def one_point(orbitals, response, residual, old_direction, old_norm, band_energy, kinetic, form_factor, sphere_index, atom_positions, proj_atom, coupling, potential):
    norm_now = jnp.sum(residual * residual, axis=(1, 2))
    ratio = norm_now / old_norm
    direction = residual + ratio[:, None, None] * old_direction
    tab_real, tab_imag = projector_tables(form_factor, sphere_index, atom_positions, proj_atom, NG)
    amp_real, amp_imag = project(direction, tab_real, tab_imag)
    q_real, q_imag = combine(amp_real, amp_imag, proj_atom, coupling)
    nonlocal_term = expand(q_real, q_imag, tab_real, tab_imag)

    def potential_band(coefficients):
        grid_values = to_real(coefficients, sphere_index)
        return to_recip(apply_potential(grid_values[None], potential)[0], sphere_index)

    potential_term = lax.map(potential_band, direction)
    image = kinetic[None, None, :] * direction + potential_term + nonlocal_term - band_energy[:, None, None] * direction
    curvature = jnp.sum(direction * image, axis=(1, 2))
    step = norm_now / (curvature + SMALL_TERM)

    def density_band(total, items):
        coef_orbital, coef_response, coef_direction, band_step = items
        changed = to_real(coef_response, sphere_index) + band_step * to_real(coef_direction, sphere_index)
        return total + density_terms(to_real(coef_orbital, sphere_index)[None], changed[None]), None

    density, _ = lax.scan(density_band, jnp.zeros((4, NG, NG * NG), jnp.float32), (orbitals, response, direction, step))
    return response + step[:, None, None] * direction, residual - step[:, None, None] * image, direction, density


def reference(orbitals, response, residual, old_direction, old_norm, band_energy, kinetic, form_factor, sphere_index, atom_positions, proj_atom, coupling, potential):
    next_response, next_residual, directions = [], [], []
    density = jnp.zeros((4, NG, NG * NG), jnp.float32)
    for point in range(NK):
        result = one_point(orbitals[point], response[point], residual[point], old_direction[point], old_norm[point], band_energy[point], kinetic[point], form_factor[point], sphere_index[point], atom_positions, proj_atom, coupling, potential)
        next_response.append(result[0])
        next_residual.append(result[1])
        directions.append(result[2])
        density = density + result[3]
    density = density / (NK * NPW)
    return jnp.stack(next_response), jnp.stack(next_residual), jnp.stack(directions), density
```

```python
import math

import jax
import jax.numpy as jnp
from jax import lax
from jax.experimental import pallas as pl
from jax.experimental.pallas import tpu as pltpu
from jax.sharding import PartitionSpec as P

NG = 64
STICK = 32
NB = 8
COLS = 8
PW = COLS * STICK
PA = 16
DEV = 64
ALL = COLS * DEV
ROWS1 = 17
ROWS2 = 8
SMALL_TERM = 1e-06
VOLUME = 1.0 / (NG * NG * NG)
F32 = jnp.float32
BF16 = jnp.bfloat16
LIMIT = 48 * 1024 * 1024

COS = (1.0, -19.73920440673828, 64.93911743164062, -85.45014190673828,
       60.16762924194336, -25.967599868774414, 6.528658390045166)
SIN = (6.2831854820251465, -41.34170150756836, 81.60513305664062, -76.70301818847656,
       42.02592849731445, -14.899847030639648, 3.2381374835968018)


def iota(shape, dim):
    return lax.broadcasted_iota(jnp.int32, shape, dim)


def horner(coefficients, w):
    total = jnp.full_like(w, coefficients[-1])
    for c in coefficients[-2::-1]:
        total = total * w + c
    return total


def trig_turns(turns):
    r = turns - jnp.floor(turns + 0.5)
    w = r * r
    return horner(COS, w), r * horner(SIN, w)


def trig_wound(wound):
    r = (((wound + 32) & 63) - 32).astype(F32) * (1.0 / 64.0)
    w = r * r
    return horner(COS, w), r * horner(SIN, w)


def split(x):
    high = x.astype(BF16)
    return high, (x - high.astype(F32)).astype(BF16)


def dot(a, b, form="nn"):
    return lax.dot_general(
        a, b, (((1,), (0 if form == "nn" else 1,)), ((), ())), preferred_element_type=F32
    )


def dot3(a, b, form="nn"):
    return dot(a[0], b[0], form) + dot(a[1], b[0], form) + dot(a[0], b[1], form)


def swap_sign(x):
    lane = iota(x.shape, x.ndim - 1)
    return jnp.where(lane < 64, -1.0, 1.0) * pltpu.roll(x, 64, x.ndim - 1)


def row_to_col(row, n):
    shape = (n, row.shape[1])
    return jnp.sum(jnp.where(iota(shape, 0) == iota(shape, 1), row, 0.0), axis=1, keepdims=True)


def col_to_row(col, width):
    shape = (col.shape[0], width)
    return jnp.sum(jnp.where(iota(shape, 0) == iota(shape, 1), col, 0.0), axis=0, keepdims=True)


def signed(g):
    return jnp.where(g < 32, g, g - 64).astype(F32)


def atom_phases(index, positions):
    fx = signed(index >> 12)
    fy = signed((index >> 6) & 63)
    fz = signed(index & 63)
    tx, ty, tz = (row_to_col(positions[i : i + 1, :], NG) for i in range(3))
    turns = tx * fx + ty * fy + tz * fz
    cosine, sine = trig_turns(turns)
    return jnp.concatenate([cosine, sine], axis=0)


def depth_table():
    shape = (NG, PW)
    wound = iota(shape, 0) * ((iota(shape, 1) & 31) - 16)
    cosine, sine = trig_wound(wound)
    return jnp.concatenate([cosine, sine], axis=0)


def send_kernel(orb_ref, resp_ref, res_ref, old_ref, form_ref, index_ref, pos_ref, out_ref):
    arrays = (orb_ref, resp_ref, res_ref, old_ref)
    lines = jnp.concatenate(
        [ref[0, :, 2 * s + c, :] for c in range(2) for ref in arrays for s in range(2)], axis=0
    )
    lines = split(lines)
    table = depth_table()
    group = iota(table.shape, 1) >> 5
    for b in range(COLS):
        z = dot3(split(jnp.where(group == b, table, 0.0)), lines, "nt")
        out_ref[pl.ds(b, DEV, stride=ROWS1), :] = z[:64] + swap_sign(z[64:])

    index = index_ref[...]
    phases = split(atom_phases(index, pos_ref[...]))
    form_re, form_im = form_ref[0, 0], form_ref[0, 1]
    for n in range(NB):
        parts_re, parts_im = [], []
        for ref in arrays[2:]:
            for s in range(2):
                d_re = ref[0, n, 2 * s : 2 * s + 1, :]
                d_im = ref[0, n, 2 * s + 1 : 2 * s + 2, :]
                parts_re.append(form_re * d_re + form_im * d_im)
                parts_im.append(form_re * d_im - form_im * d_re)
        values = split(jnp.concatenate(parts_re + parts_im, axis=0))
        z = dot3(phases, values, "nt")
        out_ref[pl.ds(COLS + n, DEV, stride=ROWS1), :] = z[:64] + swap_sign(z[64:])

    squares = jnp.zeros((NB, PW), F32)
    for comp in range(4):
        r = res_ref[0, :, comp, :]
        squares = squares + r * r
    row = col_to_row(jnp.sum(squares, axis=1, keepdims=True), 128)
    codes = (index >> 6).astype(F32)
    lane = iota((1, PW), 1)
    target = iota((1, 128), 1)
    for b in range(COLS):
        code = jnp.sum(jnp.where(lane == STICK * b, codes, 0.0), axis=1, keepdims=True)
        row = jnp.where(target == COLS + b, code, row)
    out_ref[pl.ds(COLS + NB, DEV, stride=ROWS1), :] = jnp.broadcast_to(row, (DEV, 128))


def own_columns(recv_ref):
    values = jnp.concatenate(
        [recv_ref[pl.ds(b, DEV, stride=ROWS1), :] for b in range(COLS)], axis=0
    )
    return values.T


def column_codes(extra):
    turned = extra.T
    codes = jnp.concatenate(
        [turned[COLS + b : COLS + b + 1, :] for b in range(COLS)], axis=1
    ).astype(jnp.int32)
    return codes


def x_tables(codes, cos_ref, sin_ref):
    shape = (NG, ALL)
    cosine, sine = trig_wound(iota(shape, 0) * (codes >> 6))
    cos_ref[...] = cosine
    sin_ref[...] = sine


def y_forward(extra, table_ref):
    shape = (DEV, 128)
    lane = iota(shape, 1)
    for b in range(COLS):
        gy = extra[:, COLS + b : COLS + b + 1].astype(jnp.int32) & 63
        cosine, sine = trig_wound(gy * (lane & 63))
        first = jnp.where(lane < 64, cosine, sine)
        second = jnp.where(lane < 64, -sine, cosine)
        for c, part in ((0, first), (1, second)):
            high, low = split(part)
            rows = slice(c * ALL + b * DEV, c * ALL + (b + 1) * DEV)
            table_ref[rows, 0:128] = high
            table_ref[rows, 128:256] = low


def plane_chunk(re, im, first, count, cos_ref, sin_ref, table_ref, high_ref, low_ref):
    rows = re.shape[0]
    for i in range(count):
        cx = cos_ref[pl.ds(first + i, 1), :]
        sx = sin_ref[pl.ds(first + i, 1), :]
        for c, part in ((0, re * cx - im * sx), (1, re * sx + im * cx)):
            high, low = split(part)
            high_ref[i * rows : (i + 1) * rows, c * ALL : (c + 1) * ALL] = high
            low_ref[i * rows : (i + 1) * rows, c * ALL : (c + 1) * ALL] = low
    both = dot(high_ref[...], table_ref[...])
    return both[:, :128] + both[:, 128:] + dot(low_ref[...], table_ref[:, :128])


def potential_kernel(
    recv_ref, old_norm_ref, res_ref, old_ref, kin_ref, energy_ref, atom_ref, slots_ref,
    coup_ref, pot_ref, out_ref, grid_ref, scalars_ref,
    cos_ref, sin_ref, table_ref, back_high, back_low, high_ref, low_ref, prod_ref, pair_ref,
):
    extra = recv_ref[pl.ds(COLS + NB, DEV, stride=ROWS1), :]
    norm = row_to_col(jnp.sum(extra, axis=0, keepdims=True), NB)
    beta = norm / row_to_col(old_norm_ref[...], NB)
    codes = column_codes(extra)
    x_tables(codes, cos_ref, sin_ref)
    y_forward(extra, table_ref)
    cosine, sine = trig_wound(iota((NG, ALL), 0) * (codes & 63))
    for rows, parts in ((slice(0, 64), (cosine, -sine)), (slice(64, 128), (sine, cosine))):
        for c in range(2):
            high, low = split(parts[c])
            back_high[rows, c * ALL : (c + 1) * ALL] = high
            back_low[rows, c * ALL : (c + 1) * ALL] = low

    values = own_columns(recv_ref)
    beta2 = jnp.concatenate([beta, beta], axis=0)
    re = values[32:48] + beta2 * values[48:64]
    im = values[96:112] + beta2 * values[112:128]

    def chunk(k, carry):
        acc_re, acc_im, local = carry
        first = k * 16
        grid = plane_chunk(re, im, first, 16, cos_ref, sin_ref, table_ref, high_ref, low_ref)
        grid_ref[pl.ds(pl.multiple_of(k * 256, 256), 256), :] = grid
        for i in range(16):
            up = grid[i * 16 : i * 16 + 8]
            down = grid[i * 16 + 8 : i * 16 + 16]
            v0, bx, by, bz = (pot_ref[m, pl.ds(first + i, 1), :] for m in range(4))
            new_up = (v0 + bz) * up + bx * down - by * swap_sign(down)
            new_down = bx * up + by * swap_sign(up) + (v0 - bz) * down
            prod_ref[i * 16 : i * 16 + 8, :] = new_up
            prod_ref[i * 16 + 8 : i * 16 + 16, :] = new_down
            local = local + up * new_up + down * new_down
        prod = split(prod_ref[...])
        table = back_high[...]
        turned = dot(prod[0], table) + dot(prod[1], table) + dot(prod[0], back_low[...])
        for i in range(16):
            cx = cos_ref[pl.ds(first + i, 1), :]
            sx = sin_ref[pl.ds(first + i, 1), :]
            q_re = turned[i * 16 : (i + 1) * 16, :ALL]
            q_im = turned[i * 16 : (i + 1) * 16, ALL:]
            acc_re = acc_re + q_re * cx + q_im * sx
            acc_im = acc_im + q_im * cx - q_re * sx
        return acc_re, acc_im, local

    zero = jnp.zeros((16, ALL), F32)
    acc_re, acc_im, local = lax.fori_loop(0, 4, chunk, (zero, zero, jnp.zeros((NB, 128), F32)))
    acc_re = acc_re * VOLUME
    acc_im = acc_im * VOLUME
    for r in range(2):
        pieces = []
        for b in range(4 * r, 4 * r + 4):
            lanes = slice(b * DEV, (b + 1) * DEV)
            pieces += [acc_re[:, lanes], acc_im[:, lanes]]
        out_ref[pl.ds(r, DEV, stride=ROWS2), :] = jnp.concatenate(pieces, axis=0).T

    sums = [
        jnp.sum(recv_ref[pl.ds(COLS + n, DEV, stride=ROWS1), :], axis=0, keepdims=True)
        for n in range(NB)
    ]
    amps = jnp.concatenate(sums, axis=0)
    amps = amps + beta * pltpu.roll(amps, 96, 1)
    amp_re, amp_im = amps[:, 0:32], amps[:, 64:96]
    count = jnp.sum(
        jnp.where(slots_ref[...] == atom_ref[0], 1.0, 0.0), axis=1, keepdims=True
    )
    shape = (PA, 32)
    count = jnp.sum(
        jnp.where((iota(shape, 1) & 15) == iota(shape, 0), count, 0.0), axis=0, keepdims=True
    )
    h_re = 0.5 * (coup_ref[0] + coup_ref[0].T)
    h_im = 0.5 * (coup_ref[1] - coup_ref[1].T)
    by_re, by_im = amp_re * count, amp_im * count

    def exact(a, b):
        return lax.dot_general(
            a, b, (((1,), (0,)), ((), ())),
            precision=lax.Precision.HIGHEST, preferred_element_type=F32,
        )

    q_re = (exact(by_re, h_re) + exact(by_im, h_im)) * count
    q_im = (exact(by_im, h_re) - exact(by_re, h_im)) * count
    pair_ref[:, 0:32] = q_re
    pair_ref[:, 32:64] = q_im
    pair_ref[:, 64:128] = jnp.zeros((NB, 64), F32)
    even = pair_ref[pl.ds(0, 4, stride=2), :]
    odd = pair_ref[pl.ds(1, 4, stride=2), :]
    packed = even + pltpu.roll(odd, 64, 1)
    for k in range(4):
        out_ref[pl.ds(2 + k, DEV, stride=ROWS2), :] = jnp.broadcast_to(
            packed[k : k + 1], (DEV, 128)
        )

    curvature = jnp.sum(local, axis=1, keepdims=True) * VOLUME
    curvature = curvature + jnp.sum(amp_re * q_re + amp_im * q_im, axis=1, keepdims=True)
    weight = kin_ref[...] - row_to_col(energy_ref[...], NB)
    own = jnp.zeros((NB, PW), F32)
    for comp in range(4):
        d = res_ref[0, :, comp, :] + beta * old_ref[0, :, comp, :]
        own = own + d * d
    curvature = curvature + jnp.sum(own * weight, axis=1, keepdims=True)
    out_ref[pl.ds(6, DEV, stride=ROWS2), :] = jnp.broadcast_to(
        col_to_row(curvature, 128), (DEV, 128)
    )
    out_ref[pl.ds(7, DEV, stride=ROWS2), :] = jnp.zeros((DEV, 128), F32)
    lane = iota((NB, 128), 1)
    scalars_ref[...] = jnp.where(lane == 0, norm, jnp.where(lane == 1, beta, 0.0))


def orbital_kernel(recv_ref, grid_ref, cos_ref, sin_ref, table_ref, high_ref, low_ref):
    extra = recv_ref[pl.ds(COLS + NB, DEV, stride=ROWS1), :]
    x_tables(column_codes(extra), cos_ref, sin_ref)
    y_forward(extra, table_ref)
    values = own_columns(recv_ref)
    re, im = values[0:32], values[64:96]

    def chunk(k, carry):
        grid = plane_chunk(re, im, k * 8, 8, cos_ref, sin_ref, table_ref, high_ref, low_ref)
        grid_ref[pl.ds(pl.multiple_of(k * 256, 256), 256), :] = grid
        return carry

    lax.fori_loop(0, 8, chunk, 0)


def step_of(recv_ref, scalars_ref):
    total = jnp.sum(recv_ref[pl.ds(6, DEV, stride=ROWS2), :], axis=0, keepdims=True)
    return scalars_ref[:, 0:1] / (row_to_col(total, NB) + SMALL_TERM)


def density_kernel(recv_ref, scalars_ref, grid_ref, other_ref, out_ref):
    step = step_of(recv_ref, scalars_ref)
    step = jnp.broadcast_to(step, (NB, 128))
    lane = iota((1, 128), 1)

    def terms(x):
        base = pl.multiple_of(x * 32, 32)
        o_up = other_ref[pl.ds(base, 8), :]
        o_down = other_ref[pl.ds(base + 8, 8), :]
        half = pl.multiple_of(x * 16, 16)
        c_up = other_ref[pl.ds(base + 16, 8), :] + step * grid_ref[pl.ds(half, 8), :]
        c_down = other_ref[pl.ds(base + 24, 8), :] + step * grid_ref[pl.ds(half + 8, 8), :]
        same_up = o_up * c_up
        same_down = o_down * c_down
        parts = (
            same_up + same_down,
            o_up * c_down + o_down * c_up,
            o_down * swap_sign(c_up) - o_up * swap_sign(c_down),
            same_up - same_down,
        )
        sums = []
        for part in parts:
            row = jnp.sum(part, axis=0, keepdims=True)
            sums.append(2.0 * (row + pltpu.roll(row, 64, 1)))
        return sums

    def pair(p, carry):
        even = terms(2 * p)
        odd = terms(2 * p + 1)
        for m in range(4):
            row = jnp.where(lane < 64, even[m], odd[m])
            for copy in range(8):
                out_ref[pl.ds(copy * 128 + m * 32 + p, 1), :] = row
        return carry

    lax.fori_loop(0, 32, pair, 0, unroll=4)


def finish_kernel(
    recv_ref, scalars_ref, resp_ref, res_ref, old_ref, kin_ref, energy_ref, form_ref,
    index_ref, pos_ref, next_ref, residual_ref, direction_ref,
):
    step = step_of(recv_ref, scalars_ref)
    beta = scalars_ref[:, 1:2]
    table = depth_table()
    table = split(jnp.concatenate([table[:64], table[64:]], axis=1))
    group = iota((32, PW), 1) >> 5
    local = jnp.zeros((32, PW), F32)
    for r in range(2):
        values = recv_ref[pl.ds(r, DEV, stride=ROWS2), :].T
        z = dot3(split(values), table)
        for i in range(4):
            re_c, re_s = z[i * 32 : i * 32 + 16, :PW], z[i * 32 : i * 32 + 16, PW:]
            im_c, im_s = z[i * 32 + 16 : i * 32 + 32, :PW], z[i * 32 + 16 : i * 32 + 32, PW:]
            part = jnp.concatenate([re_c + im_s, im_c - re_s], axis=0)
            local = local + jnp.where(group == 4 * r + i, part, 0.0)

    phases = atom_phases(index_ref[...], pos_ref[...])
    phases = split(jnp.concatenate([phases[:64], phases[64:]], axis=1))
    form_re, form_im = form_ref[0, 0], form_ref[0, 1]
    rows_re, rows_im = [[], []], [[], []]
    for k in range(4):
        values = recv_ref[pl.ds(2 + k, DEV, stride=ROWS2), :].T
        z = dot3(split(values), phases)
        for i in range(2):
            for s in range(2):
                a = i * 64 + s * 16
                re_c, re_s = z[a : a + 16, :PW], z[a : a + 16, PW:]
                im_c, im_s = z[a + 32 : a + 48, :PW], z[a + 32 : a + 48, PW:]
                w_re = re_c + im_s
                w_im = im_c - re_s
                rows_re[s].append(
                    jnp.sum(form_re * w_re - form_im * w_im, axis=0, keepdims=True)
                )
                rows_im[s].append(
                    jnp.sum(form_re * w_im + form_im * w_re, axis=0, keepdims=True)
                )
    weight = kin_ref[...] - row_to_col(energy_ref[...], NB)
    for s in range(2):
        for c in range(2):
            comp = 2 * s + c
            nonlocal_term = jnp.concatenate((rows_re, rows_im)[c][s], axis=0)
            residual = res_ref[0, :, comp, :]
            direction = residual + beta * old_ref[0, :, comp, :]
            place = c * 16 + s * 8
            image = weight * direction + local[place : place + 8] + nonlocal_term
            direction_ref[0, :, comp, :] = direction
            next_ref[0, :, comp, :] = resp_ref[0, :, comp, :] + step * direction
            residual_ref[0, :, comp, :] = residual - step * image


def call(kernel, outs, name, scratch=(), flops=1, size=1, smem=()):
    def run(*args):
        specs = [
            pl.BlockSpec(memory_space=pltpu.SMEM if i in smem else pltpu.VMEM)
            for i in range(len(args))
        ]
        single = not isinstance(outs, (list, tuple))
        return pl.pallas_call(
            kernel,
            out_shape=outs,
            in_specs=specs,
            out_specs=jax.tree.map(lambda _: pl.BlockSpec(memory_space=pltpu.VMEM), outs),
            scratch_shapes=list(scratch),
            compiler_params=pltpu.CompilerParams(vmem_limit_bytes=LIMIT),
            cost_estimate=pl.CostEstimate(flops=flops, bytes_accessed=size, transcendentals=0),
            name=name,
        )(*args)

    return run


def shape_of(*dims):
    return jax.ShapeDtypeStruct(dims, F32)


def exchange(values, axis, parts):
    rows = values.shape[0] // parts
    if rows % 8:
        flat = values.reshape(parts, 1, rows * 128)
        flat = lax.all_to_all(flat, axis, 0, 0, tiled=True)
        return flat.reshape(values.shape)
    out = lax.all_to_all(values.reshape(parts, rows, 128), axis, 0, 0, tiled=True)
    return out.reshape(values.shape)


def per_device(
    orbitals, response, residual, old_direction, old_norm, band_energy, kinetic, form_factor,
    sphere_index, atom_positions, proj_atom, coupling, potential,
):
    scale = 1.0 / (8 * 16384)
    me = lax.axis_index("fft").reshape(1).astype(jnp.int32)
    slots = proj_atom.reshape(PA, NG)
    plane = potential.reshape(4, NG, NG)
    plane = jnp.concatenate([plane, plane], axis=2)

    sent = call(send_kernel, shape_of(DEV * ROWS1, 128), "lines_and_amplitudes")(
        orbitals, response, residual, old_direction, form_factor, sphere_index, atom_positions
    )
    recv = exchange(sent, "fft", DEV)
    tables = [
        pltpu.VMEM((NG, ALL), F32), pltpu.VMEM((NG, ALL), F32),
        pltpu.VMEM((2 * ALL, 256), BF16),
    ]
    wide = [pltpu.VMEM((256, 2 * ALL), BF16), pltpu.VMEM((256, 2 * ALL), BF16)]
    back, grid, scalars = call(
        potential_kernel,
        (shape_of(DEV * ROWS2, 128), shape_of(NG * 16, 128), shape_of(NB, 128)),
        "potential_and_coupling",
        tables + [pltpu.VMEM((128, 2 * ALL), BF16), pltpu.VMEM((128, 2 * ALL), BF16)] + wide
        + [pltpu.VMEM((256, 128), F32), pltpu.VMEM((NB, 128), F32)],
        smem=(6,),
    )(recv, old_norm, residual, old_direction, kinetic, band_energy, me, slots, coupling, plane)
    returned = exchange(back, "fft", DEV)
    other = call(
        orbital_kernel, shape_of(NG * 32, 128), "orbital_and_response_grid", tables + wide,
        flops=3_000_000_000, size=3_000_000,
    )(recv)
    density = call(density_kernel, shape_of(8 * 128, 128), "density")(
        returned, scalars, grid, other
    )
    gathered = exchange(density, "kpool", 8)
    outs = call(
        finish_kernel, (shape_of(1, NB, 4, PW),) * 3, "new_vectors",
        flops=3_000_000_000, size=3_000_000,
    )(
        returned, scalars, response, residual, old_direction, kinetic, band_energy, form_factor,
        sphere_index, atom_positions,
    )
    total = jnp.sum(gathered.reshape(8, 128, 128), axis=0) * scale
    return outs[0], outs[1], outs[2], total.reshape(4, 1, NG * NG)


def solution(mesh):
    vector = P("kpool", None, None, "fft")
    in_specs = (
        vector, vector, vector, vector, P("kpool", None), P("kpool", None), P("kpool", "fft"),
        vector, P("kpool", "fft"), P(), P(), P(), P(None, "fft", None),
    )
    out_specs = (vector, vector, vector, P(None, "fft", None))
    return jax.shard_map(
        per_device, mesh=mesh, in_specs=in_specs, out_specs=out_specs, check_vma=False
    )
```

```python
import math

import jax
import jax.numpy as jnp
from jax import lax
from jax.experimental import pallas as pl
from jax.experimental.pallas import tpu as pltpu
from jax.sharding import PartitionSpec as P

NG = 64
STICK = 32
NB = 8
COLS = 8
PW = COLS * STICK
PA = 16
DEV = 64
EXTRA = 16
MIRROR = [(i, i ^ 1) for i in range(DEV)]
HALF = NG // 2
ALL = COLS * DEV
ROWS1 = 17
ROWS2 = 5
SMALL_TERM = 1e-06
VOLUME = 1.0 / (NG * NG * NG)
F32 = jnp.float32
BF16 = jnp.bfloat16
LIMIT = 48 * 1024 * 1024

COS = (1.0, -19.73920440673828, 64.93911743164062, -85.45014190673828,
       60.16762924194336, -25.967599868774414, 6.528658390045166)
SIN = (6.2831854820251465, -41.34170150756836, 81.60513305664062, -76.70301818847656,
       42.02592849731445, -14.899847030639648, 3.2381374835968018)


def iota(shape, dim):
    return lax.broadcasted_iota(jnp.int32, shape, dim)


def horner(coefficients, w):
    total = jnp.full_like(w, coefficients[-1])
    for c in coefficients[-2::-1]:
        total = total * w + c
    return total


def trig_turns(turns):
    r = turns - jnp.floor(turns + 0.5)
    w = r * r
    return horner(COS, w), r * horner(SIN, w)


def trig_wound(wound):
    r = (((wound + 32) & 63) - 32).astype(F32) * (1.0 / 64.0)
    w = r * r
    return horner(COS, w), r * horner(SIN, w)


def split(x):
    high = x.astype(BF16)
    return high, (x - high.astype(F32)).astype(BF16)


def dot(a, b, form="nn"):
    return lax.dot_general(
        a, b, (((1,), (0 if form == "nn" else 1,)), ((), ())), preferred_element_type=F32
    )


def dot3(a, b, form="nn"):
    return dot(a[0], b[0], form) + dot(a[1], b[0], form) + dot(a[0], b[1], form)


def swap_sign(x):
    lane = iota(x.shape, x.ndim - 1)
    return jnp.where(lane < 64, -1.0, 1.0) * pltpu.roll(x, 64, x.ndim - 1)


def row_to_col(row, n):
    shape = (n, row.shape[1])
    return jnp.sum(jnp.where(iota(shape, 0) == iota(shape, 1), row, 0.0), axis=1, keepdims=True)


def col_to_row(col, width):
    shape = (col.shape[0], width)
    return jnp.sum(jnp.where(iota(shape, 0) == iota(shape, 1), col, 0.0), axis=0, keepdims=True)


def signed(g):
    return jnp.where(g < 32, g, g - 64).astype(F32)


def atom_phases(index, positions):
    fx = signed(index >> 12)
    fy = signed((index >> 6) & 63)
    fz = signed(index & 63)
    tx, ty, tz = (row_to_col(positions[i : i + 1, :], NG) for i in range(3))
    turns = tx * fx + ty * fy + tz * fz
    cosine, sine = trig_turns(turns)
    return jnp.concatenate([cosine, sine], axis=0)


def depth_table():
    shape = (NG, PW)
    wound = iota(shape, 0) * ((iota(shape, 1) & 31) - 16)
    cosine, sine = trig_wound(wound)
    return jnp.concatenate([cosine, sine], axis=0)


def send_kernel(
    orb_hbm, resp_hbm, res_hbm, old_hbm, form_hbm, index_hbm, pos_hbm, out_ref,
    orb_ref, resp_ref, res_ref, old_ref, form_ref, index_ref, pos_ref, sems,
):
    arrays = (orb_ref, resp_ref, res_ref, old_ref)
    copies = fetch(
        (
            (orb_hbm, orb_ref), (resp_hbm, resp_ref), (res_hbm, res_ref), (old_hbm, old_ref),
            (form_hbm, form_ref), (index_hbm, index_ref), (pos_hbm, pos_ref),
        ),
        sems,
    )
    table = depth_table()
    for copy in copies:
        copy.wait()
    lines = jnp.concatenate(
        [ref[0, :, 2 * s + c, :] for c in range(2) for ref in arrays for s in range(2)], axis=0
    )
    lines = split(lines)
    group = iota(table.shape, 1) >> 5
    for b in range(COLS):
        z = dot3(split(jnp.where(group == b, table, 0.0)), lines, "nt")
        out_ref[pl.ds(b, DEV, stride=ROWS1), :] = z[:64] + swap_sign(z[64:])

    index = index_ref[...]
    phases = split(atom_phases(index, pos_ref[...]))
    form_re, form_im = form_ref[0, 0], form_ref[0, 1]
    for n in range(NB):
        parts_re, parts_im = [], []
        for ref in arrays[2:]:
            for s in range(2):
                d_re = ref[0, n, 2 * s : 2 * s + 1, :]
                d_im = ref[0, n, 2 * s + 1 : 2 * s + 2, :]
                parts_re.append(form_re * d_re + form_im * d_im)
                parts_im.append(form_re * d_im - form_im * d_re)
        values = split(jnp.concatenate(parts_re + parts_im, axis=0))
        z = dot3(phases, values, "nt")
        out_ref[pl.ds(COLS + n, DEV, stride=ROWS1), :] = z[:64] + swap_sign(z[64:])

    squares = jnp.zeros((NB, PW), F32)
    for comp in range(4):
        r = res_ref[0, :, comp, :]
        squares = squares + r * r
    row = col_to_row(jnp.sum(squares, axis=1, keepdims=True), 128)
    codes = (index >> 6).astype(F32)
    lane = iota((1, PW), 1)
    target = iota((1, 128), 1)
    for b in range(COLS):
        code = jnp.sum(jnp.where(lane == STICK * b, codes, 0.0), axis=1, keepdims=True)
        row = jnp.where(target == COLS + b, code, row)
    out_ref[pl.ds(EXTRA, DEV, stride=ROWS1), :] = jnp.broadcast_to(row, (DEV, 128))


def own_columns(recv_ref):
    values = jnp.concatenate(
        [recv_ref[pl.ds(b, DEV, stride=ROWS1), :] for b in range(COLS)], axis=0
    )
    return values.T


def column_codes(extra):
    turned = extra.T
    codes = jnp.concatenate(
        [turned[COLS + b : COLS + b + 1, :] for b in range(COLS)], axis=1
    ).astype(jnp.int32)
    return codes


def x_tables(codes, cos_ref, sin_ref):
    shape = (HALF, ALL)
    cosine, sine = trig_wound(iota(shape, 0) * (codes >> 6))
    cos_ref[...] = cosine
    sin_ref[...] = sine


def y_tables(extra, high_ref, low_ref):
    shape = (DEV, 128)
    lane = iota(shape, 1)
    for b in range(COLS):
        code = extra[:, COLS + b : COLS + b + 1].astype(jnp.int32)
        wound = (code & 63) * (lane & 63)
        cosine, sine = trig_wound(wound)
        odd = jnp.broadcast_to(((code >> 6) & 1) == 1, shape)
        first = jnp.where(lane < 64, cosine, sine)
        second = jnp.where(lane < 64, -sine, cosine)
        for c, part in ((0, first), (1, second)):
            rows = slice(c * ALL + b * DEV, c * ALL + (b + 1) * DEV)
            for parity, mine in ((0, jnp.where(odd, 0.0, part)), (1, jnp.where(odd, part, 0.0))):
                high, low = split(mine)
                high_ref[rows, parity * 128 : (parity + 1) * 128] = high
                low_ref[rows, parity * 128 : (parity + 1) * 128] = low


def plane_chunk(re, im, first, count, cos_ref, sin_ref, tables, scratch):
    rows = re.shape[0]
    high_ref, low_ref = scratch
    for i in range(count):
        cx = cos_ref[pl.ds(first + i, 1), :]
        sx = sin_ref[pl.ds(first + i, 1), :]
        for c, part in ((0, re * cx - im * sx), (1, re * sx + im * cx)):
            high, low = split(part)
            high_ref[i * rows : (i + 1) * rows, c * ALL : (c + 1) * ALL] = high
            low_ref[i * rows : (i + 1) * rows, c * ALL : (c + 1) * ALL] = low
    high = high_ref[...]
    table = tables[0][...]
    both = dot(high, table) + dot(low_ref[...], table) + dot(high, tables[1][...])
    return both[:, :128] + both[:, 128:], both[:, :128] - both[:, 128:]


def fetch(pairs, sems):
    copies = [
        pltpu.make_async_copy(source, target, sems.at[i])
        for i, (source, target) in enumerate(pairs)
    ]
    for copy in copies:
        copy.start()
    return copies


def potential_kernel(
    recv_ref, atom_ref, slots_ref, pot_ref, old_norm_hbm, res_hbm, old_hbm, kin_hbm,
    energy_hbm, coup_hbm,
    out_ref, grid_ref, scalars_ref,
    old_norm_ref, res_ref, old_ref, kin_ref, energy_ref, coup_ref, sems,
    cos_ref, sin_ref, table_high, table_low, high_ref, low_ref, prod_ref, pair_ref,
):
    copies = fetch(
        (
            (old_norm_hbm, old_norm_ref), (res_hbm, res_ref), (old_hbm, old_ref),
            (kin_hbm, kin_ref), (energy_hbm, energy_ref), (coup_hbm, coup_ref),
        ),
        sems,
    )
    extra = recv_ref[pl.ds(EXTRA, DEV, stride=ROWS1), :]
    codes = column_codes(extra)
    x_tables(codes, cos_ref, sin_ref)
    y_tables(extra, table_high, table_low)
    tables = (table_high, table_low)
    for copy in copies:
        copy.wait()
    norm = row_to_col(jnp.sum(extra, axis=0, keepdims=True), NB)
    beta = norm / row_to_col(old_norm_ref[...], NB)
    values = own_columns(recv_ref)
    beta2 = jnp.concatenate([beta, beta], axis=0)
    re = values[32:48] + beta2 * values[48:64]
    im = values[96:112] + beta2 * values[112:128]

    acc_re = jnp.zeros((16, ALL), F32)
    acc_im = jnp.zeros((16, ALL), F32)
    local = jnp.zeros((NB, 128), F32)
    for k in range(2):
        first = k * 16
        grids = plane_chunk(re, im, first, 16, cos_ref, sin_ref, tables, (high_ref.at[k], low_ref.at[k]))
        for i in range(16):
            products = []
            for half in range(2):
                grid = grids[half]
                x = first + i + 32 * half
                up = grid[i * 16 : i * 16 + 8]
                down = grid[i * 16 + 8 : i * 16 + 16]
                grid_ref[x * 16 : x * 16 + 8, :] = up
                grid_ref[x * 16 + 8 : x * 16 + 16, :] = down
                v0, bx, by, bz = (pot_ref[m, x : x + 1, :] for m in range(4))
                new_up = (v0 + bz) * up + bx * down - by * swap_sign(down)
                new_down = bx * up + by * swap_sign(up) + (v0 - bz) * down
                local = local + up * new_up + down * new_down
                products.append((new_up, new_down))
            for j in range(2):
                rows = slice(i * 16 + 8 * j, i * 16 + 8 * j + 8)
                prod_ref[k, rows, 0:128] = products[0][j] + products[1][j]
                prod_ref[k, rows, 128:256] = products[0][j] - products[1][j]
        turned = dot3(split(prod_ref[k]), (table_high[...], table_low[...]), "nt")
        for i in range(16):
            cx = cos_ref[first + i : first + i + 1, :]
            sx = sin_ref[first + i : first + i + 1, :]
            q_re = turned[i * 16 : (i + 1) * 16, :ALL]
            q_im = turned[i * 16 : (i + 1) * 16, ALL:]
            acc_re = acc_re + q_re * cx + q_im * sx
            acc_im = acc_im + q_im * cx - q_re * sx
    acc_re = acc_re * VOLUME
    acc_im = acc_im * VOLUME
    for r in range(2):
        pieces = []
        for b in range(4 * r, 4 * r + 4):
            lanes = slice(b * DEV, (b + 1) * DEV)
            pieces += [acc_re[:, lanes], acc_im[:, lanes]]
        out_ref[pl.ds(r, DEV, stride=ROWS2), :] = jnp.concatenate(pieces, axis=0).T

    sums = [
        jnp.sum(recv_ref[pl.ds(COLS + n, DEV, stride=ROWS1), :], axis=0, keepdims=True)
        for n in range(NB)
    ]
    amps = jnp.concatenate(sums, axis=0)
    amps = amps + beta * pltpu.roll(amps, 96, 1)
    amp_re, amp_im = amps[:, 0:32], amps[:, 64:96]
    count = jnp.sum(
        jnp.where(slots_ref[...] == atom_ref[0], 1.0, 0.0), axis=1, keepdims=True
    )
    shape = (PA, 32)
    count = jnp.sum(
        jnp.where((iota(shape, 1) & 15) == iota(shape, 0), count, 0.0), axis=0, keepdims=True
    )
    h_re = 0.5 * (coup_ref[0] + coup_ref[0].T)
    h_im = 0.5 * (coup_ref[1] - coup_ref[1].T)
    by_re, by_im = amp_re * count, amp_im * count

    def exact(a, b):
        return lax.dot_general(
            a, b, (((1,), (0,)), ((), ())),
            precision=lax.Precision.HIGHEST, preferred_element_type=F32,
        )

    q_re = (exact(by_re, h_re) + exact(by_im, h_im)) * count
    q_im = (exact(by_im, h_re) - exact(by_re, h_im)) * count
    pair_ref[:, 0:32] = q_re
    pair_ref[:, 32:64] = q_im
    pair_ref[:, 64:128] = jnp.zeros((NB, 64), F32)
    first_half = pair_ref[pl.ds(0, 4, stride=2), :]
    second_half = pair_ref[pl.ds(1, 4, stride=2), :]
    packed = first_half + pltpu.roll(second_half, 64, 1)
    odd = (iota((DEV, 128), 0) & 1) == 1
    for k in range(2):
        out_ref[pl.ds(2 + k, DEV, stride=ROWS2), :] = jnp.where(
            odd, packed[2 + k : 3 + k], packed[k : k + 1]
        )

    curvature = jnp.sum(local, axis=1, keepdims=True) * VOLUME
    curvature = curvature + jnp.sum(amp_re * q_re + amp_im * q_im, axis=1, keepdims=True)
    weight = kin_ref[...] - row_to_col(energy_ref[...], NB)
    own = jnp.zeros((NB, PW), F32)
    for comp in range(4):
        d = res_ref[0, :, comp, :] + beta * old_ref[0, :, comp, :]
        own = own + d * d
    curvature = curvature + jnp.sum(own * weight, axis=1, keepdims=True)
    out_ref[pl.ds(4, DEV, stride=ROWS2), :] = jnp.broadcast_to(
        col_to_row(curvature, 128), (DEV, 128)
    )
    lane = iota((NB, 128), 1)
    scalars_ref[...] = jnp.where(lane == 0, norm, jnp.where(lane == 1, beta, 0.0))


def orbital_kernel(
    recv_ref, grid_ref, cos_ref, sin_ref, table_high, table_low, high_ref, low_ref
):
    extra = recv_ref[pl.ds(EXTRA, DEV, stride=ROWS1), :]
    x_tables(column_codes(extra), cos_ref, sin_ref)
    y_tables(extra, table_high, table_low)
    values = own_columns(recv_ref)
    re, im = values[0:32], values[64:96]

    def chunk(k, carry):
        grids = plane_chunk(
            re, im, k * 8, 8, cos_ref, sin_ref, (table_high, table_low), (high_ref, low_ref)
        )
        for half in range(2):
            place = pl.multiple_of(k * 256 + half * 1024, 256)
            grid_ref[pl.ds(place, 256), :] = grids[half]
        return carry

    lax.fori_loop(0, 4, chunk, 0)


def step_of(recv_ref, scalars_ref):
    total = jnp.sum(recv_ref[pl.ds(4, DEV, stride=ROWS2), :], axis=0, keepdims=True)
    return scalars_ref[:, 0:1] / (row_to_col(total, NB) + SMALL_TERM)


def density_kernel(
    recv_ref, scalars_ref, grid_ref, other_ref, out_ref, half_ref, sum_ref
):
    step = jnp.broadcast_to(step_of(recv_ref, scalars_ref), (NB, 128))
    lane = iota((NB, 128), 1)

    def terms(x):
        base = pl.multiple_of(x * 32, 32)
        o_up = other_ref[pl.ds(base, 8), :]
        o_down = other_ref[pl.ds(base + 8, 8), :]
        half = pl.multiple_of(x * 16, 16)
        c_up = other_ref[pl.ds(base + 16, 8), :] + step * grid_ref[pl.ds(half, 8), :]
        c_down = other_ref[pl.ds(base + 24, 8), :] + step * grid_ref[pl.ds(half + 8, 8), :]
        same_up = o_up * c_up
        same_down = o_down * c_down
        return (
            same_up + same_down,
            o_up * c_down + o_down * c_up,
            o_down * swap_sign(c_up) - o_up * swap_sign(c_down),
            same_up - same_down,
        )

    def pair(p, carry):
        even = terms(2 * p)
        odd = terms(2 * p + 1)
        for m in range(4):
            both = jnp.where(lane < 64, even[m], odd[m]) + pltpu.roll(
                jnp.where(lane < 64, odd[m], even[m]), 64, 1
            )
            sum_ref[pl.ds(m * 32 + p, 1), :] = 2.0 * jnp.sum(both, axis=0, keepdims=True)
        return carry

    lax.fori_loop(0, 32, pair, 0, unroll=8)
    total = sum_ref[...]
    for copy in range(8):
        out_ref[copy * 128 : (copy + 1) * 128, :] = total
    for k in range(2):
        half_ref[k * DEV : (k + 1) * DEV, :] = recv_ref[pl.ds(2 + k, DEV, stride=ROWS2), :]


def finish_kernel(
    parity_ref, half_ref, other_ref, recv_ref, scalars_ref, resp_ref, res_ref, old_ref, kin_ref, energy_ref, form_ref,
    index_ref, pos_ref, next_ref, residual_ref, direction_ref,
):
    step = step_of(recv_ref, scalars_ref)
    beta = scalars_ref[:, 1:2]
    table = depth_table()
    table = split(jnp.concatenate([table[:64], table[64:]], axis=1))
    group = iota((32, PW), 1) >> 5
    local = jnp.zeros((32, PW), F32)
    for r in range(2):
        values = recv_ref[pl.ds(r, DEV, stride=ROWS2), :].T
        z = dot3(split(values), table)
        for i in range(4):
            re_c, re_s = z[i * 32 : i * 32 + 16, :PW], z[i * 32 : i * 32 + 16, PW:]
            im_c, im_s = z[i * 32 + 16 : i * 32 + 32, :PW], z[i * 32 + 16 : i * 32 + 32, PW:]
            part = jnp.concatenate([re_c + im_s, im_c - re_s], axis=0)
            local = local + jnp.where(group == 4 * r + i, part, 0.0)

    phases = atom_phases(index_ref[...], pos_ref[...])
    phases = split(jnp.concatenate([phases[:64], phases[64:]], axis=1))
    form_re, form_im = form_ref[0, 0], form_ref[0, 1]
    rows_re, rows_im = [[], []], [[], []]
    for k in range(4):
        rows = slice((k & 1) * DEV, (k & 1) * DEV + DEV)
        mine = parity_ref[0] == (k >> 1)
        values = jnp.where(mine, half_ref[rows, :], other_ref[rows, :]).T
        z = dot3(split(values), phases)
        for i in range(2):
            for s in range(2):
                a = i * 64 + s * 16
                re_c, re_s = z[a : a + 16, :PW], z[a : a + 16, PW:]
                im_c, im_s = z[a + 32 : a + 48, :PW], z[a + 32 : a + 48, PW:]
                w_re = re_c + im_s
                w_im = im_c - re_s
                rows_re[s].append(
                    jnp.sum(form_re * w_re - form_im * w_im, axis=0, keepdims=True)
                )
                rows_im[s].append(
                    jnp.sum(form_re * w_im + form_im * w_re, axis=0, keepdims=True)
                )
    weight = kin_ref[...] - row_to_col(energy_ref[...], NB)
    for s in range(2):
        for c in range(2):
            comp = 2 * s + c
            nonlocal_term = jnp.concatenate((rows_re, rows_im)[c][s], axis=0)
            residual = res_ref[0, :, comp, :]
            direction = residual + beta * old_ref[0, :, comp, :]
            place = c * 16 + s * 8
            image = weight * direction + local[place : place + 8] + nonlocal_term
            direction_ref[0, :, comp, :] = direction
            next_ref[0, :, comp, :] = resp_ref[0, :, comp, :] + step * direction
            residual_ref[0, :, comp, :] = residual - step * image


def call(kernel, outs, name, scratch=(), flops=1, size=1, smem=(), hbm=()):
    def space(i):
        return pltpu.SMEM if i in smem else pltpu.HBM if i in hbm else pltpu.VMEM

    def run(*args):
        specs = [pl.BlockSpec(memory_space=space(i)) for i in range(len(args))]
        args = [
            pltpu.with_memory_space_constraint(a, pltpu.HBM) if i in hbm else a
            for i, a in enumerate(args)
        ]
        return pl.pallas_call(
            kernel,
            out_shape=outs,
            in_specs=specs,
            out_specs=jax.tree.map(lambda _: pl.BlockSpec(memory_space=pltpu.VMEM), outs),
            scratch_shapes=list(scratch),
            compiler_params=pltpu.CompilerParams(vmem_limit_bytes=LIMIT),
            cost_estimate=pl.CostEstimate(flops=flops, bytes_accessed=size, transcendentals=0),
            name=name,
        )(*args)

    return run


def shape_of(*dims):
    return jax.ShapeDtypeStruct(dims, F32)


def exchange(values, axis, parts):
    rows = values.shape[0] // parts
    if rows % 8:
        flat = values.reshape(parts, 1, rows * 128)
        flat = lax.all_to_all(flat, axis, 0, 0, tiled=True)
        return flat.reshape(values.shape)
    out = lax.all_to_all(values.reshape(parts, rows, 128), axis, 0, 0, tiled=True)
    return out.reshape(values.shape)


def per_device(
    orbitals, response, residual, old_direction, old_norm, band_energy, kinetic, form_factor,
    sphere_index, atom_positions, proj_atom, coupling, potential,
):
    scale = 1.0 / (8 * 16384)
    me = lax.axis_index("fft").reshape(1).astype(jnp.int32)
    slots = proj_atom.reshape(PA, NG)
    plane = potential.reshape(4, NG, NG)
    plane = jnp.concatenate([plane, plane], axis=2)

    parity = me & 1
    vector = pltpu.VMEM((1, NB, 4, PW), F32)
    sent = call(
        send_kernel, shape_of(DEV * ROWS1, 128), "lines_and_amplitudes",
        [vector] * 4 + [
            pltpu.VMEM((1, 2, PA, PW), F32), pltpu.VMEM((1, PW), jnp.int32),
            pltpu.VMEM((3, NG), F32), pltpu.SemaphoreType.DMA((7,)),
        ],
        hbm=range(7),
    )(orbitals, response, residual, old_direction, form_factor, sphere_index, atom_positions)
    recv = exchange(sent, "fft", DEV)
    tables = [
        pltpu.VMEM((HALF, ALL), F32), pltpu.VMEM((HALF, ALL), F32),
        pltpu.VMEM((2 * ALL, 256), BF16), pltpu.VMEM((2 * ALL, 256), BF16),
    ]
    back, grid, scalars = call(
        potential_kernel,
        (shape_of(DEV * ROWS2, 128), shape_of(NG * 16, 128), shape_of(NB, 128)),
        "potential_and_coupling",
        [
            pltpu.VMEM((1, NB), F32), vector, vector, pltpu.VMEM((1, PW), F32),
            pltpu.VMEM((1, NB), F32), pltpu.VMEM((2, 32, 32), F32),
            pltpu.SemaphoreType.DMA((6,)),
        ]
        + tables
        + [pltpu.VMEM((2, 256, 2 * ALL), BF16), pltpu.VMEM((2, 256, 2 * ALL), BF16)]
        + [pltpu.VMEM((2, 256, 256), F32), pltpu.VMEM((NB, 128), F32)],
        smem=(1,), hbm=range(4, 10),
    )(recv, me, slots, plane, old_norm, residual, old_direction, kinetic, band_energy, coupling)
    returned = exchange(back, "fft", DEV)
    other = call(
        orbital_kernel, shape_of(NG * 32, 128), "orbital_and_response_grid",
        tables + [pltpu.VMEM((256, 2 * ALL), BF16), pltpu.VMEM((256, 2 * ALL), BF16)],
        flops=3_000_000_000, size=3_000_000,
    )(recv)
    density, half = call(
        density_kernel, (shape_of(8 * 128, 128), shape_of(2 * DEV, 128)), "density",
        [pltpu.VMEM((128, 128), F32)],
    )(returned, scalars, grid, other)
    gathered = exchange(density, "kpool", 8)
    other_half = lax.ppermute(half, "fft", MIRROR)
    outs = call(
        finish_kernel, (shape_of(1, NB, 4, PW),) * 3, "new_vectors",
        flops=3_000_000_000, size=3_000_000, smem=(0,),
    )(
        parity, half, other_half, returned, scalars, response, residual, old_direction, kinetic, band_energy, form_factor,
        sphere_index, atom_positions,
    )
    total = jnp.sum(gathered.reshape(8, 128, 128), axis=0) * scale
    return outs[0], outs[1], outs[2], total.reshape(4, 1, NG * NG)


def solution(mesh):
    vector = P("kpool", None, None, "fft")
    in_specs = (
        vector, vector, vector, vector, P("kpool", None), P("kpool", None), P("kpool", "fft"),
        vector, P("kpool", "fft"), P(), P(), P(), P(None, "fft", None),
    )
    out_specs = (vector, vector, vector, P(None, "fft", None))
    return jax.shard_map(
        per_device, mesh=mesh, in_specs=in_specs, out_specs=out_specs, check_vma=False
    )
```

```python
import math

import jax
import jax.numpy as jnp
from jax import lax
from jax.experimental import pallas as pl
from jax.experimental.pallas import tpu as pltpu
from jax.sharding import PartitionSpec as P

NG = 64
STICK = 32
NB = 8
COLS = 8
PW = COLS * STICK
PA = 16
DEV = 64
EXTRA = 16
MIRROR = [(i, i ^ 1) for i in range(DEV)]
HALF = NG // 2
CH = 2
CX = HALF // CH
ALL = COLS * DEV
ROWS1 = 17
ROWS2 = 5
SMALL_TERM = 1e-06
VOLUME = 1.0 / (NG * NG * NG)
F32 = jnp.float32
BF16 = jnp.bfloat16
LIMIT = 48 * 1024 * 1024

COS = (1.0, -19.73920440673828, 64.93911743164062, -85.45014190673828,
       60.16762924194336, -25.967599868774414, 6.528658390045166)
SIN = (6.2831854820251465, -41.34170150756836, 81.60513305664062, -76.70301818847656,
       42.02592849731445, -14.899847030639648, 3.2381374835968018)


def iota(shape, dim):
    return lax.broadcasted_iota(jnp.int32, shape, dim)


def horner(coefficients, w):
    total = jnp.full_like(w, coefficients[-1])
    for c in coefficients[-2::-1]:
        total = total * w + c
    return total


def trig_turns(turns):
    r = turns - jnp.floor(turns + 0.5)
    w = r * r
    return horner(COS, w), r * horner(SIN, w)


def trig_wound(wound):
    r = (((wound + 32) & 63) - 32).astype(F32) * (1.0 / 64.0)
    w = r * r
    return horner(COS, w), r * horner(SIN, w)


def split(x):
    high = x.astype(BF16)
    return high, (x - high.astype(F32)).astype(BF16)


def dot(a, b, form="nn"):
    return lax.dot_general(
        a, b, (((1,), (0 if form == "nn" else 1,)), ((), ())), preferred_element_type=F32
    )


def dot3(a, b, form="nn"):
    return dot(a[0], b[0], form) + dot(a[1], b[0], form) + dot(a[0], b[1], form)


def swap_sign(x):
    lane = iota(x.shape, x.ndim - 1)
    return jnp.where(lane < 64, -1.0, 1.0) * pltpu.roll(x, 64, x.ndim - 1)


def row_to_col(row, n):
    shape = (n, row.shape[1])
    return jnp.sum(jnp.where(iota(shape, 0) == iota(shape, 1), row, 0.0), axis=1, keepdims=True)


def col_to_row(col, width):
    shape = (col.shape[0], width)
    return jnp.sum(jnp.where(iota(shape, 0) == iota(shape, 1), col, 0.0), axis=0, keepdims=True)


def signed(g):
    return jnp.where(g < 32, g, g - 64).astype(F32)


def atom_phases(index, positions):
    fx = signed(index >> 12)
    fy = signed((index >> 6) & 63)
    fz = signed(index & 63)
    tx, ty, tz = (row_to_col(positions[i : i + 1, :], NG) for i in range(3))
    turns = tx * fx + ty * fy + tz * fz
    cosine, sine = trig_turns(turns)
    return jnp.concatenate([cosine, sine], axis=0)


def depth_table():
    shape = (NG, PW)
    wound = iota(shape, 0) * ((iota(shape, 1) & 31) - 16)
    cosine, sine = trig_wound(wound)
    return jnp.concatenate([cosine, sine], axis=0)


def send_kernel(
    orb_hbm, resp_hbm, res_hbm, old_hbm, form_hbm, index_hbm, pos_hbm, out_ref,
    orb_ref, resp_ref, res_ref, old_ref, form_ref, index_ref, pos_ref, sems,
):
    arrays = (orb_ref, resp_ref, res_ref, old_ref)
    copies = fetch(
        (
            (index_hbm, index_ref), (pos_hbm, pos_ref), (orb_hbm, orb_ref), (resp_hbm, resp_ref),
            (res_hbm, res_ref), (old_hbm, old_ref), (form_hbm, form_ref),
        ),
        sems,
    )
    table = depth_table()
    for copy in copies[:2]:
        copy.wait()
    index = index_ref[...]
    phases = split(atom_phases(index, pos_ref[...]))
    for copy in copies[2:]:
        copy.wait()
    lines = jnp.concatenate(
        [ref[0, :, 2 * s + c, :] for c in range(2) for ref in arrays for s in range(2)], axis=0
    )
    lines = split(lines)
    group = iota(table.shape, 1) >> 5
    for b in range(COLS):
        z = dot3(split(jnp.where(group == b, table, 0.0)), lines, "nt")
        out_ref[pl.ds(b, DEV, stride=ROWS1), :] = z[:64] + swap_sign(z[64:])

    form_re, form_im = form_ref[0, 0], form_ref[0, 1]
    for n in range(NB):
        parts_re, parts_im = [], []
        for ref in arrays[2:]:
            for s in range(2):
                d_re = ref[0, n, 2 * s : 2 * s + 1, :]
                d_im = ref[0, n, 2 * s + 1 : 2 * s + 2, :]
                parts_re.append(form_re * d_re + form_im * d_im)
                parts_im.append(form_re * d_im - form_im * d_re)
        values = split(jnp.concatenate(parts_re + parts_im, axis=0))
        z = dot3(phases, values, "nt")
        out_ref[pl.ds(COLS + n, DEV, stride=ROWS1), :] = z[:64] + swap_sign(z[64:])

    squares = jnp.zeros((NB, PW), F32)
    for comp in range(4):
        r = res_ref[0, :, comp, :]
        squares = squares + r * r
    row = col_to_row(jnp.sum(squares, axis=1, keepdims=True), 128)
    codes = (index >> 6).astype(F32)
    lane = iota((1, PW), 1)
    target = iota((1, 128), 1)
    for b in range(COLS):
        code = jnp.sum(jnp.where(lane == STICK * b, codes, 0.0), axis=1, keepdims=True)
        row = jnp.where(target == COLS + b, code, row)
    out_ref[pl.ds(EXTRA, DEV, stride=ROWS1), :] = jnp.broadcast_to(row, (DEV, 128))


def own_columns(recv_ref):
    values = jnp.concatenate(
        [recv_ref[pl.ds(b, DEV, stride=ROWS1), :] for b in range(COLS)], axis=0
    )
    return values.T


def column_codes(extra):
    turned = extra.T
    codes = jnp.concatenate(
        [turned[COLS + b : COLS + b + 1, :] for b in range(COLS)], axis=1
    ).astype(jnp.int32)
    return codes


def x_tables(codes, cos_ref, sin_ref):
    shape = (HALF, ALL)
    cosine, sine = trig_wound(iota(shape, 0) * (codes >> 6))
    cos_ref[...] = cosine
    sin_ref[...] = sine


def y_tables(extra, high_ref, low_ref):
    shape = (DEV, 128)
    lane = iota(shape, 1)
    for b in range(COLS):
        code = extra[:, COLS + b : COLS + b + 1].astype(jnp.int32)
        wound = (code & 63) * (lane & 63)
        cosine, sine = trig_wound(wound)
        odd = jnp.broadcast_to(((code >> 6) & 1) == 1, shape)
        first = jnp.where(lane < 64, cosine, sine)
        second = jnp.where(lane < 64, -sine, cosine)
        for c, part in ((0, first), (1, second)):
            rows = slice(c * ALL + b * DEV, c * ALL + (b + 1) * DEV)
            for parity, mine in ((0, jnp.where(odd, 0.0, part)), (1, jnp.where(odd, part, 0.0))):
                high, low = split(mine)
                high_ref[rows, parity * 128 : (parity + 1) * 128] = high
                low_ref[rows, parity * 128 : (parity + 1) * 128] = low


def plane_chunk(re, im, first, count, cos_ref, sin_ref, tables, scratch):
    rows = re.shape[0]
    high_ref, low_ref = scratch
    for i in range(count):
        cx = cos_ref[pl.ds(first + i, 1), :]
        sx = sin_ref[pl.ds(first + i, 1), :]
        for c, part in ((0, re * cx - im * sx), (1, re * sx + im * cx)):
            high, low = split(part)
            high_ref[i * rows : (i + 1) * rows, c * ALL : (c + 1) * ALL] = high
            low_ref[i * rows : (i + 1) * rows, c * ALL : (c + 1) * ALL] = low
    high = high_ref[...]
    table = tables[0][...]
    both = dot(high, table) + dot(low_ref[...], table) + dot(high, tables[1][...])
    return both[:, :128] + both[:, 128:], both[:, :128] - both[:, 128:]


def fetch(pairs, sems):
    copies = [
        pltpu.make_async_copy(source, target, sems.at[i])
        for i, (source, target) in enumerate(pairs)
    ]
    for copy in copies:
        copy.start()
    return copies


def potential_kernel(
    recv_ref, atom_ref, slots_ref, pot_ref, old_norm_hbm, res_hbm, old_hbm, kin_hbm,
    energy_hbm, coup_hbm,
    out_ref, grid_ref, scalars_ref,
    old_norm_ref, res_ref, old_ref, kin_ref, energy_ref, coup_ref, sems,
    cos_ref, sin_ref, table_high, table_low, high_ref, low_ref, prod_ref, pair_ref,
):
    copies = fetch(
        (
            (old_norm_hbm, old_norm_ref), (res_hbm, res_ref), (old_hbm, old_ref),
            (kin_hbm, kin_ref), (energy_hbm, energy_ref), (coup_hbm, coup_ref),
        ),
        sems,
    )
    extra = recv_ref[pl.ds(EXTRA, DEV, stride=ROWS1), :]
    codes = column_codes(extra)
    x_tables(codes, cos_ref, sin_ref)
    y_tables(extra, table_high, table_low)
    tables = (table_high, table_low)
    for copy in copies:
        copy.wait()
    norm = row_to_col(jnp.sum(extra, axis=0, keepdims=True), NB)
    beta = norm / row_to_col(old_norm_ref[...], NB)
    values = own_columns(recv_ref)
    beta2 = jnp.concatenate([beta, beta], axis=0)
    re = values[32:48] + beta2 * values[48:64]
    im = values[96:112] + beta2 * values[112:128]

    acc_re = jnp.zeros((16, ALL), F32)
    acc_im = jnp.zeros((16, ALL), F32)
    local = jnp.zeros((NB, 128), F32)
    chunks = []
    for k in range(CH):
        chunks.append(plane_chunk(
            re, im, k * CX, CX, cos_ref, sin_ref, tables, (high_ref.at[k], low_ref.at[k])
        ))
    turns = []
    for k in range(CH):
        first = k * CX
        grids = chunks[k]
        for i in range(CX):
            products = []
            for half in range(2):
                grid = grids[half]
                x = first + i + 32 * half
                up = grid[i * 16 : i * 16 + 8]
                down = grid[i * 16 + 8 : i * 16 + 16]
                grid_ref[x * 16 : x * 16 + 8, :] = up
                grid_ref[x * 16 + 8 : x * 16 + 16, :] = down
                v0, bx, by, bz = (pot_ref[m, x : x + 1, :] for m in range(4))
                new_up = (v0 + bz) * up + bx * down - by * swap_sign(down)
                new_down = bx * up + by * swap_sign(up) + (v0 - bz) * down
                local = local + up * new_up + down * new_down
                products.append((new_up, new_down))
            for j in range(2):
                rows = slice(i * 16 + 8 * j, i * 16 + 8 * j + 8)
                prod_ref[k, rows, 0:128] = products[0][j] + products[1][j]
                prod_ref[k, rows, 128:256] = products[0][j] - products[1][j]
        turns.append(dot3(split(prod_ref[k]), (table_high[...], table_low[...]), "nt"))
    for k in range(CH):
        for i in range(CX):
            x = k * CX + i
            cx = cos_ref[x : x + 1, :]
            sx = sin_ref[x : x + 1, :]
            q_re = turns[k][i * 16 : (i + 1) * 16, :ALL]
            q_im = turns[k][i * 16 : (i + 1) * 16, ALL:]
            acc_re = acc_re + q_re * cx + q_im * sx
            acc_im = acc_im + q_im * cx - q_re * sx
    acc_re = acc_re * VOLUME
    acc_im = acc_im * VOLUME
    for r in range(2):
        pieces = []
        for b in range(4 * r, 4 * r + 4):
            lanes = slice(b * DEV, (b + 1) * DEV)
            pieces += [acc_re[:, lanes], acc_im[:, lanes]]
        out_ref[pl.ds(r, DEV, stride=ROWS2), :] = jnp.concatenate(pieces, axis=0).T

    sums = [
        jnp.sum(recv_ref[pl.ds(COLS + n, DEV, stride=ROWS1), :], axis=0, keepdims=True)
        for n in range(NB)
    ]
    amps = jnp.concatenate(sums, axis=0)
    amps = amps + beta * pltpu.roll(amps, 96, 1)
    amp_re, amp_im = amps[:, 0:32], amps[:, 64:96]
    count = jnp.sum(
        jnp.where(slots_ref[...] == atom_ref[0], 1.0, 0.0), axis=1, keepdims=True
    )
    shape = (PA, 32)
    count = jnp.sum(
        jnp.where((iota(shape, 1) & 15) == iota(shape, 0), count, 0.0), axis=0, keepdims=True
    )
    h_re = 0.5 * (coup_ref[0] + coup_ref[0].T)
    h_im = 0.5 * (coup_ref[1] - coup_ref[1].T)
    by_re, by_im = amp_re * count, amp_im * count

    def exact(a, b):
        return lax.dot_general(
            a, b, (((1,), (0,)), ((), ())),
            precision=lax.Precision.HIGHEST, preferred_element_type=F32,
        )

    q_re = (exact(by_re, h_re) + exact(by_im, h_im)) * count
    q_im = (exact(by_im, h_re) - exact(by_re, h_im)) * count
    pair_ref[:, 0:32] = q_re
    pair_ref[:, 32:64] = q_im
    pair_ref[:, 64:128] = jnp.zeros((NB, 64), F32)
    first_half = pair_ref[pl.ds(0, 4, stride=2), :]
    second_half = pair_ref[pl.ds(1, 4, stride=2), :]
    packed = first_half + pltpu.roll(second_half, 64, 1)
    odd = (iota((DEV, 128), 0) & 1) == 1
    for k in range(2):
        out_ref[pl.ds(2 + k, DEV, stride=ROWS2), :] = jnp.where(
            odd, packed[2 + k : 3 + k], packed[k : k + 1]
        )

    curvature = jnp.sum(local, axis=1, keepdims=True) * VOLUME
    curvature = curvature + jnp.sum(amp_re * q_re + amp_im * q_im, axis=1, keepdims=True)
    weight = kin_ref[...] - row_to_col(energy_ref[...], NB)
    own = jnp.zeros((NB, PW), F32)
    for comp in range(4):
        d = res_ref[0, :, comp, :] + beta * old_ref[0, :, comp, :]
        own = own + d * d
    curvature = curvature + jnp.sum(own * weight, axis=1, keepdims=True)
    out_ref[pl.ds(4, DEV, stride=ROWS2), :] = jnp.broadcast_to(
        col_to_row(curvature, 128), (DEV, 128)
    )
    lane = iota((NB, 128), 1)
    scalars_ref[...] = jnp.where(lane == 0, norm, jnp.where(lane == 1, beta, 0.0))


def orbital_kernel(
    recv_ref, grid_ref, base_ref, slope_ref, cos_ref, sin_ref, table_high, table_low, high_ref,
    low_ref,
):
    extra = recv_ref[pl.ds(EXTRA, DEV, stride=ROWS1), :]
    x_tables(column_codes(extra), cos_ref, sin_ref)
    y_tables(extra, table_high, table_low)
    values = own_columns(recv_ref)
    re, im = values[0:32], values[64:96]
    lane = iota((NB, 128), 1)

    def terms(o_up, o_down, c_up, c_down):
        same_up = o_up * c_up
        same_down = o_down * c_down
        return (
            same_up + same_down,
            o_up * c_down + o_down * c_up,
            o_down * swap_sign(c_up) - o_up * swap_sign(c_down),
            same_up - same_down,
        )

    def fold(even, odd):
        return 2.0 * (
            jnp.where(lane < 64, even, odd)
            + pltpu.roll(jnp.where(lane < 64, odd, even), 64, 1)
        )

    def chunk(k, carry):
        grids = plane_chunk(
            re, im, k * 8, 8, cos_ref, sin_ref, (table_high, table_low), (high_ref, low_ref)
        )
        for half in range(2):
            for j in range(4):
                with_response, with_direction = [], []
                for i in (2 * j, 2 * j + 1):
                    o_up, o_down, r_up, r_down = (
                        grids[half][i * 32 + 8 * q : i * 32 + 8 * q + 8] for q in range(4)
                    )
                    place = pl.multiple_of((k * 8 + i + 32 * half) * 16, 16)
                    d_up = grid_ref[pl.ds(place, 8), :]
                    d_down = grid_ref[pl.ds(place + 8, 8), :]
                    with_response.append(terms(o_up, o_down, r_up, r_down))
                    with_direction.append(terms(o_up, o_down, d_up, d_down))
                for m in range(4):
                    row = m * 32 + 16 * half + j + 4 * k
                    base_ref[pl.ds(row, 1), :] = jnp.sum(
                        fold(with_response[0][m], with_response[1][m]), axis=0, keepdims=True
                    )
                    slope_ref[pl.ds(row, NB, stride=128), :] = fold(
                        with_direction[0][m], with_direction[1][m]
                    )
        return carry

    lax.fori_loop(0, 4, chunk, 0)


def step_of(recv_ref, scalars_ref):
    total = jnp.sum(recv_ref[pl.ds(4, DEV, stride=ROWS2), :], axis=0, keepdims=True)
    return scalars_ref[:, 0:1] / (row_to_col(total, NB) + SMALL_TERM)


def density_kernel(recv_ref, scalars_ref, base_ref, slope_ref, out_ref, half_ref):
    step = step_of(recv_ref, scalars_ref)
    total = base_ref[...]
    for n in range(NB):
        total = total + step[n : n + 1, :] * slope_ref[n * 128 : (n + 1) * 128, :]
    for copy in range(8):
        out_ref[copy * 128 : (copy + 1) * 128, :] = total
    for k in range(2):
        half_ref[k * DEV : (k + 1) * DEV, :] = recv_ref[pl.ds(2 + k, DEV, stride=ROWS2), :]


def finish_kernel(
    parity_ref, half_ref, other_ref, recv_ref, scalars_ref, resp_ref, res_ref, old_ref, kin_ref, energy_ref, form_ref,
    index_ref, pos_ref, next_ref, residual_ref, direction_ref,
):
    step = step_of(recv_ref, scalars_ref)
    beta = scalars_ref[:, 1:2]
    table = depth_table()
    table = split(jnp.concatenate([table[:64], table[64:]], axis=1))
    group = iota((32, PW), 1) >> 5
    local = jnp.zeros((32, PW), F32)
    for r in range(2):
        values = recv_ref[pl.ds(r, DEV, stride=ROWS2), :].T
        z = dot3(split(values), table)
        for i in range(4):
            re_c, re_s = z[i * 32 : i * 32 + 16, :PW], z[i * 32 : i * 32 + 16, PW:]
            im_c, im_s = z[i * 32 + 16 : i * 32 + 32, :PW], z[i * 32 + 16 : i * 32 + 32, PW:]
            part = jnp.concatenate([re_c + im_s, im_c - re_s], axis=0)
            local = local + jnp.where(group == 4 * r + i, part, 0.0)

    phases = atom_phases(index_ref[...], pos_ref[...])
    phases = split(jnp.concatenate([phases[:64], phases[64:]], axis=1))
    form_re, form_im = form_ref[0, 0], form_ref[0, 1]
    rows_re, rows_im = [[], []], [[], []]
    for k in range(4):
        rows = slice((k & 1) * DEV, (k & 1) * DEV + DEV)
        mine = parity_ref[0] == (k >> 1)
        values = jnp.where(mine, half_ref[rows, :], other_ref[rows, :]).T
        z = dot3(split(values), phases)
        for i in range(2):
            for s in range(2):
                a = i * 64 + s * 16
                re_c, re_s = z[a : a + 16, :PW], z[a : a + 16, PW:]
                im_c, im_s = z[a + 32 : a + 48, :PW], z[a + 32 : a + 48, PW:]
                w_re = re_c + im_s
                w_im = im_c - re_s
                rows_re[s].append(
                    jnp.sum(form_re * w_re - form_im * w_im, axis=0, keepdims=True)
                )
                rows_im[s].append(
                    jnp.sum(form_re * w_im + form_im * w_re, axis=0, keepdims=True)
                )
    weight = kin_ref[...] - row_to_col(energy_ref[...], NB)
    for s in range(2):
        for c in range(2):
            comp = 2 * s + c
            nonlocal_term = jnp.concatenate((rows_re, rows_im)[c][s], axis=0)
            residual = res_ref[0, :, comp, :]
            direction = residual + beta * old_ref[0, :, comp, :]
            place = c * 16 + s * 8
            image = weight * direction + local[place : place + 8] + nonlocal_term
            direction_ref[0, :, comp, :] = direction
            next_ref[0, :, comp, :] = resp_ref[0, :, comp, :] + step * direction
            residual_ref[0, :, comp, :] = residual - step * image


def call(kernel, outs, name, scratch=(), flops=1, size=1, smem=(), hbm=()):
    def space(i):
        return pltpu.SMEM if i in smem else pltpu.HBM if i in hbm else pltpu.VMEM

    def run(*args):
        specs = [pl.BlockSpec(memory_space=space(i)) for i in range(len(args))]
        args = [
            pltpu.with_memory_space_constraint(a, pltpu.HBM) if i in hbm else a
            for i, a in enumerate(args)
        ]
        return pl.pallas_call(
            kernel,
            out_shape=outs,
            in_specs=specs,
            out_specs=jax.tree.map(lambda _: pl.BlockSpec(memory_space=pltpu.VMEM), outs),
            scratch_shapes=list(scratch),
            compiler_params=pltpu.CompilerParams(vmem_limit_bytes=LIMIT),
            cost_estimate=pl.CostEstimate(flops=flops, bytes_accessed=size, transcendentals=0),
            name=name,
        )(*args)

    return run


def shape_of(*dims):
    return jax.ShapeDtypeStruct(dims, F32)


def exchange(values, axis, parts):
    rows = values.shape[0] // parts
    if rows % 8:
        flat = values.reshape(parts, 1, rows * 128)
        flat = lax.all_to_all(flat, axis, 0, 0, tiled=True)
        return flat.reshape(values.shape)
    out = lax.all_to_all(values.reshape(parts, rows, 128), axis, 0, 0, tiled=True)
    return out.reshape(values.shape)


def per_device(
    orbitals, response, residual, old_direction, old_norm, band_energy, kinetic, form_factor,
    sphere_index, atom_positions, proj_atom, coupling, potential,
):
    scale = 1.0 / (8 * 16384)
    me = lax.axis_index("fft").reshape(1).astype(jnp.int32)
    slots = proj_atom.reshape(PA, NG)
    plane = potential.reshape(4, NG, NG)
    plane = jnp.concatenate([plane, plane], axis=2)

    parity = me & 1
    vector = pltpu.VMEM((1, NB, 4, PW), F32)
    sent = call(
        send_kernel, shape_of(DEV * ROWS1, 128), "lines_and_amplitudes",
        [vector] * 4 + [
            pltpu.VMEM((1, 2, PA, PW), F32), pltpu.VMEM((1, PW), jnp.int32),
            pltpu.VMEM((3, NG), F32), pltpu.SemaphoreType.DMA((7,)),
        ],
        hbm=range(7),
    )(orbitals, response, residual, old_direction, form_factor, sphere_index, atom_positions)
    recv = exchange(sent, "fft", DEV)
    tables = [
        pltpu.VMEM((HALF, ALL), F32), pltpu.VMEM((HALF, ALL), F32),
        pltpu.VMEM((2 * ALL, 256), BF16), pltpu.VMEM((2 * ALL, 256), BF16),
    ]
    back, grid, scalars = call(
        potential_kernel,
        (shape_of(DEV * ROWS2, 128), shape_of(NG * 16, 128), shape_of(NB, 128)),
        "potential_and_coupling",
        [
            pltpu.VMEM((1, NB), F32), vector, vector, pltpu.VMEM((1, PW), F32),
            pltpu.VMEM((1, NB), F32), pltpu.VMEM((2, 32, 32), F32),
            pltpu.SemaphoreType.DMA((6,)),
        ]
        + tables
        + [pltpu.VMEM((CH, 512 // CH, 2 * ALL), BF16), pltpu.VMEM((CH, 512 // CH, 2 * ALL), BF16)]
        + [pltpu.VMEM((CH, 512 // CH, 256), F32), pltpu.VMEM((NB, 128), F32)],
        smem=(1,), hbm=range(4, 10),
    )(recv, me, slots, plane, old_norm, residual, old_direction, kinetic, band_energy, coupling)
    returned = exchange(back, "fft", DEV)
    base, slope = call(
        orbital_kernel, (shape_of(128, 128), shape_of(NB * 128, 128)), "density_terms",
        tables + [pltpu.VMEM((256, 2 * ALL), BF16), pltpu.VMEM((256, 2 * ALL), BF16)],
        flops=3_000_000_000, size=3_000_000,
    )(recv, grid)
    density, half = call(
        density_kernel, (shape_of(8 * 128, 128), shape_of(2 * DEV, 128)), "density"
    )(returned, scalars, base, slope)
    gathered = exchange(density, "kpool", 8)
    other_half = lax.ppermute(half, "fft", MIRROR)
    outs = call(
        finish_kernel, (shape_of(1, NB, 4, PW),) * 3, "new_vectors",
        flops=3_000_000_000, size=3_000_000, smem=(0,),
    )(
        parity, half, other_half, returned, scalars, response, residual, old_direction, kinetic, band_energy, form_factor,
        sphere_index, atom_positions,
    )
    total = jnp.sum(gathered.reshape(8, 128, 128), axis=0) * scale
    return outs[0], outs[1], outs[2], total.reshape(4, 1, NG * NG)


def solution(mesh):
    vector = P("kpool", None, None, "fft")
    in_specs = (
        vector, vector, vector, vector, P("kpool", None), P("kpool", None), P("kpool", "fft"),
        vector, P("kpool", "fft"), P(), P(), P(), P(None, "fft", None),
    )
    out_specs = (vector, vector, vector, P(None, "fft", None))
    return jax.shard_map(
        per_device, mesh=mesh, in_specs=in_specs, out_specs=out_specs, check_vma=False
    )
```

```python
import math

import jax
import jax.numpy as jnp
from jax import lax
from jax.experimental import pallas as pl
from jax.experimental.pallas import tpu as pltpu
from jax.sharding import PartitionSpec as P

NG = 64
STICK = 32
NB = 8
COLS = 8
PW = COLS * STICK
PA = 16
DEV = 64
ZS = 16
YS = 4
EXTRA = 40
SAME_Z = [[z * YS + y for y in range(YS)] for z in range(ZS)]
SAME_Y = [[z * YS + y for z in range(ZS)] for y in range(YS)]
MIRROR = [(i, i ^ 1) for i in range(DEV)]
HALF = NG // 2
CH = 2
CX = HALF // CH
ALL = COLS * DEV
STAGE1 = 16 * ZS + 8
STAGE2 = 41
ROWS2 = 5
SMALL_TERM = 1e-06
VOLUME = 1.0 / (NG * NG * NG)
F32 = jnp.float32
BF16 = jnp.bfloat16
LIMIT = 48 * 1024 * 1024

COS = (1.0, -19.73920440673828, 64.93911743164062, -85.45014190673828,
       60.16762924194336, -25.967599868774414, 6.528658390045166)
SIN = (6.2831854820251465, -41.34170150756836, 81.60513305664062, -76.70301818847656,
       42.02592849731445, -14.899847030639648, 3.2381374835968018)


def iota(shape, dim):
    return lax.broadcasted_iota(jnp.int32, shape, dim)


def horner(coefficients, w):
    total = jnp.full_like(w, coefficients[-1])
    for c in coefficients[-2::-1]:
        total = total * w + c
    return total


def trig_turns(turns):
    r = turns - jnp.floor(turns + 0.5)
    w = r * r
    return horner(COS, w), r * horner(SIN, w)


def trig_wound(wound):
    r = (((wound + 32) & 63) - 32).astype(F32) * (1.0 / 64.0)
    w = r * r
    return horner(COS, w), r * horner(SIN, w)


def split(x):
    high = x.astype(BF16)
    return high, (x - high.astype(F32)).astype(BF16)


def dot(a, b, form="nn"):
    return lax.dot_general(
        a, b, (((1,), (0 if form == "nn" else 1,)), ((), ())), preferred_element_type=F32
    )


def dot3(a, b, form="nn"):
    return dot(a[0], b[0], form) + dot(a[1], b[0], form) + dot(a[0], b[1], form)


def swap_sign(x):
    lane = iota(x.shape, x.ndim - 1)
    return jnp.where(lane < 64, -1.0, 1.0) * pltpu.roll(x, 64, x.ndim - 1)


def row_to_col(row, n):
    shape = (n, row.shape[1])
    return jnp.sum(jnp.where(iota(shape, 0) == iota(shape, 1), row, 0.0), axis=1, keepdims=True)


def col_to_row(col, width):
    shape = (col.shape[0], width)
    return jnp.sum(jnp.where(iota(shape, 0) == iota(shape, 1), col, 0.0), axis=0, keepdims=True)


def signed(g):
    return jnp.where(g < 32, g, g - 64).astype(F32)


def device_order(i):
    return ((i & 15) << 2) | (i >> 4)


def atom_phases(index, positions, order=lambda i: i):
    fx = signed(index >> 12)
    fy = signed((index >> 6) & 63)
    fz = signed(index & 63)
    mine = iota((NG, NG), 1) == order(iota((NG, NG), 0))
    tx, ty, tz = (
        jnp.sum(jnp.where(mine, positions[i : i + 1, :], 0.0), axis=1, keepdims=True)
        for i in range(3)
    )
    turns = tx * fx + ty * fy + tz * fz
    cosine, sine = trig_turns(turns)
    return jnp.concatenate([cosine, sine], axis=0)


def depth_table(order=lambda i: i):
    shape = (NG, PW)
    wound = order(iota(shape, 0)) * ((iota(shape, 1) & 31) - 16)
    cosine, sine = trig_wound(wound)
    return jnp.concatenate([cosine, sine], axis=0)


def send_kernel(
    orb_hbm, resp_hbm, res_hbm, old_hbm, form_hbm, index_hbm, pos_hbm, out_ref,
    orb_ref, resp_ref, res_ref, old_ref, form_ref, index_ref, pos_ref, sems,
):
    def store(r, value):
        for y in range(YS):
            out_ref[pl.ds(y * STAGE1 + r, ZS, stride=16), :] = value[y * ZS : (y + 1) * ZS]

    arrays = (orb_ref, resp_ref, res_ref, old_ref)
    copies = fetch(
        (
            (index_hbm, index_ref), (pos_hbm, pos_ref), (orb_hbm, orb_ref), (resp_hbm, resp_ref),
            (res_hbm, res_ref), (old_hbm, old_ref), (form_hbm, form_ref),
        ),
        sems,
    )
    table = depth_table(device_order)
    for copy in copies[:2]:
        copy.wait()
    index = index_ref[...]
    phases = split(atom_phases(index, pos_ref[...], device_order))
    for copy in copies[2:]:
        copy.wait()
    lines = jnp.concatenate(
        [ref[0, :, 2 * s + c, :] for c in range(2) for ref in arrays for s in range(2)], axis=0
    )
    lines = split(lines)
    group = iota(table.shape, 1) >> 5
    for b in range(COLS):
        z = dot3(split(jnp.where(group == b, table, 0.0)), lines, "nt")
        store(b, z[:64] + swap_sign(z[64:]))

    form_re, form_im = form_ref[0, 0], form_ref[0, 1]
    for n in range(NB):
        parts_re, parts_im = [], []
        for ref in arrays[2:]:
            for s in range(2):
                d_re = ref[0, n, 2 * s : 2 * s + 1, :]
                d_im = ref[0, n, 2 * s + 1 : 2 * s + 2, :]
                parts_re.append(form_re * d_re + form_im * d_im)
                parts_im.append(form_re * d_im - form_im * d_re)
        values = split(jnp.concatenate(parts_re + parts_im, axis=0))
        z = dot3(phases, values, "nt")
        store(COLS + n, z[:64] + swap_sign(z[64:]))

    squares = jnp.zeros((NB, PW), F32)
    for comp in range(4):
        r = res_ref[0, :, comp, :]
        squares = squares + r * r
    row = col_to_row(jnp.sum(squares, axis=1, keepdims=True), 128)
    codes = (index >> 6).astype(F32)
    lane = iota((1, PW), 1)
    target = iota((1, 128), 1)
    for b in range(COLS):
        code = jnp.sum(jnp.where(lane == STICK * b, codes, 0.0), axis=1, keepdims=True)
        row = jnp.where(target == COLS + b, code, row)
    for y in range(YS):
        out_ref[(y + 1) * STAGE1 - 8 : (y + 1) * STAGE1, :] = jnp.broadcast_to(row, (8, 128))


def regroup_kernel(in_ref, out_ref):
    for y in range(YS):
        for b in range(COLS):
            out_ref[pl.ds(y * COLS + b, ZS, stride=STAGE2), :] = in_ref[
                pl.ds(y * STAGE1 + b, ZS, stride=16), :
            ]
    for n in range(NB):
        parts = [in_ref[pl.ds(y * STAGE1 + COLS + n, ZS, stride=16), :] for y in range(YS)]
        out_ref[pl.ds(YS * COLS + n, ZS, stride=STAGE2), :] = (
            (parts[0] + parts[1]) + (parts[2] + parts[3])
        )
    lane = iota((8, 128), 1)
    row = jnp.zeros((8, 128), F32)
    for y in range(YS):
        extra = in_ref[(y + 1) * STAGE1 - 8 : (y + 1) * STAGE1, :]
        row = row + jnp.where(lane < NB, extra, 0.0)
        first = NB + y * COLS
        moved = extra if y == 0 else pltpu.roll(extra, y * COLS, 1)
        row = row + jnp.where((lane >= first) & (lane < first + COLS), moved, 0.0)
    out_ref[pl.ds(EXTRA, ZS, stride=STAGE2), :] = jnp.concatenate([row, row], axis=0)


def own_columns(recv_ref):
    values = jnp.concatenate(
        [
            recv_ref[pl.ds(y * COLS + b, ZS, stride=STAGE2), :]
            for b in range(COLS)
            for y in range(YS)
        ],
        axis=0,
    )
    return values.T


def column_codes(extra):
    codes = extra.astype(jnp.int32)
    shape = (128, ALL)
    lane = iota(shape, 1)
    pick = jnp.where(iota(shape, 0) == NB + ((lane >> 4) & 3) * COLS + (lane >> 6), 1.0, 0.0)
    mine = (iota((ZS, ALL), 1) & 15) == iota((ZS, ALL), 0)
    used = iota((ZS, 128), 1) >= NB
    parts = []
    for value in (codes >> 6, codes & 63):
        value = jnp.where(used, value, 0).astype(F32).astype(BF16)
        spread = dot(value, pick.astype(BF16))
        parts.append(
            jnp.sum(jnp.where(mine, spread, 0.0), axis=0, keepdims=True).astype(jnp.int32)
        )
    return parts


def x_tables(codes, cos_ref, sin_ref):
    shape = (HALF, ALL)
    cosine, sine = trig_wound(iota(shape, 0) * codes[0])
    cos_ref[...] = cosine
    sin_ref[...] = sine


def y_tables(extra, high_ref, low_ref):
    shape = (DEV, 128)
    lane = iota(shape, 1)
    for b in range(COLS):
        lanes = [NB + y * COLS + b for y in range(YS)]
        code = jnp.concatenate([extra[:, i : i + 1] for i in lanes], axis=0).astype(jnp.int32)
        wound = (code & 63) * (lane & 63)
        cosine, sine = trig_wound(wound)
        odd = jnp.broadcast_to(((code >> 6) & 1) == 1, shape)
        first = jnp.where(lane < 64, cosine, sine)
        second = jnp.where(lane < 64, -sine, cosine)
        for c, part in ((0, first), (1, second)):
            rows = slice(c * ALL + b * DEV, c * ALL + (b + 1) * DEV)
            for parity, mine in ((0, jnp.where(odd, 0.0, part)), (1, jnp.where(odd, part, 0.0))):
                high, low = split(mine)
                high_ref[rows, parity * 128 : (parity + 1) * 128] = high
                low_ref[rows, parity * 128 : (parity + 1) * 128] = low


def plane_chunk(re, im, first, count, cos_ref, sin_ref, tables, scratch):
    rows = re.shape[0]
    high_ref, low_ref = scratch
    for i in range(count):
        cx = cos_ref[pl.ds(first + i, 1), :]
        sx = sin_ref[pl.ds(first + i, 1), :]
        for c, part in ((0, re * cx - im * sx), (1, re * sx + im * cx)):
            high, low = split(part)
            high_ref[i * rows : (i + 1) * rows, c * ALL : (c + 1) * ALL] = high
            low_ref[i * rows : (i + 1) * rows, c * ALL : (c + 1) * ALL] = low
    high = high_ref[...]
    table = tables[0][...]
    both = dot(high, table) + dot(low_ref[...], table) + dot(high, tables[1][...])
    return both[:, :128] + both[:, 128:], both[:, :128] - both[:, 128:]


def fetch(pairs, sems):
    copies = [
        pltpu.make_async_copy(source, target, sems.at[i])
        for i, (source, target) in enumerate(pairs)
    ]
    for copy in copies:
        copy.start()
    return copies


def potential_kernel(
    recv_ref, atom_ref, slots_ref, pot_ref, old_norm_hbm, res_hbm, old_hbm, kin_hbm,
    energy_hbm, coup_hbm,
    out_ref, grid_ref, scalars_ref,
    old_norm_ref, res_ref, old_ref, kin_ref, energy_ref, coup_ref, sems,
    cos_ref, sin_ref, table_high, table_low, high_ref, low_ref, prod_ref, pair_ref,
):
    copies = fetch(
        (
            (old_norm_hbm, old_norm_ref), (res_hbm, res_ref), (old_hbm, old_ref),
            (kin_hbm, kin_ref), (energy_hbm, energy_ref), (coup_hbm, coup_ref),
        ),
        sems,
    )
    def store(r, value):
        for y in range(YS):
            out_ref[pl.ds(y * ROWS2 + r, ZS, stride=YS * ROWS2), :] = value[
                y * ZS : (y + 1) * ZS
            ]

    extra = recv_ref[pl.ds(EXTRA, ZS, stride=STAGE2), :]
    codes = column_codes(extra)
    x_tables(codes, cos_ref, sin_ref)
    y_tables(extra, table_high, table_low)
    tables = (table_high, table_low)
    for copy in copies:
        copy.wait()
    norm = row_to_col(jnp.sum(extra, axis=0, keepdims=True), NB)
    beta = norm / row_to_col(old_norm_ref[...], NB)
    values = own_columns(recv_ref)
    beta2 = jnp.concatenate([beta, beta], axis=0)
    re = values[32:48] + beta2 * values[48:64]
    im = values[96:112] + beta2 * values[112:128]

    acc_re = jnp.zeros((16, ALL), F32)
    acc_im = jnp.zeros((16, ALL), F32)
    local = jnp.zeros((NB, 128), F32)
    chunks = []
    for k in range(CH):
        chunks.append(plane_chunk(
            re, im, k * CX, CX, cos_ref, sin_ref, tables, (high_ref.at[k], low_ref.at[k])
        ))
    turns = []
    for k in range(CH):
        first = k * CX
        grids = chunks[k]
        for i in range(CX):
            products = []
            for half in range(2):
                grid = grids[half]
                x = first + i + 32 * half
                up = grid[i * 16 : i * 16 + 8]
                down = grid[i * 16 + 8 : i * 16 + 16]
                grid_ref[x * 16 : x * 16 + 8, :] = up
                grid_ref[x * 16 + 8 : x * 16 + 16, :] = down
                v0, bx, by, bz = (pot_ref[m, x : x + 1, :] for m in range(4))
                new_up = (v0 + bz) * up + bx * down - by * swap_sign(down)
                new_down = bx * up + by * swap_sign(up) + (v0 - bz) * down
                local = local + up * new_up + down * new_down
                products.append((new_up, new_down))
            for j in range(2):
                rows = slice(i * 16 + 8 * j, i * 16 + 8 * j + 8)
                prod_ref[k, rows, 0:128] = products[0][j] + products[1][j]
                prod_ref[k, rows, 128:256] = products[0][j] - products[1][j]
        turns.append(dot3(split(prod_ref[k]), (table_high[...], table_low[...]), "nt"))
    for k in range(CH):
        for i in range(CX):
            x = k * CX + i
            cx = cos_ref[x : x + 1, :]
            sx = sin_ref[x : x + 1, :]
            q_re = turns[k][i * 16 : (i + 1) * 16, :ALL]
            q_im = turns[k][i * 16 : (i + 1) * 16, ALL:]
            acc_re = acc_re + q_re * cx + q_im * sx
            acc_im = acc_im + q_im * cx - q_re * sx
    acc_re = acc_re * VOLUME
    acc_im = acc_im * VOLUME
    for r in range(2):
        pieces = []
        for b in range(4 * r, 4 * r + 4):
            lanes = slice(b * DEV, (b + 1) * DEV)
            pieces += [acc_re[:, lanes], acc_im[:, lanes]]
        store(r, jnp.concatenate(pieces, axis=0).T)

    sums = [
        jnp.sum(recv_ref[pl.ds(YS * COLS + n, ZS, stride=STAGE2), :], axis=0, keepdims=True)
        for n in range(NB)
    ]
    amps = jnp.concatenate(sums, axis=0)
    amps = amps + beta * pltpu.roll(amps, 96, 1)
    amp_re, amp_im = amps[:, 0:32], amps[:, 64:96]
    count = jnp.sum(
        jnp.where(slots_ref[...] == atom_ref[0], 1.0, 0.0), axis=1, keepdims=True
    )
    shape = (PA, 32)
    count = jnp.sum(
        jnp.where((iota(shape, 1) & 15) == iota(shape, 0), count, 0.0), axis=0, keepdims=True
    )
    h_re = 0.5 * (coup_ref[0] + coup_ref[0].T)
    h_im = 0.5 * (coup_ref[1] - coup_ref[1].T)
    by_re, by_im = amp_re * count, amp_im * count

    def exact(a, b):
        return lax.dot_general(
            a, b, (((1,), (0,)), ((), ())),
            precision=lax.Precision.HIGHEST, preferred_element_type=F32,
        )

    q_re = (exact(by_re, h_re) + exact(by_im, h_im)) * count
    q_im = (exact(by_im, h_re) - exact(by_re, h_im)) * count
    pair_ref[:, 0:32] = q_re
    pair_ref[:, 32:64] = q_im
    pair_ref[:, 64:128] = jnp.zeros((NB, 64), F32)
    first_half = pair_ref[pl.ds(0, 4, stride=2), :]
    second_half = pair_ref[pl.ds(1, 4, stride=2), :]
    packed = first_half + pltpu.roll(second_half, 64, 1)
    odd = ((iota((DEV, 128), 0) >> 4) & 1) == 1
    for k in range(2):
        store(2 + k, jnp.where(odd, packed[2 + k : 3 + k], packed[k : k + 1]))

    curvature = jnp.sum(local, axis=1, keepdims=True) * VOLUME
    curvature = curvature + jnp.sum(amp_re * q_re + amp_im * q_im, axis=1, keepdims=True)
    weight = kin_ref[...] - row_to_col(energy_ref[...], NB)
    own = jnp.zeros((NB, PW), F32)
    for comp in range(4):
        d = res_ref[0, :, comp, :] + beta * old_ref[0, :, comp, :]
        own = own + d * d
    curvature = curvature + jnp.sum(own * weight, axis=1, keepdims=True)
    store(4, jnp.broadcast_to(col_to_row(curvature, 128), (DEV, 128)))
    lane = iota((NB, 128), 1)
    scalars_ref[...] = jnp.where(lane == 0, norm, jnp.where(lane == 1, beta, 0.0))


def orbital_kernel(
    recv_ref, grid_ref, base_ref, slope_ref, cos_ref, sin_ref, table_high, table_low, high_ref,
    low_ref,
):
    extra = recv_ref[pl.ds(EXTRA, ZS, stride=STAGE2), :]
    x_tables(column_codes(extra), cos_ref, sin_ref)
    y_tables(extra, table_high, table_low)
    values = own_columns(recv_ref)
    re, im = values[0:32], values[64:96]
    lane = iota((NB, 128), 1)

    def terms(o_up, o_down, c_up, c_down):
        same_up = o_up * c_up
        same_down = o_down * c_down
        return (
            same_up + same_down,
            o_up * c_down + o_down * c_up,
            o_down * swap_sign(c_up) - o_up * swap_sign(c_down),
            same_up - same_down,
        )

    def fold(even, odd):
        return 2.0 * (
            jnp.where(lane < 64, even, odd)
            + pltpu.roll(jnp.where(lane < 64, odd, even), 64, 1)
        )

    def chunk(k, carry):
        grids = plane_chunk(
            re, im, k * 8, 8, cos_ref, sin_ref, (table_high, table_low), (high_ref, low_ref)
        )
        for half in range(2):
            for j in range(4):
                with_response, with_direction = [], []
                for i in (2 * j, 2 * j + 1):
                    o_up, o_down, r_up, r_down = (
                        grids[half][i * 32 + 8 * q : i * 32 + 8 * q + 8] for q in range(4)
                    )
                    place = pl.multiple_of((k * 8 + i + 32 * half) * 16, 16)
                    d_up = grid_ref[pl.ds(place, 8), :]
                    d_down = grid_ref[pl.ds(place + 8, 8), :]
                    with_response.append(terms(o_up, o_down, r_up, r_down))
                    with_direction.append(terms(o_up, o_down, d_up, d_down))
                for m in range(4):
                    row = m * 32 + 16 * half + j + 4 * k
                    base_ref[pl.ds(row, 1), :] = jnp.sum(
                        fold(with_response[0][m], with_response[1][m]), axis=0, keepdims=True
                    )
                    slope_ref[pl.ds(row, NB, stride=128), :] = fold(
                        with_direction[0][m], with_direction[1][m]
                    )
        return carry

    lax.fori_loop(0, 4, chunk, 0)


def step_of(recv_ref, scalars_ref):
    total = jnp.sum(recv_ref[pl.ds(4, DEV, stride=ROWS2), :], axis=0, keepdims=True)
    return scalars_ref[:, 0:1] / (row_to_col(total, NB) + SMALL_TERM)


def density_kernel(recv_ref, scalars_ref, base_ref, slope_ref, out_ref, half_ref):
    step = step_of(recv_ref, scalars_ref)
    total = base_ref[...]
    for n in range(NB):
        total = total + step[n : n + 1, :] * slope_ref[n * 128 : (n + 1) * 128, :]
    for copy in range(8):
        out_ref[copy * 128 : (copy + 1) * 128, :] = total
    for k in range(2):
        half_ref[k * DEV : (k + 1) * DEV, :] = recv_ref[pl.ds(2 + k, DEV, stride=ROWS2), :]


def finish_kernel(
    parity_ref, half_ref, other_ref, recv_ref, scalars_ref, resp_ref, res_ref, old_ref, kin_ref, energy_ref, form_ref,
    index_ref, pos_ref, next_ref, residual_ref, direction_ref,
):
    step = step_of(recv_ref, scalars_ref)
    beta = scalars_ref[:, 1:2]
    table = depth_table()
    table = split(jnp.concatenate([table[:64], table[64:]], axis=1))
    group = iota((32, PW), 1) >> 5
    local = jnp.zeros((32, PW), F32)
    for r in range(2):
        values = recv_ref[pl.ds(r, DEV, stride=ROWS2), :].T
        z = dot3(split(values), table)
        for i in range(4):
            re_c, re_s = z[i * 32 : i * 32 + 16, :PW], z[i * 32 : i * 32 + 16, PW:]
            im_c, im_s = z[i * 32 + 16 : i * 32 + 32, :PW], z[i * 32 + 16 : i * 32 + 32, PW:]
            part = jnp.concatenate([re_c + im_s, im_c - re_s], axis=0)
            local = local + jnp.where(group == 4 * r + i, part, 0.0)

    phases = atom_phases(index_ref[...], pos_ref[...])
    phases = split(jnp.concatenate([phases[:64], phases[64:]], axis=1))
    form_re, form_im = form_ref[0, 0], form_ref[0, 1]
    rows_re, rows_im = [[], []], [[], []]
    for k in range(4):
        rows = slice((k & 1) * DEV, (k & 1) * DEV + DEV)
        mine = parity_ref[0] == (k >> 1)
        values = jnp.where(mine, half_ref[rows, :], other_ref[rows, :]).T
        z = dot3(split(values), phases)
        for i in range(2):
            for s in range(2):
                a = i * 64 + s * 16
                re_c, re_s = z[a : a + 16, :PW], z[a : a + 16, PW:]
                im_c, im_s = z[a + 32 : a + 48, :PW], z[a + 32 : a + 48, PW:]
                w_re = re_c + im_s
                w_im = im_c - re_s
                rows_re[s].append(
                    jnp.sum(form_re * w_re - form_im * w_im, axis=0, keepdims=True)
                )
                rows_im[s].append(
                    jnp.sum(form_re * w_im + form_im * w_re, axis=0, keepdims=True)
                )
    weight = kin_ref[...] - row_to_col(energy_ref[...], NB)
    for s in range(2):
        for c in range(2):
            comp = 2 * s + c
            nonlocal_term = jnp.concatenate((rows_re, rows_im)[c][s], axis=0)
            residual = res_ref[0, :, comp, :]
            direction = residual + beta * old_ref[0, :, comp, :]
            place = c * 16 + s * 8
            image = weight * direction + local[place : place + 8] + nonlocal_term
            direction_ref[0, :, comp, :] = direction
            next_ref[0, :, comp, :] = resp_ref[0, :, comp, :] + step * direction
            residual_ref[0, :, comp, :] = residual - step * image


def call(kernel, outs, name, scratch=(), flops=1, size=1, smem=(), hbm=()):
    def space(i):
        return pltpu.SMEM if i in smem else pltpu.HBM if i in hbm else pltpu.VMEM

    def run(*args):
        specs = [pl.BlockSpec(memory_space=space(i)) for i in range(len(args))]
        args = [
            pltpu.with_memory_space_constraint(a, pltpu.HBM) if i in hbm else a
            for i, a in enumerate(args)
        ]
        return pl.pallas_call(
            kernel,
            out_shape=outs,
            in_specs=specs,
            out_specs=jax.tree.map(lambda _: pl.BlockSpec(memory_space=pltpu.VMEM), outs),
            scratch_shapes=list(scratch),
            compiler_params=pltpu.CompilerParams(vmem_limit_bytes=LIMIT),
            cost_estimate=pl.CostEstimate(flops=flops, bytes_accessed=size, transcendentals=0),
            name=name,
        )(*args)

    return run


def shape_of(*dims):
    return jax.ShapeDtypeStruct(dims, F32)


def exchange(values, axis, parts, groups=None):
    rows = values.shape[0] // parts
    if rows % 8:
        flat = values.reshape(parts, 1, rows * 128)
        flat = lax.all_to_all(flat, axis, 0, 0, tiled=True, axis_index_groups=groups)
        return flat.reshape(values.shape)
    out = lax.all_to_all(
        values.reshape(parts, rows, 128), axis, 0, 0, tiled=True, axis_index_groups=groups
    )
    return out.reshape(values.shape)


def per_device(
    orbitals, response, residual, old_direction, old_norm, band_energy, kinetic, form_factor,
    sphere_index, atom_positions, proj_atom, coupling, potential,
):
    scale = 1.0 / (8 * 16384)
    me = lax.axis_index("fft").reshape(1).astype(jnp.int32)
    slots = proj_atom.reshape(PA, NG)
    plane = potential.reshape(4, NG, NG)
    plane = jnp.concatenate([plane, plane], axis=2)

    parity = me & 1
    vector = pltpu.VMEM((1, NB, 4, PW), F32)
    sent = call(
        send_kernel, shape_of(YS * STAGE1, 128), "lines_and_amplitudes",
        [vector] * 4 + [
            pltpu.VMEM((1, 2, PA, PW), F32), pltpu.VMEM((1, PW), jnp.int32),
            pltpu.VMEM((3, NG), F32), pltpu.SemaphoreType.DMA((7,)),
        ],
        hbm=range(7),
    )(orbitals, response, residual, old_direction, form_factor, sphere_index, atom_positions)
    near = exchange(sent, "fft", YS, SAME_Z)
    joined = call(regroup_kernel, shape_of(ZS * STAGE2, 128), "regroup")(near)
    recv = exchange(joined, "fft", ZS, SAME_Y)
    tables = [
        pltpu.VMEM((HALF, ALL), F32), pltpu.VMEM((HALF, ALL), F32),
        pltpu.VMEM((2 * ALL, 256), BF16), pltpu.VMEM((2 * ALL, 256), BF16),
    ]
    back, grid, scalars = call(
        potential_kernel,
        (shape_of(DEV * ROWS2, 128), shape_of(NG * 16, 128), shape_of(NB, 128)),
        "potential_and_coupling",
        [
            pltpu.VMEM((1, NB), F32), vector, vector, pltpu.VMEM((1, PW), F32),
            pltpu.VMEM((1, NB), F32), pltpu.VMEM((2, 32, 32), F32),
            pltpu.SemaphoreType.DMA((6,)),
        ]
        + tables
        + [pltpu.VMEM((CH, 512 // CH, 2 * ALL), BF16), pltpu.VMEM((CH, 512 // CH, 2 * ALL), BF16)]
        + [pltpu.VMEM((CH, 512 // CH, 256), F32), pltpu.VMEM((NB, 128), F32)],
        smem=(1,), hbm=range(4, 10),
    )(recv, me, slots, plane, old_norm, residual, old_direction, kinetic, band_energy, coupling)
    returned = exchange(back, "fft", DEV)
    base, slope = call(
        orbital_kernel, (shape_of(128, 128), shape_of(NB * 128, 128)), "density_terms",
        tables + [pltpu.VMEM((256, 2 * ALL), BF16), pltpu.VMEM((256, 2 * ALL), BF16)],
        flops=3_000_000_000, size=3_000_000,
    )(recv, grid)
    density, half = call(
        density_kernel, (shape_of(8 * 128, 128), shape_of(2 * DEV, 128)), "density"
    )(returned, scalars, base, slope)
    gathered = exchange(density, "kpool", 8)
    other_half = lax.ppermute(half, "fft", MIRROR)
    outs = call(
        finish_kernel, (shape_of(1, NB, 4, PW),) * 3, "new_vectors",
        flops=3_000_000_000, size=3_000_000, smem=(0,),
    )(
        parity, half, other_half, returned, scalars, response, residual, old_direction, kinetic, band_energy, form_factor,
        sphere_index, atom_positions,
    )
    total = jnp.sum(gathered.reshape(8, 128, 128), axis=0) * scale
    return outs[0], outs[1], outs[2], total.reshape(4, 1, NG * NG)


def solution(mesh):
    vector = P("kpool", None, None, "fft")
    in_specs = (
        vector, vector, vector, vector, P("kpool", None), P("kpool", None), P("kpool", "fft"),
        vector, P("kpool", "fft"), P(), P(), P(), P(None, "fft", None),
    )
    out_specs = (vector, vector, vector, P(None, "fft", None))
    return jax.shard_map(
        per_device, mesh=mesh, in_specs=in_specs, out_specs=out_specs, check_vma=False
    )
```

```python
import math

import jax
import jax.numpy as jnp
from jax import lax
from jax.experimental import pallas as pl
from jax.experimental.pallas import tpu as pltpu
from jax.sharding import PartitionSpec as P

NG = 64
STICK = 32
NB = 8
COLS = 8
PW = COLS * STICK
PA = 16
DEV = 64
ZS = 16
YS = 4
EXTRA = 40
SAME_Z = [[z * YS + y for y in range(YS)] for z in range(ZS)]
SAME_Y = [[z * YS + y for z in range(ZS)] for y in range(YS)]
MIRROR = [(i, i ^ 1) for i in range(DEV)]
HALF = NG // 2
CH = 2
CX = HALF // CH
ALL = COLS * DEV
STAGE1 = 16 * ZS + 8
STAGE2 = 41
ROWS2 = 5
SMALL_TERM = 1e-06
VOLUME = 1.0 / (NG * NG * NG)
F32 = jnp.float32
BF16 = jnp.bfloat16
LIMIT = 48 * 1024 * 1024

COS = (1.0, -19.73920440673828, 64.93911743164062, -85.45014190673828,
       60.16762924194336, -25.967599868774414, 6.528658390045166)
SIN = (6.2831854820251465, -41.34170150756836, 81.60513305664062, -76.70301818847656,
       42.02592849731445, -14.899847030639648, 3.2381374835968018)


def iota(shape, dim):
    return lax.broadcasted_iota(jnp.int32, shape, dim)


def horner(coefficients, w):
    total = jnp.full_like(w, coefficients[-1])
    for c in coefficients[-2::-1]:
        total = total * w + c
    return total


def trig_turns(turns):
    r = turns - jnp.floor(turns + 0.5)
    w = r * r
    return horner(COS, w), r * horner(SIN, w)


def trig_wound(wound):
    r = (((wound + 32) & 63) - 32).astype(F32) * (1.0 / 64.0)
    w = r * r
    return horner(COS, w), r * horner(SIN, w)


def split(x):
    high = x.astype(BF16)
    return high, (x - high.astype(F32)).astype(BF16)


def dot(a, b, form="nn"):
    return lax.dot_general(
        a, b, (((1,), (0 if form == "nn" else 1,)), ((), ())), preferred_element_type=F32
    )


def dot3(a, b, form="nn"):
    return dot(a[0], b[0], form) + dot(a[1], b[0], form) + dot(a[0], b[1], form)


def swap_sign(x):
    lane = iota(x.shape, x.ndim - 1)
    return jnp.where(lane < 64, -1.0, 1.0) * pltpu.roll(x, 64, x.ndim - 1)


def row_to_col(row, n):
    shape = (n, row.shape[1])
    return jnp.sum(jnp.where(iota(shape, 0) == iota(shape, 1), row, 0.0), axis=1, keepdims=True)


def col_to_row(col, width):
    shape = (col.shape[0], width)
    return jnp.sum(jnp.where(iota(shape, 0) == iota(shape, 1), col, 0.0), axis=0, keepdims=True)


def signed(g):
    return jnp.where(g < 32, g, g - 64).astype(F32)


def device_order(i):
    return ((i & 15) << 2) | (i >> 4)


def atom_phases(index, positions, order=lambda i: i):
    fx = signed(index >> 12)
    fy = signed((index >> 6) & 63)
    fz = signed(index & 63)
    mine = iota((NG, NG), 1) == order(iota((NG, NG), 0))
    tx, ty, tz = (
        jnp.sum(jnp.where(mine, positions[i : i + 1, :], 0.0), axis=1, keepdims=True)
        for i in range(3)
    )
    turns = tx * fx + ty * fy + tz * fz
    cosine, sine = trig_turns(turns)
    return jnp.concatenate([cosine, sine], axis=0)


def depth_table(order=lambda i: i):
    shape = (NG, PW)
    wound = order(iota(shape, 0)) * ((iota(shape, 1) & 31) - 16)
    cosine, sine = trig_wound(wound)
    return jnp.concatenate([cosine, sine], axis=0)


def send_kernel(
    orb_hbm, resp_hbm, res_hbm, old_hbm, form_hbm, index_hbm, pos_hbm, out_ref,
    orb_ref, resp_ref, res_ref, old_ref, form_ref, index_ref, pos_ref, sems,
):
    def store(r, value):
        for y in range(YS):
            out_ref[pl.ds(y * STAGE1 + r, ZS, stride=16), :] = value[y * ZS : (y + 1) * ZS]

    arrays = (orb_ref, resp_ref, res_ref, old_ref)
    copies = fetch(
        (
            (index_hbm, index_ref), (pos_hbm, pos_ref), (orb_hbm, orb_ref), (resp_hbm, resp_ref),
            (res_hbm, res_ref), (old_hbm, old_ref), (form_hbm, form_ref),
        ),
        sems,
    )
    table = depth_table(device_order)
    for copy in copies[:2]:
        copy.wait()
    index = index_ref[...]
    phases = split(atom_phases(index, pos_ref[...], device_order))
    for copy in copies[2:]:
        copy.wait()
    lines = jnp.concatenate(
        [ref[0, :, 2 * s + c, :] for c in range(2) for ref in arrays for s in range(2)], axis=0
    )
    lines = split(lines)
    group = iota(table.shape, 1) >> 5
    for b in range(COLS):
        z = dot3(split(jnp.where(group == b, table, 0.0)), lines, "nt")
        store(b, z[:64] + swap_sign(z[64:]))

    form_re, form_im = form_ref[0, 0], form_ref[0, 1]
    for n in range(NB):
        parts_re, parts_im = [], []
        for ref in arrays[2:]:
            for s in range(2):
                d_re = ref[0, n, 2 * s : 2 * s + 1, :]
                d_im = ref[0, n, 2 * s + 1 : 2 * s + 2, :]
                parts_re.append(form_re * d_re + form_im * d_im)
                parts_im.append(form_re * d_im - form_im * d_re)
        values = split(jnp.concatenate(parts_re + parts_im, axis=0))
        z = dot3(phases, values, "nt")
        store(COLS + n, z[:64] + swap_sign(z[64:]))

    squares = jnp.zeros((NB, PW), F32)
    for comp in range(4):
        r = res_ref[0, :, comp, :]
        squares = squares + r * r
    row = col_to_row(jnp.sum(squares, axis=1, keepdims=True), 128)
    codes = (index >> 6).astype(F32)
    lane = iota((1, PW), 1)
    target = iota((1, 128), 1)
    for b in range(COLS):
        code = jnp.sum(jnp.where(lane == STICK * b, codes, 0.0), axis=1, keepdims=True)
        row = jnp.where(target == COLS + b, code, row)
    for y in range(YS):
        out_ref[(y + 1) * STAGE1 - 8 : (y + 1) * STAGE1, :] = jnp.broadcast_to(row, (8, 128))


def regroup_kernel(in_ref, out_ref):
    for y in range(YS):
        for b in range(COLS):
            out_ref[pl.ds(y * COLS + b, ZS, stride=STAGE2), :] = in_ref[
                pl.ds(y * STAGE1 + b, ZS, stride=16), :
            ]
    for n in range(NB):
        parts = [in_ref[pl.ds(y * STAGE1 + COLS + n, ZS, stride=16), :] for y in range(YS)]
        out_ref[pl.ds(YS * COLS + n, ZS, stride=STAGE2), :] = (
            (parts[0] + parts[1]) + (parts[2] + parts[3])
        )
    lane = iota((8, 128), 1)
    row = jnp.zeros((8, 128), F32)
    for y in range(YS):
        extra = in_ref[(y + 1) * STAGE1 - 8 : (y + 1) * STAGE1, :]
        row = row + jnp.where(lane < NB, extra, 0.0)
        first = NB + y * COLS
        moved = extra if y == 0 else pltpu.roll(extra, y * COLS, 1)
        row = row + jnp.where((lane >= first) & (lane < first + COLS), moved, 0.0)
    out_ref[pl.ds(EXTRA, ZS, stride=STAGE2), :] = jnp.concatenate([row, row], axis=0)


def own_columns(recv_ref):
    values = jnp.concatenate(
        [
            recv_ref[pl.ds(y * COLS + b, ZS, stride=STAGE2), :]
            for b in range(COLS)
            for y in range(YS)
        ],
        axis=0,
    )
    return values.T


def column_codes(extra):
    codes = extra.astype(jnp.int32)
    shape = (128, ALL)
    lane = iota(shape, 1)
    pick = jnp.where(iota(shape, 0) == NB + ((lane >> 4) & 3) * COLS + (lane >> 6), 1.0, 0.0)
    mine = (iota((ZS, ALL), 1) & 15) == iota((ZS, ALL), 0)
    used = iota((ZS, 128), 1) >= NB
    parts = []
    for value in (codes >> 6, codes & 63):
        value = jnp.where(used, value, 0).astype(F32).astype(BF16)
        spread = dot(value, pick.astype(BF16))
        parts.append(
            jnp.sum(jnp.where(mine, spread, 0.0), axis=0, keepdims=True).astype(jnp.int32)
        )
    return parts


def x_tables(codes, cos_ref, sin_ref):
    shape = (HALF, ALL)
    cosine, sine = trig_wound(iota(shape, 0) * codes[0])
    cos_ref[...] = cosine
    sin_ref[...] = sine


def y_tables(extra, high_ref, low_ref):
    shape = (DEV, 128)
    lane = iota(shape, 1)
    for b in range(COLS):
        lanes = [NB + y * COLS + b for y in range(YS)]
        code = jnp.concatenate([extra[:, i : i + 1] for i in lanes], axis=0).astype(jnp.int32)
        wound = (code & 63) * (lane & 63)
        cosine, sine = trig_wound(wound)
        odd = jnp.broadcast_to(((code >> 6) & 1) == 1, shape)
        first = jnp.where(lane < 64, cosine, sine)
        second = jnp.where(lane < 64, -sine, cosine)
        for c, part in ((0, first), (1, second)):
            rows = slice(c * ALL + b * DEV, c * ALL + (b + 1) * DEV)
            for parity, mine in ((0, jnp.where(odd, 0.0, part)), (1, jnp.where(odd, part, 0.0))):
                high, low = split(mine)
                high_ref[rows, parity * 128 : (parity + 1) * 128] = high
                low_ref[rows, parity * 128 : (parity + 1) * 128] = low


def plane_chunk(re, im, first, count, cos_ref, sin_ref, tables, scratch):
    rows = re.shape[0]
    high_ref, low_ref = scratch
    for i in range(count):
        cx = cos_ref[pl.ds(first + i, 1), :]
        sx = sin_ref[pl.ds(first + i, 1), :]
        for c, part in ((0, re * cx - im * sx), (1, re * sx + im * cx)):
            high, low = split(part)
            high_ref[i * rows : (i + 1) * rows, c * ALL : (c + 1) * ALL] = high
            low_ref[i * rows : (i + 1) * rows, c * ALL : (c + 1) * ALL] = low
    high = high_ref[...]
    table = tables[0][...]
    both = dot(high, table) + dot(low_ref[...], table) + dot(high, tables[1][...])
    return both[:, :128] + both[:, 128:], both[:, :128] - both[:, 128:]


def fetch(pairs, sems):
    copies = [
        pltpu.make_async_copy(source, target, sems.at[i])
        for i, (source, target) in enumerate(pairs)
    ]
    for copy in copies:
        copy.start()
    return copies


def twice(row, half):
    lane = iota(row.shape, 1)
    return jnp.where((lane >= 64) == (half == 1), row, pltpu.roll(row, 64, 1))


def potential_kernel(
    recv_ref, atom_ref, slots_hbm, pot_hbm, old_norm_hbm, res_hbm, old_hbm, kin_hbm,
    energy_hbm, coup_hbm,
    out_ref, grid_ref, scalars_ref,
    slots_ref, pot_ref, old_norm_ref, res_ref, old_ref, kin_ref, energy_ref, coup_ref, sems,
    cos_ref, sin_ref, table_high, table_low, high_ref, low_ref, prod_ref, pair_ref,
):
    copies = fetch(
        (
            (pot_hbm, pot_ref), (old_norm_hbm, old_norm_ref), (res_hbm, res_ref),
            (old_hbm, old_ref), (slots_hbm, slots_ref), (kin_hbm, kin_ref), (energy_hbm, energy_ref), (coup_hbm, coup_ref),
        ),
        sems,
    )
    def store(r, value):
        for y in range(YS):
            out_ref[pl.ds(y * ROWS2 + r, ZS, stride=YS * ROWS2), :] = value[
                y * ZS : (y + 1) * ZS
            ]

    extra = recv_ref[pl.ds(EXTRA, ZS, stride=STAGE2), :]
    codes = column_codes(extra)
    x_tables(codes, cos_ref, sin_ref)
    y_tables(extra, table_high, table_low)
    tables = (table_high, table_low)
    for copy in copies:
        copy.wait()
    norm = row_to_col(jnp.sum(extra, axis=0, keepdims=True), NB)
    beta = norm / row_to_col(old_norm_ref[...], NB)
    values = own_columns(recv_ref)
    beta2 = jnp.concatenate([beta, beta], axis=0)
    re = values[32:48] + beta2 * values[48:64]
    im = values[96:112] + beta2 * values[112:128]

    acc_re = jnp.zeros((16, ALL), F32)
    acc_im = jnp.zeros((16, ALL), F32)
    local = jnp.zeros((NB, 128), F32)
    chunks = []
    for k in range(CH):
        chunks.append(plane_chunk(
            re, im, k * CX, CX, cos_ref, sin_ref, tables, (high_ref.at[k], low_ref.at[k])
        ))
    turns = []
    for k in range(CH):
        first = k * CX
        grids = chunks[k]
        for i in range(CX):
            products = []
            for half in range(2):
                grid = grids[half]
                x = first + i + 32 * half
                up = grid[i * 16 : i * 16 + 8]
                down = grid[i * 16 + 8 : i * 16 + 16]
                grid_ref[x * 16 : x * 16 + 8, :] = up
                grid_ref[x * 16 + 8 : x * 16 + 16, :] = down
                v0, bx, by, bz = (
                    twice(pot_ref[m, :, x // 2 * 128 : x // 2 * 128 + 128], x % 2)
                    for m in range(4)
                )
                new_up = (v0 + bz) * up + bx * down - by * swap_sign(down)
                new_down = bx * up + by * swap_sign(up) + (v0 - bz) * down
                local = local + up * new_up + down * new_down
                products.append((new_up, new_down))
            for j in range(2):
                rows = slice(i * 16 + 8 * j, i * 16 + 8 * j + 8)
                prod_ref[k, rows, 0:128] = products[0][j] + products[1][j]
                prod_ref[k, rows, 128:256] = products[0][j] - products[1][j]
        turns.append(dot3(split(prod_ref[k]), (table_high[...], table_low[...]), "nt"))
    for k in range(CH):
        for i in range(CX):
            x = k * CX + i
            cx = cos_ref[x : x + 1, :]
            sx = sin_ref[x : x + 1, :]
            q_re = turns[k][i * 16 : (i + 1) * 16, :ALL]
            q_im = turns[k][i * 16 : (i + 1) * 16, ALL:]
            acc_re = acc_re + q_re * cx + q_im * sx
            acc_im = acc_im + q_im * cx - q_re * sx
    acc_re = acc_re * VOLUME
    acc_im = acc_im * VOLUME
    for r in range(2):
        pieces = []
        for b in range(4 * r, 4 * r + 4):
            lanes = slice(b * DEV, (b + 1) * DEV)
            pieces += [acc_re[:, lanes], acc_im[:, lanes]]
        store(r, jnp.concatenate(pieces, axis=0).T)

    sums = [
        jnp.sum(recv_ref[pl.ds(YS * COLS + n, ZS, stride=STAGE2), :], axis=0, keepdims=True)
        for n in range(NB)
    ]
    amps = jnp.concatenate(sums, axis=0)
    amps = amps + beta * pltpu.roll(amps, 96, 1)
    amp_re, amp_im = amps[:, 0:32], amps[:, 64:96]
    here = jnp.where(slots_ref[...] == atom_ref[0], 1.0, 0.0)
    lane = iota(here.shape, 1)
    count = jnp.zeros((1, 32), F32)
    for half in range(2):
        mine = jnp.sum(jnp.where((lane >= 64) == (half == 1), here, 0.0), axis=1, keepdims=True)
        place = 2 * iota((8, 32), 0) + half
        count = count + jnp.sum(
            jnp.where((iota((8, 32), 1) & 15) == place, mine, 0.0), axis=0, keepdims=True
        )
    h_re = 0.5 * (coup_ref[0] + coup_ref[0].T)
    h_im = 0.5 * (coup_ref[1] - coup_ref[1].T)
    by_re, by_im = amp_re * count, amp_im * count

    def exact(a, b):
        return lax.dot_general(
            a, b, (((1,), (0,)), ((), ())),
            precision=lax.Precision.HIGHEST, preferred_element_type=F32,
        )

    q_re = (exact(by_re, h_re) + exact(by_im, h_im)) * count
    q_im = (exact(by_im, h_re) - exact(by_re, h_im)) * count
    pair_ref[:, 0:32] = q_re
    pair_ref[:, 32:64] = q_im
    pair_ref[:, 64:128] = jnp.zeros((NB, 64), F32)
    first_half = pair_ref[pl.ds(0, 4, stride=2), :]
    second_half = pair_ref[pl.ds(1, 4, stride=2), :]
    packed = first_half + pltpu.roll(second_half, 64, 1)
    odd = ((iota((DEV, 128), 0) >> 4) & 1) == 1
    for k in range(2):
        store(2 + k, jnp.where(odd, packed[2 + k : 3 + k], packed[k : k + 1]))

    curvature = jnp.sum(local, axis=1, keepdims=True) * VOLUME
    curvature = curvature + jnp.sum(amp_re * q_re + amp_im * q_im, axis=1, keepdims=True)
    weight = kin_ref[...] - row_to_col(energy_ref[...], NB)
    own = jnp.zeros((NB, PW), F32)
    for comp in range(4):
        d = res_ref[0, :, comp, :] + beta * old_ref[0, :, comp, :]
        own = own + d * d
    curvature = curvature + jnp.sum(own * weight, axis=1, keepdims=True)
    store(4, jnp.broadcast_to(col_to_row(curvature, 128), (DEV, 128)))
    lane = iota((NB, 128), 1)
    scalars_ref[...] = jnp.where(lane == 0, norm, jnp.where(lane == 1, beta, 0.0))


def orbital_kernel(
    recv_ref, grid_ref, base_ref, slope_ref, cos_ref, sin_ref, table_high, table_low, high_ref,
    low_ref,
):
    extra = recv_ref[pl.ds(EXTRA, ZS, stride=STAGE2), :]
    x_tables(column_codes(extra), cos_ref, sin_ref)
    y_tables(extra, table_high, table_low)
    values = own_columns(recv_ref)
    re, im = values[0:32], values[64:96]
    lane = iota((NB, 128), 1)

    def terms(o_up, o_down, c_up, c_down):
        same_up = o_up * c_up
        same_down = o_down * c_down
        return (
            same_up + same_down,
            o_up * c_down + o_down * c_up,
            o_down * swap_sign(c_up) - o_up * swap_sign(c_down),
            same_up - same_down,
        )

    def fold(even, odd):
        return 2.0 * (
            jnp.where(lane < 64, even, odd)
            + pltpu.roll(jnp.where(lane < 64, odd, even), 64, 1)
        )

    def chunk(k, carry):
        grids = plane_chunk(
            re, im, k * 8, 8, cos_ref, sin_ref, (table_high, table_low), (high_ref, low_ref)
        )
        for half in range(2):
            for j in range(4):
                with_response, with_direction = [], []
                for i in (2 * j, 2 * j + 1):
                    o_up, o_down, r_up, r_down = (
                        grids[half][i * 32 + 8 * q : i * 32 + 8 * q + 8] for q in range(4)
                    )
                    place = pl.multiple_of((k * 8 + i + 32 * half) * 16, 16)
                    d_up = grid_ref[pl.ds(place, 8), :]
                    d_down = grid_ref[pl.ds(place + 8, 8), :]
                    with_response.append(terms(o_up, o_down, r_up, r_down))
                    with_direction.append(terms(o_up, o_down, d_up, d_down))
                for m in range(4):
                    row = m * 32 + 16 * half + j + 4 * k
                    base_ref[pl.ds(row, 1), :] = jnp.sum(
                        fold(with_response[0][m], with_response[1][m]), axis=0, keepdims=True
                    )
                    slope_ref[pl.ds(row, NB, stride=128), :] = fold(
                        with_direction[0][m], with_direction[1][m]
                    )
        return carry

    lax.fori_loop(0, 4, chunk, 0)


def step_of(recv_ref, scalars_ref):
    total = jnp.sum(recv_ref[pl.ds(4, DEV, stride=ROWS2), :], axis=0, keepdims=True)
    return scalars_ref[:, 0:1] / (row_to_col(total, NB) + SMALL_TERM)


def density_kernel(recv_ref, scalars_ref, base_ref, slope_ref, out_ref, half_ref):
    step = step_of(recv_ref, scalars_ref)
    total = base_ref[...]
    for n in range(NB):
        total = total + step[n : n + 1, :] * slope_ref[n * 128 : (n + 1) * 128, :]
    for copy in range(8):
        out_ref[copy * 128 : (copy + 1) * 128, :] = total
    for k in range(2):
        half_ref[k * DEV : (k + 1) * DEV, :] = recv_ref[pl.ds(2 + k, DEV, stride=ROWS2), :]


def finish_kernel(
    parity_ref, half_ref, other_ref, recv_ref, scalars_ref, resp_ref, res_ref, old_ref, kin_ref, energy_ref, form_ref,
    index_ref, pos_ref, next_ref, residual_ref, direction_ref,
):
    step = step_of(recv_ref, scalars_ref)
    beta = scalars_ref[:, 1:2]
    table = depth_table()
    table = split(jnp.concatenate([table[:64], table[64:]], axis=1))
    group = iota((32, PW), 1) >> 5
    local = jnp.zeros((32, PW), F32)
    for r in range(2):
        values = recv_ref[pl.ds(r, DEV, stride=ROWS2), :].T
        z = dot3(split(values), table)
        for i in range(4):
            re_c, re_s = z[i * 32 : i * 32 + 16, :PW], z[i * 32 : i * 32 + 16, PW:]
            im_c, im_s = z[i * 32 + 16 : i * 32 + 32, :PW], z[i * 32 + 16 : i * 32 + 32, PW:]
            part = jnp.concatenate([re_c + im_s, im_c - re_s], axis=0)
            local = local + jnp.where(group == 4 * r + i, part, 0.0)

    phases = atom_phases(index_ref[...], pos_ref[...])
    phases = split(jnp.concatenate([phases[:64], phases[64:]], axis=1))
    form_re, form_im = form_ref[0, 0], form_ref[0, 1]
    rows_re, rows_im = [[], []], [[], []]
    for k in range(4):
        rows = slice((k & 1) * DEV, (k & 1) * DEV + DEV)
        mine = parity_ref[0] == (k >> 1)
        values = jnp.where(mine, half_ref[rows, :], other_ref[rows, :]).T
        z = dot3(split(values), phases)
        for i in range(2):
            for s in range(2):
                a = i * 64 + s * 16
                re_c, re_s = z[a : a + 16, :PW], z[a : a + 16, PW:]
                im_c, im_s = z[a + 32 : a + 48, :PW], z[a + 32 : a + 48, PW:]
                w_re = re_c + im_s
                w_im = im_c - re_s
                rows_re[s].append(
                    jnp.sum(form_re * w_re - form_im * w_im, axis=0, keepdims=True)
                )
                rows_im[s].append(
                    jnp.sum(form_re * w_im + form_im * w_re, axis=0, keepdims=True)
                )
    weight = kin_ref[...] - row_to_col(energy_ref[...], NB)
    for s in range(2):
        for c in range(2):
            comp = 2 * s + c
            nonlocal_term = jnp.concatenate((rows_re, rows_im)[c][s], axis=0)
            residual = res_ref[0, :, comp, :]
            direction = residual + beta * old_ref[0, :, comp, :]
            place = c * 16 + s * 8
            image = weight * direction + local[place : place + 8] + nonlocal_term
            direction_ref[0, :, comp, :] = direction
            next_ref[0, :, comp, :] = resp_ref[0, :, comp, :] + step * direction
            residual_ref[0, :, comp, :] = residual - step * image


def call(kernel, outs, name, scratch=(), flops=1, size=1, smem=(), hbm=()):
    def space(i):
        return pltpu.SMEM if i in smem else pltpu.HBM if i in hbm else pltpu.VMEM

    def run(*args):
        specs = [pl.BlockSpec(memory_space=space(i)) for i in range(len(args))]
        args = [
            pltpu.with_memory_space_constraint(a, pltpu.HBM) if i in hbm else a
            for i, a in enumerate(args)
        ]
        return pl.pallas_call(
            kernel,
            out_shape=outs,
            in_specs=specs,
            out_specs=jax.tree.map(lambda _: pl.BlockSpec(memory_space=pltpu.VMEM), outs),
            scratch_shapes=list(scratch),
            compiler_params=pltpu.CompilerParams(vmem_limit_bytes=LIMIT),
            cost_estimate=pl.CostEstimate(flops=flops, bytes_accessed=size, transcendentals=0),
            name=name,
        )(*args)

    return run


def shape_of(*dims):
    return jax.ShapeDtypeStruct(dims, F32)


def exchange(values, axis, parts, groups=None):
    rows = values.shape[0] // parts
    if rows % 8:
        flat = values.reshape(parts, 1, rows * 128)
        flat = lax.all_to_all(flat, axis, 0, 0, tiled=True, axis_index_groups=groups)
        return flat.reshape(values.shape)
    out = lax.all_to_all(
        values.reshape(parts, rows, 128), axis, 0, 0, tiled=True, axis_index_groups=groups
    )
    return out.reshape(values.shape)


def per_device(
    orbitals, response, residual, old_direction, old_norm, band_energy, kinetic, form_factor,
    sphere_index, atom_positions, proj_atom, coupling, potential,
):
    scale = 1.0 / (8 * 16384)
    me = lax.axis_index("fft").reshape(1).astype(jnp.int32)
    slots = proj_atom.reshape(8, 128)

    parity = me & 1
    vector = pltpu.VMEM((1, NB, 4, PW), F32)
    sent = call(
        send_kernel, shape_of(YS * STAGE1, 128), "lines_and_amplitudes",
        [vector] * 4 + [
            pltpu.VMEM((1, 2, PA, PW), F32), pltpu.VMEM((1, PW), jnp.int32),
            pltpu.VMEM((3, NG), F32), pltpu.SemaphoreType.DMA((7,)),
        ],
        hbm=range(7),
    )(orbitals, response, residual, old_direction, form_factor, sphere_index, atom_positions)
    sent, me, parity = lax.optimization_barrier((sent, me, parity))
    near = exchange(sent, "fft", YS, SAME_Z)
    joined = call(regroup_kernel, shape_of(ZS * STAGE2, 128), "regroup")(near)
    recv = exchange(joined, "fft", ZS, SAME_Y)
    tables = [
        pltpu.VMEM((HALF, ALL), F32), pltpu.VMEM((HALF, ALL), F32),
        pltpu.VMEM((2 * ALL, 256), BF16), pltpu.VMEM((2 * ALL, 256), BF16),
    ]
    back, grid, scalars = call(
        potential_kernel,
        (shape_of(DEV * ROWS2, 128), shape_of(NG * 16, 128), shape_of(NB, 128)),
        "potential_and_coupling",
        [
            pltpu.VMEM((8, 128), jnp.int32), pltpu.VMEM((4, 1, NG * NG), F32),
            pltpu.VMEM((1, NB), F32), vector, vector, pltpu.VMEM((1, PW), F32),
            pltpu.VMEM((1, NB), F32), pltpu.VMEM((2, 32, 32), F32),
            pltpu.SemaphoreType.DMA((8,)),
        ]
        + tables
        + [pltpu.VMEM((CH, 512 // CH, 2 * ALL), BF16), pltpu.VMEM((CH, 512 // CH, 2 * ALL), BF16)]
        + [pltpu.VMEM((CH, 512 // CH, 256), F32), pltpu.VMEM((NB, 128), F32)],
        smem=(1,), hbm=range(2, 10),
    )(recv, me, slots, potential, old_norm, residual, old_direction, kinetic, band_energy, coupling)
    returned = exchange(back, "fft", DEV)
    base, slope = call(
        orbital_kernel, (shape_of(128, 128), shape_of(NB * 128, 128)), "density_terms",
        tables + [pltpu.VMEM((256, 2 * ALL), BF16), pltpu.VMEM((256, 2 * ALL), BF16)],
        flops=3_000_000_000, size=3_000_000,
    )(recv, grid)
    density, half = call(
        density_kernel, (shape_of(8 * 128, 128), shape_of(2 * DEV, 128)), "density"
    )(returned, scalars, base, slope)
    gathered = exchange(density, "kpool", 8)
    other_half = lax.ppermute(half, "fft", MIRROR)
    outs = call(
        finish_kernel, (shape_of(1, NB, 4, PW),) * 3, "new_vectors",
        flops=3_000_000_000, size=3_000_000, smem=(0,),
    )(
        parity, half, other_half, returned, scalars, response, residual, old_direction, kinetic, band_energy, form_factor,
        sphere_index, atom_positions,
    )
    total = jnp.sum(gathered.reshape(8, 128, 128), axis=0) * scale
    return outs[0], outs[1], outs[2], total.reshape(4, 1, NG * NG)


def solution(mesh):
    vector = P("kpool", None, None, "fft")
    in_specs = (
        vector, vector, vector, vector, P("kpool", None), P("kpool", None), P("kpool", "fft"),
        vector, P("kpool", "fft"), P(), P(), P(), P(None, "fft", None),
    )
    out_specs = (vector, vector, vector, P(None, "fft", None))
    return jax.shard_map(
        per_device, mesh=mesh, in_specs=in_specs, out_specs=out_specs, check_vma=False
    )
```

```python
import math

import jax
import jax.numpy as jnp
from jax import lax
from jax.experimental import pallas as pl
from jax.experimental.pallas import tpu as pltpu
from jax.sharding import PartitionSpec as P

NG = 64
STICK = 32
NB = 8
COLS = 8
PW = COLS * STICK
PA = 16
DEV = 64
ZS = 16
YS = 4
EXTRA = 40
FIRST_Z = 8
FIRST_Y = 2
ORDER_Z = [(z + FIRST_Z) % ZS for z in range(ZS)]
ORDER_Y = [(y + FIRST_Y) % YS for y in range(YS)]
SAME_Z = [[z * YS + y for y in ORDER_Y] for z in range(ZS)]
SAME_Y = [[z * YS + y for z in ORDER_Z] for y in range(YS)]
EVERY = [[z * YS + y for z in ORDER_Z for y in ORDER_Y]]
POINTS = [[4, 5, 6, 7, 0, 1, 2, 3]]
MIRROR = [(i, i ^ 1) for i in range(DEV)]
HALF = NG // 2
CH = 2
CX = HALF // CH
ALL = COLS * DEV
STAGE1 = 16 * ZS + 8
STAGE2 = 41
ROWS2 = 5
SMALL_TERM = 1e-06
VOLUME = 1.0 / (NG * NG * NG)
F32 = jnp.float32
BF16 = jnp.bfloat16
LIMIT = 48 * 1024 * 1024

COS = (1.0, -19.73920440673828, 64.93911743164062, -85.45014190673828,
       60.16762924194336, -25.967599868774414, 6.528658390045166)
SIN = (6.2831854820251465, -41.34170150756836, 81.60513305664062, -76.70301818847656,
       42.02592849731445, -14.899847030639648, 3.2381374835968018)


def iota(shape, dim):
    return lax.broadcasted_iota(jnp.int32, shape, dim)


def horner(coefficients, w):
    total = jnp.full_like(w, coefficients[-1])
    for c in coefficients[-2::-1]:
        total = total * w + c
    return total


def trig_turns(turns):
    r = turns - jnp.floor(turns + 0.5)
    w = r * r
    return horner(COS, w), r * horner(SIN, w)


def trig_wound(wound):
    r = (((wound + 32) & 63) - 32).astype(F32) * (1.0 / 64.0)
    w = r * r
    return horner(COS, w), r * horner(SIN, w)


def split(x):
    high = x.astype(BF16)
    return high, (x - high.astype(F32)).astype(BF16)


def dot(a, b, form="nn"):
    return lax.dot_general(
        a, b, (((1,), (0 if form == "nn" else 1,)), ((), ())), preferred_element_type=F32
    )


def dot3(a, b, form="nn"):
    return dot(a[0], b[0], form) + dot(a[1], b[0], form) + dot(a[0], b[1], form)


def swap_sign(x):
    lane = iota(x.shape, x.ndim - 1)
    return jnp.where(lane < 64, -1.0, 1.0) * pltpu.roll(x, 64, x.ndim - 1)


def row_to_col(row, n):
    shape = (n, row.shape[1])
    return jnp.sum(jnp.where(iota(shape, 0) == iota(shape, 1), row, 0.0), axis=1, keepdims=True)


def col_to_row(col, width):
    shape = (col.shape[0], width)
    return jnp.sum(jnp.where(iota(shape, 0) == iota(shape, 1), col, 0.0), axis=0, keepdims=True)


def signed(g):
    return jnp.where(g < 32, g, g - 64).astype(F32)


def device_at(z, y):
    return (((z + FIRST_Z) & 15) << 2) | ((y + FIRST_Y) & 3)


def by_y(i):
    return device_at(i & 15, i >> 4)


def by_z(i):
    return device_at(i >> 2, i & 3)


def atom_phases(index, positions, order=lambda i: i):
    fx = signed(index >> 12)
    fy = signed((index >> 6) & 63)
    fz = signed(index & 63)
    mine = iota((NG, NG), 1) == order(iota((NG, NG), 0))
    tx, ty, tz = (
        jnp.sum(jnp.where(mine, positions[i : i + 1, :], 0.0), axis=1, keepdims=True)
        for i in range(3)
    )
    turns = tx * fx + ty * fy + tz * fz
    cosine, sine = trig_turns(turns)
    return jnp.concatenate([cosine, sine], axis=0)


def depth_table(order=lambda i: i):
    shape = (NG, PW)
    wound = order(iota(shape, 0)) * ((iota(shape, 1) & 31) - 16)
    cosine, sine = trig_wound(wound)
    return jnp.concatenate([cosine, sine], axis=0)


def send_kernel(
    orb_hbm, resp_hbm, res_hbm, old_hbm, form_hbm, index_hbm, pos_hbm, out_ref,
    orb_ref, resp_ref, res_ref, old_ref, form_ref, index_ref, pos_ref, sems,
):
    def store(r, value):
        for y in range(YS):
            out_ref[pl.ds(y * STAGE1 + r, ZS, stride=16), :] = value[y * ZS : (y + 1) * ZS]

    arrays = (orb_ref, resp_ref, res_ref, old_ref)
    copies = fetch(
        (
            (index_hbm, index_ref), (pos_hbm, pos_ref), (orb_hbm, orb_ref), (resp_hbm, resp_ref),
            (res_hbm, res_ref), (old_hbm, old_ref), (form_hbm, form_ref),
        ),
        sems,
    )
    table = depth_table(by_y)
    for copy in copies[:2]:
        copy.wait()
    index = index_ref[...]
    phases = split(atom_phases(index, pos_ref[...], by_y))
    for copy in copies[2:]:
        copy.wait()
    lines = jnp.concatenate(
        [ref[0, :, 2 * s + c, :] for c in range(2) for ref in arrays for s in range(2)], axis=0
    )
    lines = split(lines)
    group = iota(table.shape, 1) >> 5
    for b in range(COLS):
        z = dot3(split(jnp.where(group == b, table, 0.0)), lines, "nt")
        store(b, z[:64] + swap_sign(z[64:]))

    form_re, form_im = form_ref[0, 0], form_ref[0, 1]
    for n in range(NB):
        parts_re, parts_im = [], []
        for ref in arrays[2:]:
            for s in range(2):
                d_re = ref[0, n, 2 * s : 2 * s + 1, :]
                d_im = ref[0, n, 2 * s + 1 : 2 * s + 2, :]
                parts_re.append(form_re * d_re + form_im * d_im)
                parts_im.append(form_re * d_im - form_im * d_re)
        values = split(jnp.concatenate(parts_re + parts_im, axis=0))
        z = dot3(phases, values, "nt")
        store(COLS + n, z[:64] + swap_sign(z[64:]))

    squares = jnp.zeros((NB, PW), F32)
    for comp in range(4):
        r = res_ref[0, :, comp, :]
        squares = squares + r * r
    row = col_to_row(jnp.sum(squares, axis=1, keepdims=True), 128)
    codes = (index >> 6).astype(F32)
    lane = iota((1, PW), 1)
    target = iota((1, 128), 1)
    for b in range(COLS):
        code = jnp.sum(jnp.where(lane == STICK * b, codes, 0.0), axis=1, keepdims=True)
        row = jnp.where(target == COLS + b, code, row)
    for y in range(YS):
        out_ref[(y + 1) * STAGE1 - 8 : (y + 1) * STAGE1, :] = jnp.broadcast_to(row, (8, 128))


def regroup_kernel(in_ref, out_ref):
    for y in range(YS):
        for b in range(COLS):
            out_ref[pl.ds(y * COLS + b, ZS, stride=STAGE2), :] = in_ref[
                pl.ds(y * STAGE1 + b, ZS, stride=16), :
            ]
    for n in range(NB):
        parts = [in_ref[pl.ds(y * STAGE1 + COLS + n, ZS, stride=16), :] for y in range(YS)]
        out_ref[pl.ds(YS * COLS + n, ZS, stride=STAGE2), :] = (
            (parts[0] + parts[1]) + (parts[2] + parts[3])
        )
    lane = iota((8, 128), 1)
    row = jnp.zeros((8, 128), F32)
    for y in range(YS):
        extra = in_ref[(y + 1) * STAGE1 - 8 : (y + 1) * STAGE1, :]
        row = row + jnp.where(lane < NB, extra, 0.0)
        first = NB + y * COLS
        moved = extra if y == 0 else pltpu.roll(extra, y * COLS, 1)
        row = row + jnp.where((lane >= first) & (lane < first + COLS), moved, 0.0)
    out_ref[pl.ds(EXTRA, ZS, stride=STAGE2), :] = jnp.concatenate([row, row], axis=0)


def own_columns(recv_ref):
    values = jnp.concatenate(
        [
            recv_ref[pl.ds(y * COLS + b, ZS, stride=STAGE2), :]
            for b in range(COLS)
            for y in range(YS)
        ],
        axis=0,
    )
    return values.T


def column_codes(extra):
    codes = extra.astype(jnp.int32)
    shape = (128, ALL)
    lane = iota(shape, 1)
    pick = jnp.where(iota(shape, 0) == NB + ((lane >> 4) & 3) * COLS + (lane >> 6), 1.0, 0.0)
    mine = (iota((ZS, ALL), 1) & 15) == iota((ZS, ALL), 0)
    used = iota((ZS, 128), 1) >= NB
    parts = []
    for value in (codes >> 6, codes & 63):
        value = jnp.where(used, value, 0).astype(F32).astype(BF16)
        spread = dot(value, pick.astype(BF16))
        parts.append(
            jnp.sum(jnp.where(mine, spread, 0.0), axis=0, keepdims=True).astype(jnp.int32)
        )
    return parts


def x_tables(codes, cos_ref, sin_ref):
    shape = (HALF, ALL)
    cosine, sine = trig_wound(iota(shape, 0) * codes[0])
    cos_ref[...] = cosine
    sin_ref[...] = sine


def y_tables(extra, high_ref, low_ref):
    shape = (DEV, 128)
    lane = iota(shape, 1)
    for b in range(COLS):
        lanes = [NB + y * COLS + b for y in range(YS)]
        code = jnp.concatenate([extra[:, i : i + 1] for i in lanes], axis=0).astype(jnp.int32)
        wound = (code & 63) * (lane & 63)
        cosine, sine = trig_wound(wound)
        odd = jnp.broadcast_to(((code >> 6) & 1) == 1, shape)
        first = jnp.where(lane < 64, cosine, sine)
        second = jnp.where(lane < 64, -sine, cosine)
        for c, part in ((0, first), (1, second)):
            rows = slice(c * ALL + b * DEV, c * ALL + (b + 1) * DEV)
            for parity, mine in ((0, jnp.where(odd, 0.0, part)), (1, jnp.where(odd, part, 0.0))):
                high, low = split(mine)
                high_ref[rows, parity * 128 : (parity + 1) * 128] = high
                low_ref[rows, parity * 128 : (parity + 1) * 128] = low


def plane_chunk(re, im, first, count, cos_ref, sin_ref, tables, scratch):
    rows = re.shape[0]
    high_ref, low_ref = scratch
    for i in range(count):
        cx = cos_ref[pl.ds(first + i, 1), :]
        sx = sin_ref[pl.ds(first + i, 1), :]
        for c, part in ((0, re * cx - im * sx), (1, re * sx + im * cx)):
            high, low = split(part)
            high_ref[i * rows : (i + 1) * rows, c * ALL : (c + 1) * ALL] = high
            low_ref[i * rows : (i + 1) * rows, c * ALL : (c + 1) * ALL] = low
    high = high_ref[...]
    table = tables[0][...]
    both = dot(high, table) + dot(low_ref[...], table) + dot(high, tables[1][...])
    return both[:, :128] + both[:, 128:], both[:, :128] - both[:, 128:]


def fetch(pairs, sems):
    copies = [
        pltpu.make_async_copy(source, target, sems.at[i])
        for i, (source, target) in enumerate(pairs)
    ]
    for copy in copies:
        copy.start()
    return copies


def twice(row, half):
    lane = iota(row.shape, 1)
    return jnp.where((lane >= 64) == (half == 1), row, pltpu.roll(row, 64, 1))


def potential_kernel(
    recv_ref, atom_ref, slots_hbm, pot_hbm, old_norm_hbm, res_hbm, old_hbm, kin_hbm,
    energy_hbm, coup_hbm,
    out_ref, grid_ref, scalars_ref,
    slots_ref, pot_ref, old_norm_ref, res_ref, old_ref, kin_ref, energy_ref, coup_ref, sems,
    cos_ref, sin_ref, table_high, table_low, high_ref, low_ref, prod_ref, pair_ref,
):
    copies = fetch(
        (
            (pot_hbm, pot_ref), (old_norm_hbm, old_norm_ref), (res_hbm, res_ref),
            (old_hbm, old_ref), (slots_hbm, slots_ref), (kin_hbm, kin_ref), (energy_hbm, energy_ref), (coup_hbm, coup_ref),
        ),
        sems,
    )
    def store(r, value):
        for y in range(YS):
            out_ref[pl.ds(y * ROWS2 + r, ZS, stride=YS * ROWS2), :] = value[
                y * ZS : (y + 1) * ZS
            ]

    extra = recv_ref[pl.ds(EXTRA, ZS, stride=STAGE2), :]
    codes = column_codes(extra)
    x_tables(codes, cos_ref, sin_ref)
    y_tables(extra, table_high, table_low)
    tables = (table_high, table_low)
    for copy in copies:
        copy.wait()
    norm = row_to_col(jnp.sum(extra, axis=0, keepdims=True), NB)
    beta = norm / row_to_col(old_norm_ref[...], NB)
    values = own_columns(recv_ref)
    beta2 = jnp.concatenate([beta, beta], axis=0)
    re = values[32:48] + beta2 * values[48:64]
    im = values[96:112] + beta2 * values[112:128]

    acc_re = jnp.zeros((16, ALL), F32)
    acc_im = jnp.zeros((16, ALL), F32)
    local = jnp.zeros((NB, 128), F32)
    chunks = []
    for k in range(CH):
        chunks.append(plane_chunk(
            re, im, k * CX, CX, cos_ref, sin_ref, tables, (high_ref.at[k], low_ref.at[k])
        ))
    turns = []
    for k in range(CH):
        first = k * CX
        grids = chunks[k]
        for i in range(CX):
            products = []
            for half in range(2):
                grid = grids[half]
                x = first + i + 32 * half
                up = grid[i * 16 : i * 16 + 8]
                down = grid[i * 16 + 8 : i * 16 + 16]
                grid_ref[x * 16 : x * 16 + 8, :] = up
                grid_ref[x * 16 + 8 : x * 16 + 16, :] = down
                v0, bx, by, bz = (
                    twice(pot_ref[m, :, x // 2 * 128 : x // 2 * 128 + 128], x % 2)
                    for m in range(4)
                )
                new_up = (v0 + bz) * up + bx * down - by * swap_sign(down)
                new_down = bx * up + by * swap_sign(up) + (v0 - bz) * down
                local = local + up * new_up + down * new_down
                products.append((new_up, new_down))
            for j in range(2):
                rows = slice(i * 16 + 8 * j, i * 16 + 8 * j + 8)
                prod_ref[k, rows, 0:128] = products[0][j] + products[1][j]
                prod_ref[k, rows, 128:256] = products[0][j] - products[1][j]
        turns.append(dot3(split(prod_ref[k]), (table_high[...], table_low[...]), "nt"))
    for k in range(CH):
        for i in range(CX):
            x = k * CX + i
            cx = cos_ref[x : x + 1, :]
            sx = sin_ref[x : x + 1, :]
            q_re = turns[k][i * 16 : (i + 1) * 16, :ALL]
            q_im = turns[k][i * 16 : (i + 1) * 16, ALL:]
            acc_re = acc_re + q_re * cx + q_im * sx
            acc_im = acc_im + q_im * cx - q_re * sx
    acc_re = acc_re * VOLUME
    acc_im = acc_im * VOLUME
    for r in range(2):
        pieces = []
        for b in range(4 * r, 4 * r + 4):
            lanes = slice(b * DEV, (b + 1) * DEV)
            pieces += [acc_re[:, lanes], acc_im[:, lanes]]
        store(r, jnp.concatenate(pieces, axis=0).T)

    sums = [
        jnp.sum(recv_ref[pl.ds(YS * COLS + n, ZS, stride=STAGE2), :], axis=0, keepdims=True)
        for n in range(NB)
    ]
    amps = jnp.concatenate(sums, axis=0)
    amps = amps + beta * pltpu.roll(amps, 96, 1)
    amp_re, amp_im = amps[:, 0:32], amps[:, 64:96]
    here = jnp.where(slots_ref[...] == atom_ref[0], 1.0, 0.0)
    lane = iota(here.shape, 1)
    count = jnp.zeros((1, 32), F32)
    for half in range(2):
        mine = jnp.sum(jnp.where((lane >= 64) == (half == 1), here, 0.0), axis=1, keepdims=True)
        place = 2 * iota((8, 32), 0) + half
        count = count + jnp.sum(
            jnp.where((iota((8, 32), 1) & 15) == place, mine, 0.0), axis=0, keepdims=True
        )
    h_re = 0.5 * (coup_ref[0] + coup_ref[0].T)
    h_im = 0.5 * (coup_ref[1] - coup_ref[1].T)
    by_re, by_im = amp_re * count, amp_im * count

    def exact(a, b):
        return lax.dot_general(
            a, b, (((1,), (0,)), ((), ())),
            precision=lax.Precision.HIGHEST, preferred_element_type=F32,
        )

    q_re = (exact(by_re, h_re) + exact(by_im, h_im)) * count
    q_im = (exact(by_im, h_re) - exact(by_re, h_im)) * count
    pair_ref[:, 0:32] = q_re
    pair_ref[:, 32:64] = q_im
    pair_ref[:, 64:128] = jnp.zeros((NB, 64), F32)
    first_half = pair_ref[pl.ds(0, 4, stride=2), :]
    second_half = pair_ref[pl.ds(1, 4, stride=2), :]
    packed = first_half + pltpu.roll(second_half, 64, 1)
    odd = ((iota((DEV, 128), 0) >> 4) & 1) == 1
    for k in range(2):
        store(2 + k, jnp.where(odd, packed[2 + k : 3 + k], packed[k : k + 1]))

    curvature = jnp.sum(local, axis=1, keepdims=True) * VOLUME
    curvature = curvature + jnp.sum(amp_re * q_re + amp_im * q_im, axis=1, keepdims=True)
    weight = kin_ref[...] - row_to_col(energy_ref[...], NB)
    own = jnp.zeros((NB, PW), F32)
    for comp in range(4):
        d = res_ref[0, :, comp, :] + beta * old_ref[0, :, comp, :]
        own = own + d * d
    curvature = curvature + jnp.sum(own * weight, axis=1, keepdims=True)
    store(4, jnp.broadcast_to(col_to_row(curvature, 128), (DEV, 128)))
    lane = iota((NB, 128), 1)
    scalars_ref[...] = jnp.where(lane == 0, norm, jnp.where(lane == 1, beta, 0.0))


def orbital_kernel(
    recv_ref, grid_ref, base_ref, slope_ref, cos_ref, sin_ref, table_high, table_low, high_ref,
    low_ref,
):
    extra = recv_ref[pl.ds(EXTRA, ZS, stride=STAGE2), :]
    x_tables(column_codes(extra), cos_ref, sin_ref)
    y_tables(extra, table_high, table_low)
    values = own_columns(recv_ref)
    re, im = values[0:32], values[64:96]
    lane = iota((NB, 128), 1)

    def terms(o_up, o_down, c_up, c_down):
        same_up = o_up * c_up
        same_down = o_down * c_down
        return (
            same_up + same_down,
            o_up * c_down + o_down * c_up,
            o_down * swap_sign(c_up) - o_up * swap_sign(c_down),
            same_up - same_down,
        )

    def fold(even, odd):
        return 2.0 * (
            jnp.where(lane < 64, even, odd)
            + pltpu.roll(jnp.where(lane < 64, odd, even), 64, 1)
        )

    def chunk(k, carry):
        grids = plane_chunk(
            re, im, k * 8, 8, cos_ref, sin_ref, (table_high, table_low), (high_ref, low_ref)
        )
        for half in range(2):
            for j in range(4):
                with_response, with_direction = [], []
                for i in (2 * j, 2 * j + 1):
                    o_up, o_down, r_up, r_down = (
                        grids[half][i * 32 + 8 * q : i * 32 + 8 * q + 8] for q in range(4)
                    )
                    place = pl.multiple_of((k * 8 + i + 32 * half) * 16, 16)
                    d_up = grid_ref[pl.ds(place, 8), :]
                    d_down = grid_ref[pl.ds(place + 8, 8), :]
                    with_response.append(terms(o_up, o_down, r_up, r_down))
                    with_direction.append(terms(o_up, o_down, d_up, d_down))
                for m in range(4):
                    row = m * 32 + 16 * half + j + 4 * k
                    base_ref[pl.ds(row, 1), :] = jnp.sum(
                        fold(with_response[0][m], with_response[1][m]), axis=0, keepdims=True
                    )
                    slope_ref[pl.ds(row, NB, stride=128), :] = fold(
                        with_direction[0][m], with_direction[1][m]
                    )
        return carry

    lax.fori_loop(0, 4, chunk, 0)


def step_of(recv_ref, scalars_ref):
    total = jnp.sum(recv_ref[pl.ds(4, DEV, stride=ROWS2), :], axis=0, keepdims=True)
    return scalars_ref[:, 0:1] / (row_to_col(total, NB) + SMALL_TERM)


def density_kernel(recv_ref, scalars_ref, base_ref, slope_ref, out_ref, half_ref):
    step = step_of(recv_ref, scalars_ref)
    total = base_ref[...]
    for n in range(NB):
        total = total + step[n : n + 1, :] * slope_ref[n * 128 : (n + 1) * 128, :]
    for copy in range(8):
        out_ref[copy * 128 : (copy + 1) * 128, :] = total
    for k in range(2):
        half_ref[k * DEV : (k + 1) * DEV, :] = recv_ref[pl.ds(2 + k, DEV, stride=ROWS2), :]


def finish_kernel(
    parity_ref, half_ref, other_ref, recv_ref, scalars_ref, resp_ref, res_ref, old_ref, kin_ref, energy_ref, form_ref,
    index_ref, pos_ref, next_ref, residual_ref, direction_ref,
):
    step = step_of(recv_ref, scalars_ref)
    beta = scalars_ref[:, 1:2]
    table = depth_table(by_z)
    table = split(jnp.concatenate([table[:64], table[64:]], axis=1))
    group = iota((32, PW), 1) >> 5
    local = jnp.zeros((32, PW), F32)
    for r in range(2):
        values = recv_ref[pl.ds(r, DEV, stride=ROWS2), :].T
        z = dot3(split(values), table)
        for i in range(4):
            re_c, re_s = z[i * 32 : i * 32 + 16, :PW], z[i * 32 : i * 32 + 16, PW:]
            im_c, im_s = z[i * 32 + 16 : i * 32 + 32, :PW], z[i * 32 + 16 : i * 32 + 32, PW:]
            part = jnp.concatenate([re_c + im_s, im_c - re_s], axis=0)
            local = local + jnp.where(group == 4 * r + i, part, 0.0)

    phases = atom_phases(index_ref[...], pos_ref[...], by_z)
    phases = split(jnp.concatenate([phases[:64], phases[64:]], axis=1))
    form_re, form_im = form_ref[0, 0], form_ref[0, 1]
    rows_re, rows_im = [[], []], [[], []]
    for k in range(4):
        rows = slice((k & 1) * DEV, (k & 1) * DEV + DEV)
        mine = parity_ref[0] == (k >> 1)
        values = jnp.where(mine, half_ref[rows, :], other_ref[rows, :]).T
        z = dot3(split(values), phases)
        for i in range(2):
            for s in range(2):
                a = i * 64 + s * 16
                re_c, re_s = z[a : a + 16, :PW], z[a : a + 16, PW:]
                im_c, im_s = z[a + 32 : a + 48, :PW], z[a + 32 : a + 48, PW:]
                w_re = re_c + im_s
                w_im = im_c - re_s
                rows_re[s].append(
                    jnp.sum(form_re * w_re - form_im * w_im, axis=0, keepdims=True)
                )
                rows_im[s].append(
                    jnp.sum(form_re * w_im + form_im * w_re, axis=0, keepdims=True)
                )
    weight = kin_ref[...] - row_to_col(energy_ref[...], NB)
    for s in range(2):
        for c in range(2):
            comp = 2 * s + c
            nonlocal_term = jnp.concatenate((rows_re, rows_im)[c][s], axis=0)
            residual = res_ref[0, :, comp, :]
            direction = residual + beta * old_ref[0, :, comp, :]
            place = c * 16 + s * 8
            image = weight * direction + local[place : place + 8] + nonlocal_term
            direction_ref[0, :, comp, :] = direction
            next_ref[0, :, comp, :] = resp_ref[0, :, comp, :] + step * direction
            residual_ref[0, :, comp, :] = residual - step * image


def call(kernel, outs, name, scratch=(), flops=1, size=1, smem=(), hbm=()):
    def space(i):
        return pltpu.SMEM if i in smem else pltpu.HBM if i in hbm else pltpu.VMEM

    def run(*args):
        specs = [pl.BlockSpec(memory_space=space(i)) for i in range(len(args))]
        args = [
            pltpu.with_memory_space_constraint(a, pltpu.HBM) if i in hbm else a
            for i, a in enumerate(args)
        ]
        return pl.pallas_call(
            kernel,
            out_shape=outs,
            in_specs=specs,
            out_specs=jax.tree.map(lambda _: pl.BlockSpec(memory_space=pltpu.VMEM), outs),
            scratch_shapes=list(scratch),
            compiler_params=pltpu.CompilerParams(vmem_limit_bytes=LIMIT),
            cost_estimate=pl.CostEstimate(flops=flops, bytes_accessed=size, transcendentals=0),
            name=name,
        )(*args)

    return run


def shape_of(*dims):
    return jax.ShapeDtypeStruct(dims, F32)


def exchange(values, axis, parts, groups=None):
    rows = values.shape[0] // parts
    if rows % 8:
        flat = values.reshape(parts, 1, rows * 128)
        flat = lax.all_to_all(flat, axis, 0, 0, tiled=True, axis_index_groups=groups)
        return flat.reshape(values.shape)
    out = lax.all_to_all(
        values.reshape(parts, rows, 128), axis, 0, 0, tiled=True, axis_index_groups=groups
    )
    return out.reshape(values.shape)


def per_device(
    orbitals, response, residual, old_direction, old_norm, band_energy, kinetic, form_factor,
    sphere_index, atom_positions, proj_atom, coupling, potential,
):
    scale = 1.0 / (8 * 16384)
    me = lax.axis_index("fft").reshape(1).astype(jnp.int32)
    slots = proj_atom.reshape(8, 128)

    parity = me & 1
    vector = pltpu.VMEM((1, NB, 4, PW), F32)
    sent = call(
        send_kernel, shape_of(YS * STAGE1, 128), "lines_and_amplitudes",
        [vector] * 4 + [
            pltpu.VMEM((1, 2, PA, PW), F32), pltpu.VMEM((1, PW), jnp.int32),
            pltpu.VMEM((3, NG), F32), pltpu.SemaphoreType.DMA((7,)),
        ],
        hbm=range(7),
    )(orbitals, response, residual, old_direction, form_factor, sphere_index, atom_positions)
    sent, me, parity = lax.optimization_barrier((sent, me, parity))
    near = exchange(sent, "fft", YS, SAME_Z)
    joined = call(regroup_kernel, shape_of(ZS * STAGE2, 128), "regroup")(near)
    recv = exchange(joined, "fft", ZS, SAME_Y)
    tables = [
        pltpu.VMEM((HALF, ALL), F32), pltpu.VMEM((HALF, ALL), F32),
        pltpu.VMEM((2 * ALL, 256), BF16), pltpu.VMEM((2 * ALL, 256), BF16),
    ]
    back, grid, scalars = call(
        potential_kernel,
        (shape_of(DEV * ROWS2, 128), shape_of(NG * 16, 128), shape_of(NB, 128)),
        "potential_and_coupling",
        [
            pltpu.VMEM((8, 128), jnp.int32), pltpu.VMEM((4, 1, NG * NG), F32),
            pltpu.VMEM((1, NB), F32), vector, vector, pltpu.VMEM((1, PW), F32),
            pltpu.VMEM((1, NB), F32), pltpu.VMEM((2, 32, 32), F32),
            pltpu.SemaphoreType.DMA((8,)),
        ]
        + tables
        + [pltpu.VMEM((CH, 512 // CH, 2 * ALL), BF16), pltpu.VMEM((CH, 512 // CH, 2 * ALL), BF16)]
        + [pltpu.VMEM((CH, 512 // CH, 256), F32), pltpu.VMEM((NB, 128), F32)],
        smem=(1,), hbm=range(2, 10),
    )(recv, me, slots, potential, old_norm, residual, old_direction, kinetic, band_energy, coupling)
    returned = exchange(back, "fft", DEV, EVERY)
    base, slope = call(
        orbital_kernel, (shape_of(128, 128), shape_of(NB * 128, 128)), "density_terms",
        tables + [pltpu.VMEM((256, 2 * ALL), BF16), pltpu.VMEM((256, 2 * ALL), BF16)],
        flops=3_000_000_000, size=3_000_000,
    )(recv, grid)
    density, half = call(
        density_kernel, (shape_of(8 * 128, 128), shape_of(2 * DEV, 128)), "density"
    )(returned, scalars, base, slope)
    gathered = exchange(density, "kpool", 8, POINTS)
    other_half = lax.ppermute(half, "fft", MIRROR)
    outs = call(
        finish_kernel, (shape_of(1, NB, 4, PW),) * 3, "new_vectors",
        flops=3_000_000_000, size=3_000_000, smem=(0,),
    )(
        parity, half, other_half, returned, scalars, response, residual, old_direction, kinetic, band_energy, form_factor,
        sphere_index, atom_positions,
    )
    total = jnp.sum(gathered.reshape(8, 128, 128), axis=0) * scale
    return outs[0], outs[1], outs[2], total.reshape(4, 1, NG * NG)


def solution(mesh):
    vector = P("kpool", None, None, "fft")
    in_specs = (
        vector, vector, vector, vector, P("kpool", None), P("kpool", None), P("kpool", "fft"),
        vector, P("kpool", "fft"), P(), P(), P(), P(None, "fft", None),
    )
    out_specs = (vector, vector, vector, P(None, "fft", None))
    return jax.shard_map(
        per_device, mesh=mesh, in_specs=in_specs, out_specs=out_specs, check_vma=False
    )
```

```python
import math

import jax
import jax.numpy as jnp
from jax import lax
from jax.experimental import pallas as pl
from jax.experimental.pallas import tpu as pltpu
from jax.sharding import PartitionSpec as P

NG = 64
STICK = 32
NB = 8
COLS = 8
PW = COLS * STICK
PA = 16
DEV = 64
ZS = 16
YS = 4
EXTRA = 40
FIRST_Z = 8
FIRST_Y = 2
ORDER_Z = [(z + FIRST_Z) % ZS for z in range(ZS)]
ORDER_Y = [(y + FIRST_Y) % YS for y in range(YS)]
SAME_Z = [[z * YS + y for y in ORDER_Y] for z in range(ZS)]
SAME_Y = [[z * YS + y for z in ORDER_Z] for y in range(YS)]
EVERY = [[z * YS + y for z in ORDER_Z for y in ORDER_Y]]
POINTS = [[4, 5, 6, 7, 0, 1, 2, 3]]
MIRROR = [(i, i ^ 1) for i in range(DEV)]
HALF = NG // 2
CH = 2
CX = HALF // CH
ALL = COLS * DEV
STAGE1 = 16 * ZS + 8
STAGE2 = 41
ROWS2 = 5
SMALL_TERM = 1e-06
VOLUME = 1.0 / (NG * NG * NG)
F32 = jnp.float32
BF16 = jnp.bfloat16
LIMIT = 48 * 1024 * 1024

COS = (1.0, -19.73920440673828, 64.93911743164062, -85.45014190673828,
       60.16762924194336, -25.967599868774414, 6.528658390045166)
SIN = (6.2831854820251465, -41.34170150756836, 81.60513305664062, -76.70301818847656,
       42.02592849731445, -14.899847030639648, 3.2381374835968018)


def iota(shape, dim):
    return lax.broadcasted_iota(jnp.int32, shape, dim)


def horner(coefficients, w):
    total = jnp.full_like(w, coefficients[-1])
    for c in coefficients[-2::-1]:
        total = total * w + c
    return total


def trig_turns(turns):
    r = turns - jnp.floor(turns + 0.5)
    w = r * r
    return horner(COS, w), r * horner(SIN, w)


def trig_wound(wound):
    r = (((wound + 32) & 63) - 32).astype(F32) * (1.0 / 64.0)
    w = r * r
    return horner(COS, w), r * horner(SIN, w)


def split(x):
    high = x.astype(BF16)
    return high, (x - high.astype(F32)).astype(BF16)


def dot(a, b, form="nn"):
    return lax.dot_general(
        a, b, (((1,), (0 if form == "nn" else 1,)), ((), ())), preferred_element_type=F32
    )


def dot3(a, b, form="nn"):
    return dot(a[0], b[0], form) + dot(a[1], b[0], form) + dot(a[0], b[1], form)


def swap_sign(x):
    lane = iota(x.shape, x.ndim - 1)
    return jnp.where(lane < 64, -1.0, 1.0) * pltpu.roll(x, 64, x.ndim - 1)


def row_to_col(row, n):
    shape = (n, row.shape[1])
    return jnp.sum(jnp.where(iota(shape, 0) == iota(shape, 1), row, 0.0), axis=1, keepdims=True)


def col_to_row(col, width):
    shape = (col.shape[0], width)
    return jnp.sum(jnp.where(iota(shape, 0) == iota(shape, 1), col, 0.0), axis=0, keepdims=True)


def signed(g):
    return jnp.where(g < 32, g, g - 64).astype(F32)


def device_at(z, y):
    return (((z + FIRST_Z) & 15) << 2) | ((y + FIRST_Y) & 3)


def by_y(i):
    return device_at(i & 15, i >> 4)


def by_z(i):
    return device_at(i >> 2, i & 3)


def atom_phases(index, positions, order=lambda i: i):
    fx = signed(index >> 12)
    fy = signed((index >> 6) & 63)
    fz = signed(index & 63)
    mine = iota((NG, NG), 1) == order(iota((NG, NG), 0))
    tx, ty, tz = (
        jnp.sum(jnp.where(mine, positions[i : i + 1, :], 0.0), axis=1, keepdims=True)
        for i in range(3)
    )
    turns = tx * fx + ty * fy + tz * fz
    cosine, sine = trig_turns(turns)
    return jnp.concatenate([cosine, sine], axis=0)


def depth_table(order=lambda i: i):
    shape = (NG, PW)
    wound = order(iota(shape, 0)) * ((iota(shape, 1) & 31) - 16)
    cosine, sine = trig_wound(wound)
    return jnp.concatenate([cosine, sine], axis=0)


def send_kernel(
    orb_hbm, resp_hbm, res_hbm, old_hbm, form_hbm, index_hbm, pos_hbm, out_ref,
    orb_ref, resp_ref, res_ref, old_ref, form_ref, index_ref, pos_ref, sems,
):
    def store(r, value):
        for y in range(YS):
            out_ref[pl.ds(y * STAGE1 + r, ZS, stride=16), :] = value[y * ZS : (y + 1) * ZS]

    arrays = (orb_ref, resp_ref, res_ref, old_ref)
    copies = fetch(
        (
            (index_hbm, index_ref), (pos_hbm, pos_ref), (orb_hbm, orb_ref), (resp_hbm, resp_ref),
            (res_hbm, res_ref), (old_hbm, old_ref), (form_hbm, form_ref),
        ),
        sems,
    )
    table = depth_table(by_y)
    for copy in copies[:2]:
        copy.wait()
    index = index_ref[...]
    phases = split(atom_phases(index, pos_ref[...], by_y))
    for copy in copies[2:]:
        copy.wait()
    lines = jnp.concatenate(
        [ref[0, :, 2 * s + c, :] for c in range(2) for ref in arrays for s in range(2)], axis=0
    )
    lines = split(lines)
    group = iota(table.shape, 1) >> 5
    for b in range(COLS):
        z = dot3(split(jnp.where(group == b, table, 0.0)), lines, "nt")
        store(b, z[:64] + swap_sign(z[64:]))

    form_re, form_im = form_ref[0, 0], form_ref[0, 1]
    for n in range(NB):
        parts_re, parts_im = [], []
        for ref in arrays[2:]:
            for s in range(2):
                d_re = ref[0, n, 2 * s : 2 * s + 1, :]
                d_im = ref[0, n, 2 * s + 1 : 2 * s + 2, :]
                parts_re.append(form_re * d_re + form_im * d_im)
                parts_im.append(form_re * d_im - form_im * d_re)
        values = split(jnp.concatenate(parts_re + parts_im, axis=0))
        z = dot3(phases, values, "nt")
        store(COLS + n, z[:64] + swap_sign(z[64:]))

    squares = jnp.zeros((NB, PW), F32)
    for comp in range(4):
        r = res_ref[0, :, comp, :]
        squares = squares + r * r
    row = col_to_row(jnp.sum(squares, axis=1, keepdims=True), 128)
    codes = (index >> 6).astype(F32)
    lane = iota((1, PW), 1)
    target = iota((1, 128), 1)
    for b in range(COLS):
        code = jnp.sum(jnp.where(lane == STICK * b, codes, 0.0), axis=1, keepdims=True)
        row = jnp.where(target == COLS + b, code, row)
    for y in range(YS):
        out_ref[(y + 1) * STAGE1 - 8 : (y + 1) * STAGE1, :] = jnp.broadcast_to(row, (8, 128))


def regroup_kernel(in_ref, out_ref):
    for y in range(YS):
        for b in range(COLS):
            out_ref[pl.ds(y * COLS + b, ZS, stride=STAGE2), :] = in_ref[
                pl.ds(y * STAGE1 + b, ZS, stride=16), :
            ]
    for n in range(NB):
        parts = [in_ref[pl.ds(y * STAGE1 + COLS + n, ZS, stride=16), :] for y in range(YS)]
        out_ref[pl.ds(YS * COLS + n, ZS, stride=STAGE2), :] = (
            (parts[0] + parts[1]) + (parts[2] + parts[3])
        )
    lane = iota((8, 128), 1)
    row = jnp.zeros((8, 128), F32)
    for y in range(YS):
        extra = in_ref[(y + 1) * STAGE1 - 8 : (y + 1) * STAGE1, :]
        row = row + jnp.where(lane < NB, extra, 0.0)
        first = NB + y * COLS
        moved = extra if y == 0 else pltpu.roll(extra, y * COLS, 1)
        row = row + jnp.where((lane >= first) & (lane < first + COLS), moved, 0.0)
    out_ref[pl.ds(EXTRA, ZS, stride=STAGE2), :] = jnp.concatenate([row, row], axis=0)


def own_columns(recv_ref):
    values = jnp.concatenate(
        [
            recv_ref[pl.ds(y * COLS + b, ZS, stride=STAGE2), :]
            for b in range(COLS)
            for y in range(YS)
        ],
        axis=0,
    )
    return values.T


def column_codes(extra):
    codes = extra.astype(jnp.int32)
    shape = (128, ALL)
    lane = iota(shape, 1)
    pick = jnp.where(iota(shape, 0) == NB + ((lane >> 4) & 3) * COLS + (lane >> 6), 1.0, 0.0)
    mine = (iota((ZS, ALL), 1) & 15) == iota((ZS, ALL), 0)
    used = iota((ZS, 128), 1) >= NB
    parts = []
    for value in (codes >> 6, codes & 63):
        value = jnp.where(used, value, 0).astype(F32).astype(BF16)
        spread = dot(value, pick.astype(BF16))
        parts.append(
            jnp.sum(jnp.where(mine, spread, 0.0), axis=0, keepdims=True).astype(jnp.int32)
        )
    return parts


def x_tables(codes, cos_ref, sin_ref):
    shape = (HALF, ALL)
    cosine, sine = trig_wound(iota(shape, 0) * codes[0])
    cos_ref[...] = cosine
    sin_ref[...] = sine


def y_tables(extra, high_ref, low_ref):
    shape = (DEV, 128)
    lane = iota(shape, 1)
    for b in range(COLS):
        lanes = [NB + y * COLS + b for y in range(YS)]
        code = jnp.concatenate([extra[:, i : i + 1] for i in lanes], axis=0).astype(jnp.int32)
        wound = (code & 63) * (lane & 63)
        cosine, sine = trig_wound(wound)
        odd = jnp.broadcast_to(((code >> 6) & 1) == 1, shape)
        first = jnp.where(lane < 64, cosine, sine)
        second = jnp.where(lane < 64, -sine, cosine)
        for c, part in ((0, first), (1, second)):
            rows = slice(c * ALL + b * DEV, c * ALL + (b + 1) * DEV)
            for parity, mine in ((0, jnp.where(odd, 0.0, part)), (1, jnp.where(odd, part, 0.0))):
                high, low = split(mine)
                high_ref[rows, parity * 128 : (parity + 1) * 128] = high
                low_ref[rows, parity * 128 : (parity + 1) * 128] = low


def plane_chunk(re, im, first, count, cos_ref, sin_ref, tables, scratch):
    rows = re.shape[0]
    high_ref, low_ref = scratch
    for i in range(count):
        cx = cos_ref[pl.ds(first + i, 1), :]
        sx = sin_ref[pl.ds(first + i, 1), :]
        for c, part in ((0, re * cx - im * sx), (1, re * sx + im * cx)):
            high, low = split(part)
            high_ref[i * rows : (i + 1) * rows, c * ALL : (c + 1) * ALL] = high
            low_ref[i * rows : (i + 1) * rows, c * ALL : (c + 1) * ALL] = low
    high = high_ref[...]
    table = tables[0][...]
    both = dot(high, table) + dot(low_ref[...], table) + dot(high, tables[1][...])
    return both[:, :128] + both[:, 128:], both[:, :128] - both[:, 128:]


def fetch(pairs, sems):
    copies = [
        pltpu.make_async_copy(source, target, sems.at[i])
        for i, (source, target) in enumerate(pairs)
    ]
    for copy in copies:
        copy.start()
    return copies


def twice(row, half):
    lane = iota(row.shape, 1)
    return jnp.where((lane >= 64) == (half == 1), row, pltpu.roll(row, 64, 1))


def potential_kernel(
    recv_ref, atom_ref, slots_hbm, pot_hbm, old_norm_hbm, res_hbm, old_hbm, kin_hbm,
    energy_hbm, coup_hbm,
    out_ref, grid_ref, scalars_ref,
    slots_ref, pot_ref, old_norm_ref, res_ref, old_ref, kin_ref, energy_ref, coup_ref, sems,
    cos_ref, sin_ref, table_high, table_low, high_ref, low_ref, prod_ref, pair_ref,
):
    copies = fetch(
        (
            (pot_hbm, pot_ref), (old_norm_hbm, old_norm_ref), (res_hbm, res_ref),
            (old_hbm, old_ref), (slots_hbm, slots_ref), (kin_hbm, kin_ref), (energy_hbm, energy_ref), (coup_hbm, coup_ref),
        ),
        sems,
    )
    def store(r, value):
        for y in range(YS):
            out_ref[pl.ds(y * ROWS2 + r, ZS, stride=YS * ROWS2), :] = value[
                y * ZS : (y + 1) * ZS
            ]

    extra = recv_ref[pl.ds(EXTRA, ZS, stride=STAGE2), :]
    codes = column_codes(extra)
    x_tables(codes, cos_ref, sin_ref)
    y_tables(extra, table_high, table_low)
    tables = (table_high, table_low)
    for copy in copies:
        copy.wait()
    norm = row_to_col(jnp.sum(extra, axis=0, keepdims=True), NB)
    beta = norm / row_to_col(old_norm_ref[...], NB)
    values = own_columns(recv_ref)
    beta2 = jnp.concatenate([beta, beta], axis=0)
    re = values[32:48] + beta2 * values[48:64]
    im = values[96:112] + beta2 * values[112:128]

    acc_re = jnp.zeros((16, ALL), F32)
    acc_im = jnp.zeros((16, ALL), F32)
    local = jnp.zeros((NB, 128), F32)
    chunks = []
    for k in range(CH):
        chunks.append(plane_chunk(
            re, im, k * CX, CX, cos_ref, sin_ref, tables, (high_ref.at[k], low_ref.at[k])
        ))
    turns = []
    for k in range(CH):
        first = k * CX
        grids = chunks[k]
        for i in range(CX):
            products = []
            for half in range(2):
                grid = grids[half]
                x = first + i + 32 * half
                up = grid[i * 16 : i * 16 + 8]
                down = grid[i * 16 + 8 : i * 16 + 16]
                grid_ref[x * 16 : x * 16 + 8, :] = up
                grid_ref[x * 16 + 8 : x * 16 + 16, :] = down
                v0, bx, by, bz = (
                    twice(pot_ref[m, :, x // 2 * 128 : x // 2 * 128 + 128], x % 2)
                    for m in range(4)
                )
                new_up = (v0 + bz) * up + bx * down - by * swap_sign(down)
                new_down = bx * up + by * swap_sign(up) + (v0 - bz) * down
                local = local + up * new_up + down * new_down
                products.append((new_up, new_down))
            for j in range(2):
                rows = slice(i * 16 + 8 * j, i * 16 + 8 * j + 8)
                prod_ref[k, rows, 0:128] = products[0][j] + products[1][j]
                prod_ref[k, rows, 128:256] = products[0][j] - products[1][j]
        turns.append(dot3(split(prod_ref[k]), (table_high[...], table_low[...]), "nt"))
    for k in range(CH):
        for i in range(CX):
            x = k * CX + i
            cx = cos_ref[x : x + 1, :]
            sx = sin_ref[x : x + 1, :]
            q_re = turns[k][i * 16 : (i + 1) * 16, :ALL]
            q_im = turns[k][i * 16 : (i + 1) * 16, ALL:]
            acc_re = acc_re + q_re * cx + q_im * sx
            acc_im = acc_im + q_im * cx - q_re * sx
    acc_re = acc_re * VOLUME
    acc_im = acc_im * VOLUME
    for r in range(2):
        pieces = []
        for b in range(4 * r, 4 * r + 4):
            lanes = slice(b * DEV, (b + 1) * DEV)
            pieces += [acc_re[:, lanes], acc_im[:, lanes]]
        store(r, jnp.concatenate(pieces, axis=0).T)

    sums = [
        jnp.sum(recv_ref[pl.ds(YS * COLS + n, ZS, stride=STAGE2), :], axis=0, keepdims=True)
        for n in range(NB)
    ]
    amps = jnp.concatenate(sums, axis=0)
    amps = amps + beta * pltpu.roll(amps, 96, 1)
    amp_re, amp_im = amps[:, 0:32], amps[:, 64:96]
    here = jnp.where(slots_ref[...] == atom_ref[0], 1.0, 0.0)
    lane = iota(here.shape, 1)
    count = jnp.zeros((1, 32), F32)
    for half in range(2):
        mine = jnp.sum(jnp.where((lane >= 64) == (half == 1), here, 0.0), axis=1, keepdims=True)
        place = 2 * iota((8, 32), 0) + half
        count = count + jnp.sum(
            jnp.where((iota((8, 32), 1) & 15) == place, mine, 0.0), axis=0, keepdims=True
        )
    h_re = 0.5 * (coup_ref[0] + coup_ref[0].T)
    h_im = 0.5 * (coup_ref[1] - coup_ref[1].T)
    by_re, by_im = amp_re * count, amp_im * count

    def exact(a, b):
        return lax.dot_general(
            a, b, (((1,), (0,)), ((), ())),
            precision=lax.Precision.HIGHEST, preferred_element_type=F32,
        )

    q_re = (exact(by_re, h_re) + exact(by_im, h_im)) * count
    q_im = (exact(by_im, h_re) - exact(by_re, h_im)) * count
    pair_ref[:, 0:32] = q_re
    pair_ref[:, 32:64] = q_im
    pair_ref[:, 64:128] = jnp.zeros((NB, 64), F32)
    first_half = pair_ref[pl.ds(0, 4, stride=2), :]
    second_half = pair_ref[pl.ds(1, 4, stride=2), :]
    packed = first_half + pltpu.roll(second_half, 64, 1)
    odd = ((iota((DEV, 128), 0) >> 4) & 1) == 1
    for k in range(2):
        store(2 + k, jnp.where(odd, packed[2 + k : 3 + k], packed[k : k + 1]))

    curvature = jnp.sum(local, axis=1, keepdims=True) * VOLUME
    curvature = curvature + jnp.sum(amp_re * q_re + amp_im * q_im, axis=1, keepdims=True)
    weight = kin_ref[...] - row_to_col(energy_ref[...], NB)
    own = jnp.zeros((NB, PW), F32)
    for comp in range(4):
        d = res_ref[0, :, comp, :] + beta * old_ref[0, :, comp, :]
        own = own + d * d
    curvature = curvature + jnp.sum(own * weight, axis=1, keepdims=True)
    store(4, jnp.broadcast_to(col_to_row(curvature, 128), (DEV, 128)))
    lane = iota((NB, 128), 1)
    scalars_ref[...] = jnp.where(lane == 0, norm, jnp.where(lane == 1, beta, 0.0))


def orbital_kernel(
    recv_ref, grid_ref, base_ref, slope_ref, cos_ref, sin_ref, table_high, table_low, high_ref,
    low_ref,
):
    extra = recv_ref[pl.ds(EXTRA, ZS, stride=STAGE2), :]
    x_tables(column_codes(extra), cos_ref, sin_ref)
    y_tables(extra, table_high, table_low)
    values = own_columns(recv_ref)
    re, im = values[0:32], values[64:96]
    lane = iota((NB, 128), 1)

    def terms(o_up, o_down, c_up, c_down):
        same_up = o_up * c_up
        same_down = o_down * c_down
        return (
            same_up + same_down,
            o_up * c_down + o_down * c_up,
            o_down * swap_sign(c_up) - o_up * swap_sign(c_down),
            same_up - same_down,
        )

    def fold(even, odd):
        return 2.0 * (
            jnp.where(lane < 64, even, odd)
            + pltpu.roll(jnp.where(lane < 64, odd, even), 64, 1)
        )

    def chunk(k, carry):
        grids = plane_chunk(
            re, im, k * 8, 8, cos_ref, sin_ref, (table_high, table_low), (high_ref, low_ref)
        )
        for half in range(2):
            for j in range(4):
                with_response, with_direction = [], []
                for i in (2 * j, 2 * j + 1):
                    o_up, o_down, r_up, r_down = (
                        grids[half][i * 32 + 8 * q : i * 32 + 8 * q + 8] for q in range(4)
                    )
                    place = pl.multiple_of((k * 8 + i + 32 * half) * 16, 16)
                    d_up = grid_ref[pl.ds(place, 8), :]
                    d_down = grid_ref[pl.ds(place + 8, 8), :]
                    with_response.append(terms(o_up, o_down, r_up, r_down))
                    with_direction.append(terms(o_up, o_down, d_up, d_down))
                for m in range(4):
                    row = m * 32 + 16 * half + j + 4 * k
                    base_ref[pl.ds(row, 1), :] = jnp.sum(
                        fold(with_response[0][m], with_response[1][m]), axis=0, keepdims=True
                    )
                    slope_ref[pl.ds(row, NB, stride=128), :] = fold(
                        with_direction[0][m], with_direction[1][m]
                    )
        return carry

    lax.fori_loop(0, 4, chunk, 0)


def step_of(recv_ref, scalars_ref):
    total = jnp.sum(recv_ref[pl.ds(4, DEV, stride=ROWS2), :], axis=0, keepdims=True)
    return scalars_ref[:, 0:1] / (row_to_col(total, NB) + SMALL_TERM)


def density_kernel(recv_ref, scalars_ref, base_ref, slope_ref, out_ref, half_ref):
    step = step_of(recv_ref, scalars_ref)
    total = base_ref[...]
    for n in range(NB):
        total = total + step[n : n + 1, :] * slope_ref[n * 128 : (n + 1) * 128, :]
    for copy in range(8):
        out_ref[copy * 128 : (copy + 1) * 128, :] = total
    for k in range(2):
        half_ref[k * DEV : (k + 1) * DEV, :] = recv_ref[pl.ds(2 + k, DEV, stride=ROWS2), :]


def half_term(half_ref, phases, form_ref):
    form_re, form_im = form_ref[0, 0], form_ref[0, 1]
    rows_re, rows_im = [[], []], [[], []]
    for k in range(2):
        z = dot3(split(half_ref[k * DEV : (k + 1) * DEV, :].T), phases)
        for i in range(2):
            for s in range(2):
                a = i * 64 + s * 16
                re_c, re_s = z[a : a + 16, :PW], z[a : a + 16, PW:]
                im_c, im_s = z[a + 32 : a + 48, :PW], z[a + 32 : a + 48, PW:]
                w_re = re_c + im_s
                w_im = im_c - re_s
                rows_re[s].append(
                    jnp.sum(form_re * w_re - form_im * w_im, axis=0, keepdims=True)
                )
                rows_im[s].append(
                    jnp.sum(form_re * w_im + form_im * w_re, axis=0, keepdims=True)
                )
    return [
        [jnp.concatenate(rows[s], axis=0) for rows in (rows_re, rows_im)] for s in range(2)
    ]


def in_half(part, second):
    zero = jnp.zeros_like(part)
    return jnp.where(
        second, jnp.concatenate([zero, part], axis=0), jnp.concatenate([part, zero], axis=0)
    )


def image_kernel(
    parity_ref, half_ref, recv_ref, scalars_ref, res_ref, old_ref, kin_ref, energy_ref,
    form_ref, index_ref, pos_ref, image_ref, phases_ref,
):
    beta = scalars_ref[:, 1:2]
    table = depth_table(by_z)
    table = split(jnp.concatenate([table[:64], table[64:]], axis=1))
    group = iota((32, PW), 1) >> 5
    local = jnp.zeros((32, PW), F32)
    for r in range(2):
        values = recv_ref[pl.ds(r, DEV, stride=ROWS2), :].T
        z = dot3(split(values), table)
        for i in range(4):
            re_c, re_s = z[i * 32 : i * 32 + 16, :PW], z[i * 32 : i * 32 + 16, PW:]
            im_c, im_s = z[i * 32 + 16 : i * 32 + 32, :PW], z[i * 32 + 16 : i * 32 + 32, PW:]
            part = jnp.concatenate([re_c + im_s, im_c - re_s], axis=0)
            local = local + jnp.where(group == 4 * r + i, part, 0.0)
    phases = atom_phases(index_ref[...], pos_ref[...], by_z)
    phases = jnp.concatenate([phases[:64], phases[64:]], axis=1)
    phases_ref[...] = phases
    mine = half_term(half_ref, split(phases), form_ref)
    weight = kin_ref[...] - row_to_col(energy_ref[...], NB)
    for s in range(2):
        for c in range(2):
            comp = 2 * s + c
            direction = res_ref[0, :, comp, :] + beta * old_ref[0, :, comp, :]
            place = c * 16 + s * 8
            image_ref[comp] = (
                weight * direction + local[place : place + 8]
                + in_half(mine[s][c], parity_ref[0] == 1)
            )


def finish_kernel(
    parity_ref, other_ref, recv_ref, scalars_ref, image_ref, phases_ref, resp_ref, res_ref,
    old_ref, form_ref, next_ref, residual_ref, direction_ref,
):
    step = step_of(recv_ref, scalars_ref)
    beta = scalars_ref[:, 1:2]
    theirs = half_term(other_ref, split(phases_ref[...]), form_ref)
    for s in range(2):
        for c in range(2):
            comp = 2 * s + c
            residual = res_ref[0, :, comp, :]
            direction = residual + beta * old_ref[0, :, comp, :]
            image = image_ref[comp] + in_half(theirs[s][c], parity_ref[0] == 0)
            direction_ref[0, :, comp, :] = direction
            next_ref[0, :, comp, :] = resp_ref[0, :, comp, :] + step * direction
            residual_ref[0, :, comp, :] = residual - step * image


def call(kernel, outs, name, scratch=(), flops=1, size=1, smem=(), hbm=()):
    def space(i):
        return pltpu.SMEM if i in smem else pltpu.HBM if i in hbm else pltpu.VMEM

    def run(*args):
        specs = [pl.BlockSpec(memory_space=space(i)) for i in range(len(args))]
        args = [
            pltpu.with_memory_space_constraint(a, pltpu.HBM) if i in hbm else a
            for i, a in enumerate(args)
        ]
        return pl.pallas_call(
            kernel,
            out_shape=outs,
            in_specs=specs,
            out_specs=jax.tree.map(lambda _: pl.BlockSpec(memory_space=pltpu.VMEM), outs),
            scratch_shapes=list(scratch),
            compiler_params=pltpu.CompilerParams(vmem_limit_bytes=LIMIT),
            cost_estimate=pl.CostEstimate(flops=flops, bytes_accessed=size, transcendentals=0),
            name=name,
        )(*args)

    return run


def shape_of(*dims):
    return jax.ShapeDtypeStruct(dims, F32)


def exchange(values, axis, parts, groups=None):
    rows = values.shape[0] // parts
    if rows % 8:
        flat = values.reshape(parts, 1, rows * 128)
        flat = lax.all_to_all(flat, axis, 0, 0, tiled=True, axis_index_groups=groups)
        return flat.reshape(values.shape)
    out = lax.all_to_all(
        values.reshape(parts, rows, 128), axis, 0, 0, tiled=True, axis_index_groups=groups
    )
    return out.reshape(values.shape)


def per_device(
    orbitals, response, residual, old_direction, old_norm, band_energy, kinetic, form_factor,
    sphere_index, atom_positions, proj_atom, coupling, potential,
):
    scale = 1.0 / (8 * 16384)
    me = lax.axis_index("fft").reshape(1).astype(jnp.int32)
    slots = proj_atom.reshape(8, 128)

    parity = me & 1
    vector = pltpu.VMEM((1, NB, 4, PW), F32)
    sent = call(
        send_kernel, shape_of(YS * STAGE1, 128), "lines_and_amplitudes",
        [vector] * 4 + [
            pltpu.VMEM((1, 2, PA, PW), F32), pltpu.VMEM((1, PW), jnp.int32),
            pltpu.VMEM((3, NG), F32), pltpu.SemaphoreType.DMA((7,)),
        ],
        hbm=range(7),
    )(orbitals, response, residual, old_direction, form_factor, sphere_index, atom_positions)
    sent, me, parity = lax.optimization_barrier((sent, me, parity))
    near = exchange(sent, "fft", YS, SAME_Z)
    joined = call(regroup_kernel, shape_of(ZS * STAGE2, 128), "regroup")(near)
    recv = exchange(joined, "fft", ZS, SAME_Y)
    tables = [
        pltpu.VMEM((HALF, ALL), F32), pltpu.VMEM((HALF, ALL), F32),
        pltpu.VMEM((2 * ALL, 256), BF16), pltpu.VMEM((2 * ALL, 256), BF16),
    ]
    back, grid, scalars = call(
        potential_kernel,
        (shape_of(DEV * ROWS2, 128), shape_of(NG * 16, 128), shape_of(NB, 128)),
        "potential_and_coupling",
        [
            pltpu.VMEM((8, 128), jnp.int32), pltpu.VMEM((4, 1, NG * NG), F32),
            pltpu.VMEM((1, NB), F32), vector, vector, pltpu.VMEM((1, PW), F32),
            pltpu.VMEM((1, NB), F32), pltpu.VMEM((2, 32, 32), F32),
            pltpu.SemaphoreType.DMA((8,)),
        ]
        + tables
        + [pltpu.VMEM((CH, 512 // CH, 2 * ALL), BF16), pltpu.VMEM((CH, 512 // CH, 2 * ALL), BF16)]
        + [pltpu.VMEM((CH, 512 // CH, 256), F32), pltpu.VMEM((NB, 128), F32)],
        smem=(1,), hbm=range(2, 10),
    )(recv, me, slots, potential, old_norm, residual, old_direction, kinetic, band_energy, coupling)
    returned = exchange(back, "fft", DEV, EVERY)
    base, slope = call(
        orbital_kernel, (shape_of(128, 128), shape_of(NB * 128, 128)), "density_terms",
        tables + [pltpu.VMEM((256, 2 * ALL), BF16), pltpu.VMEM((256, 2 * ALL), BF16)],
        flops=3_000_000_000, size=3_000_000,
    )(recv, grid)
    density, half = call(
        density_kernel, (shape_of(8 * 128, 128), shape_of(2 * DEV, 128)), "density"
    )(returned, scalars, base, slope)
    gathered = exchange(density, "kpool", 8, POINTS)
    other_half = lax.ppermute(half, "fft", MIRROR)
    image, phases = call(
        image_kernel, (shape_of(4, NB, PW), shape_of(DEV, 2 * PW)), "image",
        flops=3_000_000_000, size=3_000_000, smem=(0,),
    )(
        parity, half, returned, scalars, residual, old_direction, kinetic, band_energy,
        form_factor, sphere_index, atom_positions,
    )
    outs = call(
        finish_kernel, (shape_of(1, NB, 4, PW),) * 3, "new_vectors",
        flops=1_000_000_000, size=1_000_000, smem=(0,),
    )(
        parity, other_half, returned, scalars, image, phases, response, residual, old_direction,
        form_factor,
    )
    total = jnp.sum(gathered.reshape(8, 128, 128), axis=0) * scale
    return outs[0], outs[1], outs[2], total.reshape(4, 1, NG * NG)


def solution(mesh):
    vector = P("kpool", None, None, "fft")
    in_specs = (
        vector, vector, vector, vector, P("kpool", None), P("kpool", None), P("kpool", "fft"),
        vector, P("kpool", "fft"), P(), P(), P(), P(None, "fft", None),
    )
    out_specs = (vector, vector, vector, P(None, "fft", None))
    return jax.shard_map(
        per_device, mesh=mesh, in_specs=in_specs, out_specs=out_specs, check_vma=False
    )
```
